128 devices in a mesh: queue: 16 (over z_hi, x, core), tile: 8 (over y, z_lo).
Axes of the slice: x: 4, y: 4, z: 4 (z_hi: 2, z_lo: 2; z = z_hi * 2 + z_lo), core: 2. Of those that a mesh axis runs over, the one named last changes fastest.
Arguments:
- queue_latents: float32 [128, 4, 16, 128], P('queue', None, 'tile'), may hold values from -6 to 6
- entering: float32 [2, 4, 16, 128], P(None, None, 'tile'), may hold values from -6 to 6
- levels: int32 [128], P('queue'), may hold values from 1 to 896, as said below
- time_weight: float32 [320, 320], replicated, may hold values from -0.3125 to 0.3125
- conv_in_weight: bfloat16 [3, 3, 4, 320], replicated, may hold values from -1 to 1
- conv_mid_weight: bfloat16 [3, 3, 320, 320], replicated, may hold values from -0.109375 to 0.109375
- norm_gain: float32 [320], replicated, may hold values from 0.1 to 1.9
- qkv_weight: bfloat16 [320, 960], replicated, may hold values from -0.3125 to 0.3125
- head_scale: float32 [5], replicated, may hold values from 2 to 12
- attn_out_weight: bfloat16 [320, 320], replicated, may hold values from -0.3125 to 0.3125
- eps_out_weight: bfloat16 [320, 4], replicated, may hold values from -0.3125 to 0.3125
Outputs:
- final_queue: float32 [128, 4, 16, 128], P('queue', None, 'tile')
The draws below stay inside these ranges and needn't reach their ends.
Inputs may be any that keep to these rules, and one draw needn't show every extreme that they name: `levels`: strictly rising over the slots; the last slot's level is exactly the maximum.
All inputs are finite; a program needn't handle non-finite values.
Results may differ from the reference program's by a relative error of at most 0.0012.
Values may be sent and summed in bfloat16 or wider, within the bound.
A program may use at most 128 MiB of HBM per device.

```python
import math
import jax
import jax.numpy as jnp
from jax import lax

C = 320
HEADS = 5
LW = 128
WIN = 8
STEPS = 2
FRAMES = 128
H = 16


def draw_levels(key, part):
    key = jax.random.fold_in(key, 7)
    level_gap = 900 // FRAMES
    slot_ids = jnp.arange(FRAMES, dtype=jnp.int32)
    jitter = jax.random.randint(key, (FRAMES,), 1, level_gap, dtype=jnp.int32)
    drawn = slot_ids * level_gap + jitter
    return jnp.where(slot_ids == FRAMES - 1, FRAMES * level_gap, drawn).astype(jnp.int32)


def shard_levels(own_key, extent, pieces, low, top_value):
    factor_of, own = 1.0, jax.random.fold_in(own_key, 6)
    for position, shards_of in pieces:
        heights = jnp.exp(jax.random.uniform(jax.random.fold_in(own, position), (shards_of,), jnp.float32, low / len(pieces), top_value / len(pieces)))
        factor_of = factor_of * jnp.repeat(heights, extent[position] // shards_of).reshape([-1 if axis == position else 1 for axis in range(len(extent))])
    return factor_of


def normal_values(key, shape, scale, bound, cuts=(), held_as=jnp.bfloat16):
    entries = jax.random.normal(key, shape, jnp.float32) * scale
    if len(cuts) > 0:
        entries = shard_levels(key, shape, cuts, -0.22, 0.18) * entries
    return jnp.clip(entries, min=-bound, max=bound).astype(held_as)


def setup_inputs(seed: int = 0) -> dict:
    key_list = jax.random.split(jax.random.key(seed), 12)
    queue_latents = normal_values(key_list[0], (FRAMES, 4, H, LW), 1.0, 6.0, ((0, 16), (2, 8)), jnp.float32)
    entering = normal_values(key_list[1], (STEPS, 4, H, LW), 1.0, 6.0, ((2, 8),), jnp.float32)
    levels = draw_levels(jax.random.fold_in(key_list[11], 71), 0)
    time_weight = normal_values(key_list[3], (C, C), C ** -0.5, 0.3125, (), jnp.float32)
    conv_in_weight = normal_values(key_list[4], (3, 3, 4, C), 36 ** -0.5, 1.0)
    conv_mid_weight = normal_values(key_list[5], (3, 3, C, C), (9 * C) ** -0.5, 0.109375)
    norm_gain = jnp.clip(1.0 + 0.18 * jax.random.normal(key_list[6], (C,), jnp.float32), 0.1, 1.9)
    qkv_weight = normal_values(key_list[7], (C, 3 * C), C ** -0.5, 0.3125)
    head_scale = jnp.clip(jnp.exp(jax.random.uniform(key_list[8], (HEADS,), jnp.float32, math.log(2.0), math.log(12.0))), 2.0, 12.0)
    attn_out_weight = normal_values(key_list[9], (C, C), C ** -0.5, 0.3125)
    eps_out_weight = normal_values(key_list[10], (C, 4), C ** -0.5, 0.3125)
    return dict(queue_latents=queue_latents, entering=entering, levels=levels, time_weight=time_weight, conv_in_weight=conv_in_weight, conv_mid_weight=conv_mid_weight, norm_gain=norm_gain, qkv_weight=qkv_weight, head_scale=head_scale, attn_out_weight=attn_out_weight, eps_out_weight=eps_out_weight)


def alpha_bar(level_ids):
    ratio = level_ids.astype(jnp.float32) / 1000.0
    cosine = jnp.cos((ratio + 0.008) / 1.008 * (math.pi / 2.0))
    return cosine * cosine

def embed_levels(level_ids, time_weight):
    half_width = time_weight.shape[0] // 2
    freqs = jnp.exp(-math.log(10000.0) * jnp.arange(half_width, dtype=jnp.float32) / half_width)
    angles = level_ids.astype(jnp.float32)[:, None] * freqs[None, :]
    feature = jnp.concatenate([jnp.sin(angles), jnp.cos(angles)], axis=1)
    return jnp.dot(feature, time_weight, precision=lax.Precision.HIGHEST)

def conv_full(source, kernel):
    row_count = source.shape[0]
    col_count = source.shape[1]
    padded = jnp.pad(source, ((1, 1), (1, 1), (0, 0))).astype(jnp.float32)
    total = jnp.zeros((row_count, col_count, kernel.shape[3]), jnp.float32)
    for shift_y in range(3):
        for shift_x in range(3):
            window = padded[shift_y:shift_y + row_count, shift_x:shift_x + col_count]
            total = total + jnp.einsum('hwc,cd->hwd', window, kernel[shift_y, shift_x].astype(jnp.float32))
    return total

def layer_norm(hidden, gain):
    center = lax.optimization_barrier(jnp.mean(hidden, axis=-1, keepdims=True))
    spread = lax.optimization_barrier(jnp.mean((hidden - center) * (hidden - center), axis=-1, keepdims=True))
    return ((hidden - center) * lax.rsqrt(spread + 1e-05) * gain).astype(jnp.bfloat16)

def unit_heads(project, head_count):
    shaped = project.reshape(project.shape[:-1] + (head_count, project.shape[-1] // head_count))
    return (shaped * lax.rsqrt(lax.optimization_barrier(jnp.sum(shaped * shaped, axis=-1, keepdims=True)) + 1e-06)).astype(jnp.bfloat16)

def attend(hidden_row, norm_gain, qkv_weight, head_scale, attn_out_weight, eps_out_weight):
    frame_count = hidden_row.shape[0]
    col_count = hidden_row.shape[1]
    channels = hidden_row.shape[2]
    head_count = head_scale.shape[0]
    head_dim = channels // head_count
    normed = layer_norm(hidden_row, norm_gain)
    project = jnp.einsum('fwc,cd->fwd', normed.astype(jnp.float32), qkv_weight.astype(jnp.float32))
    query = unit_heads(project[..., :channels], head_count)
    keys = unit_heads(project[..., channels:2 * channels], head_count)
    values = project[..., 2 * channels:].astype(jnp.bfloat16).reshape((frame_count, col_count, head_count, head_dim))
    scores = jnp.einsum('iwhd,jwhd->iwhj', query.astype(jnp.float32), keys.astype(jnp.float32))
    scores = scores * head_scale[None, None, :, None]
    slots = jnp.arange(frame_count, dtype=jnp.int32)
    near = jnp.abs(slots[:, None] - slots[None, :]) <= WIN
    expo = jnp.where(near[:, None, None, :], jnp.exp(scores), 0.0)
    weights = (expo / lax.optimization_barrier(jnp.sum(expo, axis=3, keepdims=True))).astype(jnp.bfloat16)
    mixed_out = jnp.einsum('iwhj,jwhd->iwhd', weights.astype(jnp.float32), values.astype(jnp.float32))
    mixed_out = mixed_out.reshape((frame_count, col_count, channels)).astype(jnp.bfloat16)
    upper = hidden_row + jnp.einsum('fwc,cd->fwd', mixed_out.astype(jnp.float32), attn_out_weight.astype(jnp.float32))
    active = jax.nn.silu(upper).astype(jnp.bfloat16)
    return jnp.einsum('fwc,cd->fwd', active.astype(jnp.float32), eps_out_weight.astype(jnp.float32))

def reference(queue_latents, entering, levels, time_weight, conv_in_weight, conv_mid_weight, norm_gain, qkv_weight, head_scale, attn_out_weight, eps_out_weight):
    target = jnp.concatenate([jnp.zeros((1,), jnp.int32), levels[:-1]])
    embedded = embed_levels(levels, time_weight)
    abar_now = alpha_bar(levels)[:, None, None, None]
    abar_next = alpha_bar(target)[:, None, None, None]
    state = queue_latents
    for step_index in range(STEPS):
        latent_bf = state.astype(jnp.bfloat16)

        def frame_net(paired):
            frame, shift_vec = paired
            source = jnp.transpose(frame, (1, 2, 0))
            hidden = conv_full(source, conv_in_weight) + shift_vec[None, None, :]
            active = jax.nn.silu(hidden).astype(jnp.bfloat16)
            return hidden + conv_full(active, conv_mid_weight)
        hidden_all = lax.map(frame_net, (latent_bf, embedded))

        def row_net(row_index):
            hidden_row = lax.dynamic_index_in_dim(hidden_all, row_index, 1, keepdims=False)
            return attend(hidden_row, norm_gain, qkv_weight, head_scale, attn_out_weight, eps_out_weight)
        noise = lax.map(row_net, jnp.arange(H, dtype=jnp.int32))
        noise = jnp.transpose(noise, (1, 3, 0, 2))
        clean = (state - jnp.sqrt(1.0 - abar_now) * noise) / jnp.sqrt(abar_now)
        updated = jnp.sqrt(abar_next) * clean + jnp.sqrt(1.0 - abar_next) * noise
        state = jnp.concatenate([updated[1:], entering[step_index][None]], axis=0)
    return state
```

```python
import math

import jax
import jax.numpy as jnp
from jax import lax
from jax.experimental import pallas as pl
from jax.experimental.pallas import tpu as pltpu
from jax.sharding import PartitionSpec as P

WIN = 8
STEPS = 2
F32 = jnp.float32
BF16 = jnp.bfloat16
MESH = pl.DeviceIdType.MESH

CH = 320
HEADS = 5
HD = 64
FR = 128
NQ = 16
NT = 8
PX = 8
ROW = 48
TAPS = 3 * ROW


def dot(a, b):
    return jnp.dot(a, b, preferred_element_type=F32)


def dot_t(a, b):
    return lax.dot_general(a, b, (((0,), (0,)), ((), ())), preferred_element_type=F32)


def sin_cos(angle):
    count = jnp.floor(angle * (2.0 / math.pi) + 0.5)
    rest = ((angle - count * 1.5703125) - count * 4.837512969970703125e-4) - count * 7.54978995489188216e-8
    square = rest * rest
    sine = rest + rest * square * (
        -1.6666654611e-1 + square * (8.3321608736e-3 - square * 1.9515295891e-4)
    )
    cosine = 1.0 - 0.5 * square + square * square * (
        4.166664568298827e-2 + square * (-1.388731625493765e-3 + square * 2.443315711809948e-5)
    )
    quarter = count - 4.0 * jnp.floor(count * 0.25)
    odd = (quarter == 1.0) | (quarter == 3.0)
    sin_out = jnp.where(odd, cosine, sine)
    cos_out = jnp.where(odd, sine, cosine)
    sin_out = jnp.where(quarter >= 2.0, -sin_out, sin_out)
    cos_out = jnp.where((quarter == 1.0) | (quarter == 2.0), -cos_out, cos_out)
    return sin_out, cos_out


def silu(x):
    half = 0.5 * x
    return half + half * jnp.tanh(half)


def lanes(shape):
    return lax.broadcasted_iota(jnp.int32, shape, 1)


def pack_latents(lat_ref, lev_ref, send_ref):
    lane = lanes((8, FR))
    row = lax.broadcasted_iota(jnp.int32, (8, FR), 0)
    pieces = []
    for c in range(4):
        for r in range(2):
            plane = lat_ref[:, c, r, :]
            own, left, right = c * 16 + r * 8, 64 + r * 8 + c * 2, 80 + r * 8 + c * 2
            pieces.append((3, own, pltpu.roll(plane, own, 1)))
            pieces.append((1, left, pltpu.roll(plane, left + 2, 1)))
            pieces.append((1, right, pltpu.roll(plane, right - 8, 1)))
    level = jnp.zeros((8, FR), F32)
    for f in range(8):
        level = jnp.where(row == f, lev_ref[f].astype(F32), level)

    def body(dest, carry):
        place = (lane - 8 * dest) & (FR - 1)
        total = jnp.zeros((8, FR), F32)
        for bits, base, plane in pieces:
            total = jnp.where((place >> bits) == (base >> bits), plane, total)
        total = pltpu.roll(total, lax.rem(FR - 8 * dest, FR), 1)
        send_ref[dest] = jnp.where(lane == 2 * ROW, level, total)
        return carry

    lax.fori_loop(0, NQ, body, 0)


def prepare(cin_ref, cmid_ref, gain_ref, qkv_ref, wo_ref, we_ref, ent_ref, taps_ref,
            band_ref, mid_ref, qkvt_ref, wot_ref, wet_ref, gain_out, near_ref, ent_out, q):
    taps_ref[...] = jnp.zeros(taps_ref.shape, F32)
    for i in range(9):
        taps_ref[4 * i : 4 * i + 4, :] = cin_ref[i // 3, i % 3].astype(F32)
    taps_t = taps_ref[...].T.astype(BF16)
    k = lanes((40, TAPS))
    m = lax.broadcasted_iota(jnp.int32, (40, TAPS), 0)
    dy = (k >= ROW).astype(jnp.int32) + (k >= 2 * ROW).astype(jnp.int32)
    rest = k - ROW * dy
    own = rest < 32
    left = rest < 40
    c = jnp.where(own, rest >> 3, (rest & 7) >> 1)
    rel = jnp.where(own, (rest & 7) + 2, jnp.where(left, rest & 1, (rest & 1) + 10))
    for w in range(PX + 2):
        dx = rel - w
        pick = (dx >= 0) & (dx <= 2) & (m == dy * 12 + dx * 4 + c)
        band_ref[w] = dot(taps_t, jnp.where(pick, 1.0, 0.0).astype(BF16)).astype(BF16)
    for dx in range(3):
        for dy_ in range(3):
            mid_ref[dx, dy_] = cmid_ref[dy_, dx].T
    qkvt_ref[...] = qkv_ref[...].T
    wot_ref[...] = wo_ref[...].T
    eps = jnp.concatenate([we_ref[...].astype(F32), jnp.zeros((CH, FR - 4), F32)], axis=1)
    wet_ref[...] = eps.T[:16].astype(BF16)
    gain_out[...] = jnp.broadcast_to(gain_ref[...], (FR, CH)).T
    key_slot = lax.broadcasted_iota(jnp.int32, (FR, FR), 0)
    query_slot = lanes((FR, FR))
    near_ref[...] = jnp.where(jnp.abs(key_slot - query_slot) <= WIN, 1.0, 0.0).astype(BF16)
    lane = lanes((8, FR))
    for s in range(STEPS):
        rows = jnp.concatenate([ent_ref[s, c, r : r + 1, :] for c in range(4) for r in range(2)], axis=0)
        rows = pltpu.roll(rows, lax.rem(FR - 8 * q, FR), 1)
        columns = jnp.concatenate([rows, jnp.zeros((FR - 8, FR), F32)], axis=0).T[:8]
        for i in range(8):
            shifted = pltpu.roll(columns, FR - 1 - i, 1)
            ent_out[s, 8 * i : 8 * i + 8, :] = jnp.where(lane == FR - 1, shifted, 0.0)


def embed(level, tw_ref, emb_ref):
    index = lax.broadcasted_iota(jnp.int32, (CH // 2, FR), 0).astype(F32)
    freqs = jnp.exp(-math.log(10000.0) * index / (CH // 2))
    sine, cosine = sin_cos(level * freqs)
    feature = jnp.concatenate([sine, cosine], axis=0)
    emb_ref[...] = lax.dot_general(
        tw_ref[...].T, feature, (((1,), (0,)), ((), ())),
        precision=lax.Precision.HIGHEST, preferred_element_type=F32)


def coefficients(level):
    lane = lanes((8, FR))
    level = jnp.broadcast_to(level, (8, FR))
    target = jnp.where(lane == 0, 0.0, pltpu.roll(level, 1, 1))
    angle = lambda l: (l / 1000.0 + 0.008) / 1.008 * (math.pi / 2.0)
    s0, c0 = sin_cos(angle(level))
    s1, c1 = sin_cos(angle(target))
    alpha = c1 / c0
    return alpha, s1 - alpha * s0


def conv_in(slots, band_ref, emb_ref, rhs_ref, hid_ref, act_ref, q, t):
    rows = []
    for slot in slots:
        for r in range(2):
            rows.append(jnp.concatenate(
                [slot[g * 16 + r * 8 : g * 16 + r * 8 + 8] for g in range(6)], axis=0).astype(BF16))
    for p in range(2):
        for half in range(2):
            rhs_ref[p, :, half * FR : (half + 1) * FR] = jnp.concatenate(
                rows[2 * p + half : 2 * p + half + 3], axis=0)

    def body(w, carry):
        for p in range(2):
            both = dot(band_ref[w], rhs_ref[p])
            for half in range(2):
                hidden = both[:, half * FR : (half + 1) * FR] + emb_ref[...]
                act_ref[w, 2 * p + half] = silu(hidden).astype(BF16)
                if p != half:
                    hid_ref[w, p] = hidden
        return carry

    lax.fori_loop(0, PX + 2, body, 0)

    @pl.when(t == 0)
    def _():
        for w in range(PX + 2):
            act_ref[w, 0] = jnp.zeros((CH, FR), BF16)

    @pl.when(t == NT - 1)
    def _():
        for w in range(PX + 2):
            act_ref[w, 3] = jnp.zeros((CH, FR), BF16)

    @pl.when(q == 0)
    def _():
        for r in range(4):
            act_ref[0, r] = jnp.zeros((CH, FR), BF16)

    @pl.when(q == NQ - 1)
    def _():
        for r in range(4):
            act_ref[PX + 1, r] = jnp.zeros((CH, FR), BF16)


def unit(x, scale):
    return (x * (lax.rsqrt(jnp.sum(x * x, axis=0, keepdims=True) + 1e-06) * scale)).astype(BF16)


def block_net(hs_ref, mid_ref, qkvt_ref, wot_ref, wet_ref, gain_ref, near_ref, hid_ref, act_ref, noise_ref):
    def body(i, carry):
        r, j = lax.div(i, 4), lax.rem(i, 4)
        block = jnp.concatenate([hid_ref[2 * j + 1, r], hid_ref[2 * j + 2, r]], axis=1)
        for dx in range(3):
            rhs = jnp.concatenate(
                [act_ref[2 * j + dx + s, pl.ds(r, 3)].reshape(3 * CH, FR) for s in range(2)], axis=1)
            lhs = jnp.concatenate([mid_ref[dx, dy] for dy in range(3)], axis=1)
            block = block + dot(lhs, rhs)
        center = jnp.mean(block, axis=0, keepdims=True)
        moved = block - center
        spread = jnp.mean(moved * moved, axis=0, keepdims=True)
        gain = jnp.concatenate([gain_ref[...]] * 2, axis=1)
        normed = (moved * lax.rsqrt(spread + 1e-05) * gain).astype(BF16)
        project = dot(qkvt_ref[...], normed)
        mixed = []
        for h in range(HEADS):
            query = unit(project[h * HD : (h + 1) * HD], hs_ref[h] * math.log2(math.e))
            key = unit(project[CH + h * HD : CH + (h + 1) * HD], 1.0)
            value = project[2 * CH + h * HD : 2 * CH + (h + 1) * HD].astype(BF16)
            value = jnp.concatenate([value, jnp.ones((16, 2 * FR), BF16)], axis=0)
            parts = []
            for s in range(2):
                cut = slice(s * FR, (s + 1) * FR)
                scores = dot_t(key[:, cut], query[:, cut])
                weights = jnp.exp2(scores).astype(BF16) * near_ref[...]
                total = dot(value[:, cut], weights)
                parts.append((total[:HD] / total[HD : HD + 1]).astype(BF16))
            mixed.append(jnp.concatenate(parts, axis=1))
        upper = block + dot(wot_ref[...], jnp.concatenate(mixed, axis=0))
        noise_ref[i] = dot(wet_ref[...], silu(upper).astype(BF16))[:8]
        return carry

    lax.fori_loop(0, PX, body, 0)


def advance(state, noise_ref, alpha, beta, entering):
    tiles = []
    for c in range(4):
        for r in range(2):
            rows = [noise_ref[r * 4 + w // 2, c : c + 1, (w % 2) * FR : (w % 2 + 1) * FR] for w in range(PX)]
            noise = jnp.concatenate(rows, axis=0)
            at = c * 16 + r * 8
            tiles.append(alpha * state[at : at + 8] + beta * noise)
    updated = jnp.concatenate(tiles, axis=0)
    return jnp.where(lanes((64, FR)) == FR - 1, entering, pltpu.roll(updated, FR - 1, 1))


def masked(slot, index, q, t):
    inside = (t > 0) if index == 0 else (t < NT - 1) if index == 2 else None
    own, left, right = slot[:64], slot[64:80], slot[80:96]
    left = jnp.where(q > 0, left, 0.0)
    right = jnp.where(q < NQ - 1, right, 0.0)
    slot = jnp.concatenate([own, left, right], axis=0)
    return slot if inside is None else jnp.where(inside, slot, 0.0)


def kernel(lat_ref, ent_ref, lev_ref, tw_hbm, cin_ref, cmid_hbm, gain_ref, qkv_hbm, hs_ref, wo_hbm, we_ref,
           out_ref,
           tw_ref, cmid_ref, qkv_ref, wo_ref, taps_ref,
           band_ref, mid_ref, qkvt_ref, wot_ref, wet_ref, gain_out, near_ref, ent_out,
           emb_ref, rhs_ref, hid_ref, act_ref, noise_ref,
           send1, recv1, halo, own_ref, left_ref, right_ref, send3, recv3,
           load_sem, send1_sem, recv1_sem, send2_sem, recv2_sem, send3_sem, recv3_sem):
    q, t = lax.axis_index("queue"), lax.axis_index("tile")
    loads = [pltpu.make_async_copy(src, dst, load_sem.at[i]) for i, (src, dst) in enumerate(
        [(cmid_hbm, cmid_ref), (qkv_hbm, qkv_ref), (wo_hbm, wo_ref), (tw_hbm, tw_ref)])]
    for load in loads:
        load.start()

    barrier = pltpu.get_barrier_semaphore()
    above, below = lax.rem(t + NT - 1, NT), lax.rem(t + 1, NT)

    def greet(k, carry):
        peer = lax.rem(q + k, NQ)
        pl.semaphore_signal(barrier, inc=1, device_id=(peer, above), device_id_type=MESH)
        pl.semaphore_signal(barrier, inc=1, device_id=(peer, below), device_id_type=MESH)
        return carry

    def greet_row(k, carry):
        pl.semaphore_signal(barrier, inc=1, device_id=(lax.rem(q + k, NQ), t), device_id_type=MESH)
        return carry

    lax.fori_loop(0, NQ, greet, 0)
    lax.fori_loop(1, NQ, greet_row, 0)
    pack_latents(lat_ref, lev_ref, send1)
    pl.semaphore_wait(barrier, 3 * NQ - 1)

    place = pl.ds(pl.multiple_of(q * 8, 8), 8)

    def to_peer(peer, row, slot):
        pltpu.make_async_remote_copy(
            src_ref=send1.at[peer], dst_ref=recv1.at[slot, place],
            send_sem=send1_sem.at[slot], recv_sem=recv1_sem.at[slot],
            device_id=(peer, row), device_id_type=MESH).start()

    def scatter_row(k, carry):
        to_peer(lax.rem(q + k, NQ), t, 1)
        return carry

    def scatter(k, carry):
        peer = lax.rem(q + k, NQ)
        to_peer(peer, above, 2)
        to_peer(peer, below, 0)
        return carry

    lax.fori_loop(1, NQ, scatter_row, 0)
    lax.fori_loop(0, NQ, scatter, 0)
    recv1[1, place] = send1[q]

    for load in loads:
        load.wait()
    prepare(cin_ref, cmid_ref, gain_ref, qkv_ref, wo_ref, we_ref, ent_ref, taps_ref,
            band_ref, mid_ref, qkvt_ref, wot_ref, wet_ref, gain_out, near_ref, ent_out, q)

    for slot in range(3):
        count = FR if slot != 1 else FR - 8
        part = recv1.at[slot, pl.ds(0, count)]
        pltpu.make_async_copy(part, part, recv1_sem.at[slot]).wait()
    slots = [recv1[slot].T for slot in range(3)]
    level = slots[1][2 * ROW : 2 * ROW + 1]
    embed(level, tw_ref, emb_ref)
    alpha, beta = coefficients(level)
    state = slots[1][:64]
    slots = [masked(slot[: 2 * ROW], i, q, t) for i, slot in enumerate(slots)]

    conv_in(slots, band_ref, emb_ref, rhs_ref, hid_ref, act_ref, q, t)
    block_net(hs_ref, mid_ref, qkvt_ref, wot_ref, wet_ref, gain_out, near_ref, hid_ref, act_ref, noise_ref)
    state = advance(state, noise_ref, alpha, beta, ent_out[0])

    own_ref[...] = state
    for r in range(2):
        for c in range(4):
            at = c * 16 + r * 8
            left_ref[r * 8 + c * 2 : r * 8 + c * 2 + 2, :] = state[at + 6 : at + 8]
            right_ref[r * 8 + c * 2 : r * 8 + c * 2 + 2, :] = state[at : at + 2]
    before, after = lax.rem(q + NQ - 1, NQ), lax.rem(q + 1, NQ)
    copies = []
    for row, slot in ((t, 1), (above, 2), (below, 0)):
        if slot != 1:
            copies.append((own_ref, (0, 64), q, row, slot))
        copies.append((left_ref, (64, 16), after, row, slot))
        copies.append((right_ref, (80, 16), before, row, slot))
    copies = [
        pltpu.make_async_remote_copy(
            src_ref=src, dst_ref=halo.at[slot, pl.ds(start, size)],
            send_sem=send2_sem.at[i], recv_sem=recv2_sem.at[i],
            device_id=(peer, row), device_id_type=MESH)
        for i, (src, (start, size), peer, row, slot) in enumerate(copies)]
    for copy in copies:
        copy.start()
    for copy in copies:
        copy.wait_recv()
    halo[1, :64] = own_ref[...]
    slots = [masked(halo[i], i, q, t) for i in range(3)]

    conv_in(slots, band_ref, emb_ref, rhs_ref, hid_ref, act_ref, q, t)
    block_net(hs_ref, mid_ref, qkvt_ref, wot_ref, wet_ref, gain_out, near_ref, hid_ref, act_ref, noise_ref)
    state = advance(own_ref[...], noise_ref, alpha, beta, ent_out[1])

    frames = jnp.concatenate([state, jnp.zeros((64, FR), F32)], axis=0).T
    for peer in range(NQ):
        send3[peer] = frames[peer * 8 : peer * 8 + 8]

    def give(k, carry):
        peer = lax.rem(q + k, NQ)
        pltpu.make_async_remote_copy(
            src_ref=send3.at[peer], dst_ref=recv3.at[q],
            send_sem=send3_sem.at[0], recv_sem=recv3_sem.at[0],
            device_id=(peer, t), device_id_type=MESH).start()
        return carry

    lax.fori_loop(1, NQ, give, 0)
    recv3[q] = send3[q]
    for copy in copies:
        copy.wait_send()
    for slot in range(3):
        part = send1.at[pl.ds(0, NQ if slot != 1 else NQ - 1)]
        pltpu.make_async_copy(part, part, send1_sem.at[slot]).wait()
    part = recv3.at[pl.ds(0, NQ - 1)]
    pltpu.make_async_copy(part, part, recv3_sem.at[0]).wait()
    part = send3.at[pl.ds(0, NQ - 1)]
    pltpu.make_async_copy(part, part, send3_sem.at[0]).wait()

    lane = lanes((8, FR))
    for c in range(4):
        for r in range(2):
            at = c * 16 + r * 8
            total = jnp.zeros((8, FR), F32)
            for source in range(NQ):
                moved = pltpu.roll(recv3[source], (FR + 8 * source - at) % FR, 1)
                total = jnp.where((lane >> 3) == source, moved, total)
            out_ref[:, c, r, :] = total


def per_device(queue_latents, entering, levels, time_weight, conv_in_weight, conv_mid_weight, norm_gain,
               qkv_weight, head_scale, attn_out_weight, eps_out_weight):
    vmem = pl.BlockSpec(memory_space=pltpu.VMEM)
    smem = pl.BlockSpec(memory_space=pltpu.SMEM)
    hbm = pl.BlockSpec(memory_space=pl.ANY)
    v = pltpu.VMEM
    dma = pltpu.SemaphoreType.DMA
    return pl.pallas_call(
        kernel,
        out_shape=jax.ShapeDtypeStruct(queue_latents.shape, F32),
        in_specs=[vmem, vmem, smem, hbm, vmem, hbm, vmem, hbm, smem, hbm, vmem],
        out_specs=vmem,
        scratch_shapes=[
            v((CH, CH), F32), v((3, 3, CH, CH), BF16), v((CH, 3 * CH), BF16), v((CH, CH), BF16), v((40, CH), F32),
            v((PX + 2, CH, TAPS), BF16), v((3, 3, CH, CH), BF16), v((3 * CH, CH), BF16), v((CH, CH), BF16),
            v((16, CH), BF16), v((CH, FR), F32), v((FR, FR), BF16), v((STEPS, 64, FR), F32),
            v((CH, FR), F32), v((2, TAPS, 2 * FR), BF16), v((PX + 2, 2, CH, FR), F32),
            v((PX + 2, 4, CH, FR), BF16), v((PX, 8, 2 * FR), F32),
            v((NQ, 8, FR), F32), v((3, FR, FR), F32), v((3, 2 * ROW, FR), F32), v((64, FR), F32),
            v((16, FR), F32), v((16, FR), F32), v((NQ, 8, FR), F32), v((NQ, 8, FR), F32),
            dma((4,)), dma((3,)), dma((3,)), dma((8,)), dma((8,)), dma((1,)), dma((1,)),
        ],
        compiler_params=pltpu.CompilerParams(
            collective_id=0, has_side_effects=True, vmem_limit_bytes=56 * 1024 * 1024),
    )(queue_latents, entering, levels, time_weight, conv_in_weight, conv_mid_weight,
      norm_gain.reshape(1, CH), qkv_weight, head_scale, attn_out_weight, eps_out_weight)


def solution(mesh):
    placed = (
        P("queue", None, "tile", None),
        P(None, None, "tile", None),
        P("queue"),
        P(),
        P(),
        P(),
        P(),
        P(),
        P(),
        P(),
        P(),
    )
    return jax.shard_map(
        per_device,
        mesh=mesh,
        in_specs=placed,
        out_specs=P("queue", None, "tile", None),
        check_vma=False,
    )
```

```python
import math

import jax
import jax.numpy as jnp
from jax import lax
from jax.experimental import pallas as pl
from jax.experimental.pallas import tpu as pltpu
from jax.sharding import PartitionSpec as P

WIN = 8
STEPS = 2
F32 = jnp.float32
BF16 = jnp.bfloat16
MESH = pl.DeviceIdType.MESH

CH = 320
HEADS = 5
HD = 64
FR = 128
NQ = 16
NT = 8
PX = 8
ROW = 48
TAPS = 3 * ROW


def dot(a, b):
    return jnp.dot(a, b, preferred_element_type=F32)


def dot_t(a, b):
    return lax.dot_general(a, b, (((0,), (0,)), ((), ())), preferred_element_type=F32)


def sin_cos(angle):
    count = jnp.floor(angle * (2.0 / math.pi) + 0.5)
    rest = ((angle - count * 1.5703125) - count * 4.837512969970703125e-4) - count * 7.54978995489188216e-8
    square = rest * rest
    sine = rest + rest * square * (
        -1.6666654611e-1 + square * (8.3321608736e-3 - square * 1.9515295891e-4)
    )
    cosine = 1.0 - 0.5 * square + square * square * (
        4.166664568298827e-2 + square * (-1.388731625493765e-3 + square * 2.443315711809948e-5)
    )
    quarter = count - 4.0 * jnp.floor(count * 0.25)
    odd = (quarter == 1.0) | (quarter == 3.0)
    sin_out = jnp.where(odd, cosine, sine)
    cos_out = jnp.where(odd, sine, cosine)
    sin_out = jnp.where(quarter >= 2.0, -sin_out, sin_out)
    cos_out = jnp.where((quarter == 1.0) | (quarter == 2.0), -cos_out, cos_out)
    return sin_out, cos_out


def silu(x):
    half = 0.5 * x
    return half + half * jnp.tanh(half)


def lanes(shape):
    return lax.broadcasted_iota(jnp.int32, shape, 1)


def pack_latents(lat_ref, lev_ref, send_ref):
    lane = lanes((8, FR))
    row = lax.broadcasted_iota(jnp.int32, (8, FR), 0)
    pieces = []
    for c in range(4):
        for r in range(2):
            plane = lat_ref[:, c, r, :]
            own, left, right = c * 16 + r * 8, 64 + r * 8 + c * 2, 80 + r * 8 + c * 2
            pieces.append((3, own, pltpu.roll(plane, own, 1)))
            pieces.append((1, left, pltpu.roll(plane, left + 2, 1)))
            pieces.append((1, right, pltpu.roll(plane, right - 8, 1)))
    level = jnp.zeros((8, FR), F32)
    for f in range(8):
        level = jnp.where(row == f, lev_ref[f].astype(F32), level)

    def body(dest, carry):
        place = (lane - 8 * dest) & (FR - 1)
        total = jnp.zeros((8, FR), F32)
        for bits, base, plane in pieces:
            total = jnp.where((place >> bits) == (base >> bits), plane, total)
        total = pltpu.roll(total, lax.rem(FR - 8 * dest, FR), 1)
        send_ref[dest] = jnp.where(lane == 2 * ROW, level, total)
        return carry

    lax.fori_loop(0, NQ, body, 0)


def prepare(cin_ref, cmid_ref, gain_ref, qkv_ref, wo_ref, we_ref, ent_ref, taps_ref,
            band_ref, mid_ref, qkvt_ref, wot_ref, wet_ref, gain_out, near_ref, ent_out, q):
    taps_ref[...] = jnp.zeros(taps_ref.shape, F32)
    for i in range(9):
        taps_ref[4 * i : 4 * i + 4, :] = cin_ref[i // 3, i % 3].astype(F32)
    taps_t = taps_ref[...].T.astype(BF16)
    k = lanes((40, TAPS))
    m = lax.broadcasted_iota(jnp.int32, (40, TAPS), 0)
    dy = (k >= ROW).astype(jnp.int32) + (k >= 2 * ROW).astype(jnp.int32)
    rest = k - ROW * dy
    own = rest < 32
    left = rest < 40
    c = jnp.where(own, rest >> 3, (rest & 7) >> 1)
    rel = jnp.where(own, (rest & 7) + 2, jnp.where(left, rest & 1, (rest & 1) + 10))
    for w in range(PX + 2):
        dx = rel - w
        pick = (dx >= 0) & (dx <= 2) & (m == dy * 12 + dx * 4 + c)
        band_ref[w] = dot(taps_t, jnp.where(pick, 1.0, 0.0).astype(BF16)).astype(BF16)
    for dx in range(3):
        mid_ref[dx] = jnp.concatenate([cmid_ref[dy_, dx] for dy_ in range(3)], axis=0).T
    qkvt_ref[...] = qkv_ref[...].T
    wot_ref[...] = wo_ref[...].T
    eps = jnp.concatenate([we_ref[...].astype(F32), jnp.zeros((CH, FR - 4), F32)], axis=1)
    wet_ref[...] = eps.T[:16].astype(BF16)
    gain_out[...] = jnp.broadcast_to(gain_ref[...], (FR, CH)).T
    key_slot = lax.broadcasted_iota(jnp.int32, (FR, FR), 0)
    query_slot = lanes((FR, FR))
    near_ref[...] = jnp.where(jnp.abs(key_slot - query_slot) <= WIN, 1.0, 0.0).astype(BF16)
    lane = lanes((8, FR))
    for s in range(STEPS):
        rows = jnp.concatenate([ent_ref[s, c, r : r + 1, :] for c in range(4) for r in range(2)], axis=0)
        rows = pltpu.roll(rows, lax.rem(FR - 8 * q, FR), 1)
        columns = jnp.concatenate([rows, jnp.zeros((FR - 8, FR), F32)], axis=0).T[:8]
        for i in range(8):
            shifted = pltpu.roll(columns, FR - 1 - i, 1)
            ent_out[s, 8 * i : 8 * i + 8, :] = jnp.where(lane == FR - 1, shifted, 0.0)


def embed(level, tw_ref, emb_ref):
    index = lax.broadcasted_iota(jnp.int32, (CH // 2, FR), 0).astype(F32)
    freqs = jnp.exp(-math.log(10000.0) * index / (CH // 2))
    sine, cosine = sin_cos(level * freqs)
    feature = jnp.concatenate([sine, cosine], axis=0)
    emb_ref[...] = lax.dot_general(
        tw_ref[...].T, feature, (((1,), (0,)), ((), ())),
        precision=lax.Precision.HIGHEST, preferred_element_type=F32)


def coefficients(level):
    lane = lanes((8, FR))
    level = jnp.broadcast_to(level, (8, FR))
    target = jnp.where(lane == 0, 0.0, pltpu.roll(level, 1, 1))
    angle = lambda l: (l / 1000.0 + 0.008) / 1.008 * (math.pi / 2.0)
    s0, c0 = sin_cos(angle(level))
    s1, c1 = sin_cos(angle(target))
    alpha = c1 / c0
    return alpha, s1 - alpha * s0


def conv_in(slots, band_ref, emb_ref, rhs_ref, hid_ref, act_ref, q, t):
    rows = []
    for slot in slots:
        for r in range(2):
            rows.append(jnp.concatenate(
                [slot[g * 16 + r * 8 : g * 16 + r * 8 + 8] for g in range(6)], axis=0).astype(BF16))
    for p in range(2):
        for half in range(2):
            rhs_ref[p, :, half * FR : (half + 1) * FR] = jnp.concatenate(
                rows[2 * p + half : 2 * p + half + 3], axis=0)

    def body(w, carry):
        for p in range(2):
            both = dot(band_ref[w], rhs_ref[p])
            for half in range(2):
                hidden = both[:, half * FR : (half + 1) * FR] + emb_ref[...]
                act_ref[w, 2 * p + half] = silu(hidden).astype(BF16)
                if p != half:
                    hid_ref[w, p] = hidden
        return carry

    lax.fori_loop(0, PX + 2, body, 0, unroll=5)

    @pl.when(t == 0)
    def _():
        for w in range(PX + 2):
            act_ref[w, 0] = jnp.zeros((CH, FR), BF16)

    @pl.when(t == NT - 1)
    def _():
        for w in range(PX + 2):
            act_ref[w, 3] = jnp.zeros((CH, FR), BF16)

    @pl.when(q == 0)
    def _():
        for r in range(4):
            act_ref[0, r] = jnp.zeros((CH, FR), BF16)

    @pl.when(q == NQ - 1)
    def _():
        for r in range(4):
            act_ref[PX + 1, r] = jnp.zeros((CH, FR), BF16)


def unit(x, scale):
    return (x * (lax.rsqrt(jnp.sum(x * x, axis=0, keepdims=True) + 1e-06) * scale)).astype(BF16)


def each_pair(bodies):
    def step(i, carry):
        for body in bodies:
            body(i)
        return carry

    lax.fori_loop(0, PX, step, 0, unroll=PX)


def block_net(hs_ref, mid_ref, qkvt_ref, wot_ref, wet_ref, gain_ref, near_ref, hid_ref, act_ref, noise_ref,
              block_ref, normed_ref, project_ref, unit_ref, key_ref, weight_ref, mixed_ref):
    def conv_mid(i):
        r, j = lax.div(i, 4), lax.rem(i, 4)
        block = jnp.concatenate([hid_ref[2 * j + 1, r], hid_ref[2 * j + 2, r]], axis=1)
        for dx in range(3):
            rhs = jnp.concatenate(
                [act_ref[2 * j + dx + s, pl.ds(r, 3)].reshape(3 * CH, FR) for s in range(2)], axis=1)
            block = block + dot(mid_ref[dx], rhs)
        block_ref[i] = block

    def norm(i):
        block = block_ref[i]
        center = jnp.mean(block, axis=0, keepdims=True)
        moved = block - center
        spread = jnp.mean(moved * moved, axis=0, keepdims=True)
        gain = jnp.concatenate([gain_ref[...]] * 2, axis=1)
        normed_ref[i] = (moved * lax.rsqrt(spread + 1e-05) * gain).astype(BF16)

    def project(i):
        project_ref[i] = dot(qkvt_ref[...], normed_ref[i])

    def units(i):
        for h in range(HEADS):
            at = h * HD
            unit_ref[i, at : at + HD] = unit(project_ref[i, at : at + HD], hs_ref[h] * math.log2(math.e))
            at = CH + h * HD
            unit_ref[i, at : at + HD] = unit(project_ref[i, at : at + HD], 1.0)
            at = 2 * CH + h * HD
            unit_ref[i, at : at + HD] = project_ref[i, at : at + HD].astype(BF16)

    def turn_keys(i):
        key_ref[i] = unit_ref[i, CH : 2 * CH].T

    def attend(i):
        for h in range(HEADS):
            for s in range(2):
                cut = slice(s * FR, (s + 1) * FR)
                scores = dot(key_ref[i, cut, h * HD : (h + 1) * HD], unit_ref[i, h * HD : (h + 1) * HD, cut])
                weight_ref[i, 2 * h + s] = jnp.exp2(scores).astype(BF16) * near_ref[...]

    def mix(i):
        ones = jnp.ones((16, 2 * FR), BF16)
        for h in range(HEADS):
            at = 2 * CH + h * HD
            value = jnp.concatenate([unit_ref[i, at : at + HD], ones], axis=0)
            for s in range(2):
                cut = slice(s * FR, (s + 1) * FR)
                total = dot(value[:, cut], weight_ref[i, 2 * h + s])
                mixed_ref[i, h * HD : (h + 1) * HD, cut] = (total[:HD] * (1.0 / total[HD : HD + 1])).astype(BF16)

    def upper(i):
        block_ref[i] = block_ref[i] + dot(wot_ref[...], mixed_ref[i])

    def active(i):
        normed_ref[i] = silu(block_ref[i]).astype(BF16)

    def noise(i):
        noise_ref[i] = dot(wet_ref[...], normed_ref[i])[:8]

    for bodies in ((conv_mid, norm), (project, units, turn_keys), (attend,), (mix,), (upper, active), (noise,)):
        each_pair(bodies)


def advance(state, noise_ref, alpha, beta, entering):
    tiles = []
    for c in range(4):
        for r in range(2):
            rows = [noise_ref[r * 4 + w // 2, c : c + 1, (w % 2) * FR : (w % 2 + 1) * FR] for w in range(PX)]
            noise = jnp.concatenate(rows, axis=0)
            at = c * 16 + r * 8
            tiles.append(alpha * state[at : at + 8] + beta * noise)
    updated = jnp.concatenate(tiles, axis=0)
    return jnp.where(lanes((64, FR)) == FR - 1, entering, pltpu.roll(updated, FR - 1, 1))


def masked(slot, index, q, t):
    inside = (t > 0) if index == 0 else (t < NT - 1) if index == 2 else None
    own, left, right = slot[:64], slot[64:80], slot[80:96]
    left = jnp.where(q > 0, left, 0.0)
    right = jnp.where(q < NQ - 1, right, 0.0)
    slot = jnp.concatenate([own, left, right], axis=0)
    return slot if inside is None else jnp.where(inside, slot, 0.0)


def kernel(lat_ref, ent_ref, lev_ref, tw_hbm, cin_ref, cmid_hbm, gain_ref, qkv_hbm, hs_ref, wo_hbm, we_ref,
           out_ref,
           tw_ref, cmid_ref, qkv_ref, wo_ref, taps_ref,
           band_ref, mid_ref, qkvt_ref, wot_ref, wet_ref, gain_out, near_ref, ent_out,
           emb_ref, rhs_ref, hid_ref, act_ref, noise_ref,
           block_ref, normed_ref, project_ref, unit_ref, key_ref, weight_ref, mixed_ref,
           send1, recv1, halo, own_ref, left_ref, right_ref, send3, recv3,
           load_sem, send1_sem, recv1_sem, send2_sem, recv2_sem, send3_sem, recv3_sem):
    q, t = lax.axis_index("queue"), lax.axis_index("tile")
    loads = [pltpu.make_async_copy(src, dst, load_sem.at[i]) for i, (src, dst) in enumerate(
        [(cmid_hbm, cmid_ref), (qkv_hbm, qkv_ref), (wo_hbm, wo_ref), (tw_hbm, tw_ref)])]
    for load in loads:
        load.start()

    barrier = pltpu.get_barrier_semaphore()
    above, below = lax.rem(t + NT - 1, NT), lax.rem(t + 1, NT)

    def greet(k, carry):
        peer = lax.rem(q + k, NQ)
        pl.semaphore_signal(barrier, inc=1, device_id=(peer, above), device_id_type=MESH)
        pl.semaphore_signal(barrier, inc=1, device_id=(peer, below), device_id_type=MESH)
        return carry

    def greet_row(k, carry):
        pl.semaphore_signal(barrier, inc=1, device_id=(lax.rem(q + k, NQ), t), device_id_type=MESH)
        return carry

    lax.fori_loop(0, NQ, greet, 0)
    lax.fori_loop(1, NQ, greet_row, 0)
    pack_latents(lat_ref, lev_ref, send1)
    pl.semaphore_wait(barrier, 3 * NQ - 1)

    place = pl.ds(pl.multiple_of(q * 8, 8), 8)

    def to_peer(peer, row, slot):
        pltpu.make_async_remote_copy(
            src_ref=send1.at[peer], dst_ref=recv1.at[slot, place],
            send_sem=send1_sem.at[slot], recv_sem=recv1_sem.at[slot],
            device_id=(peer, row), device_id_type=MESH).start()

    def scatter_row(k, carry):
        to_peer(lax.rem(q + k, NQ), t, 1)
        return carry

    def scatter(k, carry):
        peer = lax.rem(q + k, NQ)
        to_peer(peer, above, 2)
        to_peer(peer, below, 0)
        return carry

    lax.fori_loop(1, NQ, scatter_row, 0)
    lax.fori_loop(0, NQ, scatter, 0)
    recv1[1, place] = send1[q]

    for load in loads:
        load.wait()
    prepare(cin_ref, cmid_ref, gain_ref, qkv_ref, wo_ref, we_ref, ent_ref, taps_ref,
            band_ref, mid_ref, qkvt_ref, wot_ref, wet_ref, gain_out, near_ref, ent_out, q)

    for slot in range(3):
        count = FR if slot != 1 else FR - 8
        part = recv1.at[slot, pl.ds(0, count)]
        pltpu.make_async_copy(part, part, recv1_sem.at[slot]).wait()
    slots = [recv1[slot].T for slot in range(3)]
    level = slots[1][2 * ROW : 2 * ROW + 1]
    embed(level, tw_ref, emb_ref)
    alpha, beta = coefficients(level)
    state = slots[1][:64]
    slots = [masked(slot[: 2 * ROW], i, q, t) for i, slot in enumerate(slots)]

    conv_in(slots, band_ref, emb_ref, rhs_ref, hid_ref, act_ref, q, t)
    block_net(hs_ref, mid_ref, qkvt_ref, wot_ref, wet_ref, gain_out, near_ref, hid_ref, act_ref, noise_ref,
              block_ref, normed_ref, project_ref, unit_ref, key_ref, weight_ref, mixed_ref)
    state = advance(state, noise_ref, alpha, beta, ent_out[0])

    own_ref[...] = state
    for r in range(2):
        for c in range(4):
            at = c * 16 + r * 8
            left_ref[r * 8 + c * 2 : r * 8 + c * 2 + 2, :] = state[at + 6 : at + 8]
            right_ref[r * 8 + c * 2 : r * 8 + c * 2 + 2, :] = state[at : at + 2]
    before, after = lax.rem(q + NQ - 1, NQ), lax.rem(q + 1, NQ)
    copies = []
    for row, slot in ((t, 1), (above, 2), (below, 0)):
        if slot != 1:
            copies.append((own_ref, (0, 64), q, row, slot))
        copies.append((left_ref, (64, 16), after, row, slot))
        copies.append((right_ref, (80, 16), before, row, slot))
    copies = [
        pltpu.make_async_remote_copy(
            src_ref=src, dst_ref=halo.at[slot, pl.ds(start, size)],
            send_sem=send2_sem.at[i], recv_sem=recv2_sem.at[i],
            device_id=(peer, row), device_id_type=MESH)
        for i, (src, (start, size), peer, row, slot) in enumerate(copies)]
    for copy in copies:
        copy.start()
    for copy in copies:
        copy.wait_recv()
    halo[1, :64] = own_ref[...]
    slots = [masked(halo[i], i, q, t) for i in range(3)]

    conv_in(slots, band_ref, emb_ref, rhs_ref, hid_ref, act_ref, q, t)
    block_net(hs_ref, mid_ref, qkvt_ref, wot_ref, wet_ref, gain_out, near_ref, hid_ref, act_ref, noise_ref,
              block_ref, normed_ref, project_ref, unit_ref, key_ref, weight_ref, mixed_ref)
    state = advance(own_ref[...], noise_ref, alpha, beta, ent_out[1])

    frames = jnp.concatenate([state, jnp.zeros((64, FR), F32)], axis=0).T
    for peer in range(NQ):
        send3[peer] = frames[peer * 8 : peer * 8 + 8]

    def give(k, carry):
        peer = lax.rem(q + k, NQ)
        pltpu.make_async_remote_copy(
            src_ref=send3.at[peer], dst_ref=recv3.at[q],
            send_sem=send3_sem.at[0], recv_sem=recv3_sem.at[0],
            device_id=(peer, t), device_id_type=MESH).start()
        return carry

    lax.fori_loop(1, NQ, give, 0)
    recv3[q] = send3[q]
    for copy in copies:
        copy.wait_send()
    for slot in range(3):
        part = send1.at[pl.ds(0, NQ if slot != 1 else NQ - 1)]
        pltpu.make_async_copy(part, part, send1_sem.at[slot]).wait()
    part = recv3.at[pl.ds(0, NQ - 1)]
    pltpu.make_async_copy(part, part, recv3_sem.at[0]).wait()
    part = send3.at[pl.ds(0, NQ - 1)]
    pltpu.make_async_copy(part, part, send3_sem.at[0]).wait()

    lane = lanes((8, FR))
    for c in range(4):
        for r in range(2):
            at = c * 16 + r * 8
            total = jnp.zeros((8, FR), F32)
            for source in range(NQ):
                moved = pltpu.roll(recv3[source], (FR + 8 * source - at) % FR, 1)
                total = jnp.where((lane >> 3) == source, moved, total)
            out_ref[:, c, r, :] = total


def per_device(queue_latents, entering, levels, time_weight, conv_in_weight, conv_mid_weight, norm_gain,
               qkv_weight, head_scale, attn_out_weight, eps_out_weight):
    vmem = pl.BlockSpec(memory_space=pltpu.VMEM)
    smem = pl.BlockSpec(memory_space=pltpu.SMEM)
    hbm = pl.BlockSpec(memory_space=pl.ANY)
    v = pltpu.VMEM
    dma = pltpu.SemaphoreType.DMA
    return pl.pallas_call(
        kernel,
        out_shape=jax.ShapeDtypeStruct(queue_latents.shape, F32),
        in_specs=[vmem, vmem, smem, hbm, vmem, hbm, vmem, hbm, smem, hbm, vmem],
        out_specs=vmem,
        scratch_shapes=[
            v((CH, CH), F32), v((3, 3, CH, CH), BF16), v((CH, 3 * CH), BF16), v((CH, CH), BF16), v((40, CH), F32),
            v((PX + 2, CH, TAPS), BF16), v((3, CH, 3 * CH), BF16), v((3 * CH, CH), BF16), v((CH, CH), BF16),
            v((16, CH), BF16), v((CH, FR), F32), v((FR, FR), BF16), v((STEPS, 64, FR), F32),
            v((CH, FR), F32), v((2, TAPS, 2 * FR), BF16), v((PX + 2, 2, CH, FR), F32),
            v((PX + 2, 4, CH, FR), BF16), v((PX, 8, 2 * FR), F32),
            v((PX, CH, 2 * FR), F32), v((PX, CH, 2 * FR), BF16), v((PX, 3 * CH, 2 * FR), F32),
            v((PX, 3 * CH, 2 * FR), BF16), v((PX, 2 * FR, CH), BF16), v((PX, 2 * HEADS, FR, FR), BF16),
            v((PX, CH, 2 * FR), BF16),
            v((NQ, 8, FR), F32), v((3, FR, FR), F32), v((3, 2 * ROW, FR), F32), v((64, FR), F32),
            v((16, FR), F32), v((16, FR), F32), v((NQ, 8, FR), F32), v((NQ, 8, FR), F32),
            dma((4,)), dma((3,)), dma((3,)), dma((8,)), dma((8,)), dma((1,)), dma((1,)),
        ],
        compiler_params=pltpu.CompilerParams(
            collective_id=0, has_side_effects=True, vmem_limit_bytes=56 * 1024 * 1024),
    )(queue_latents, entering, levels, time_weight, conv_in_weight, conv_mid_weight,
      norm_gain.reshape(1, CH), qkv_weight, head_scale, attn_out_weight, eps_out_weight)


def solution(mesh):
    placed = (
        P("queue", None, "tile", None),
        P(None, None, "tile", None),
        P("queue"),
        P(),
        P(),
        P(),
        P(),
        P(),
        P(),
        P(),
        P(),
    )
    return jax.shard_map(
        per_device,
        mesh=mesh,
        in_specs=placed,
        out_specs=P("queue", None, "tile", None),
        check_vma=False,
    )
```

```python
import math

import jax
import jax.numpy as jnp
from jax import lax
from jax.experimental import pallas as pl
from jax.experimental.pallas import tpu as pltpu
from jax.sharding import PartitionSpec as P

WIN = 8
STEPS = 2
F32 = jnp.float32
BF16 = jnp.bfloat16
MESH = pl.DeviceIdType.MESH

CH = 320
HEADS = 5
HD = 64
FR = 128
NQ = 16
NT = 8
PX = 8
ROW = 48
TAPS = 3 * ROW


def dot(a, b):
    return jnp.dot(a, b, preferred_element_type=F32)


def dot_t(a, b):
    return lax.dot_general(a, b, (((0,), (0,)), ((), ())), preferred_element_type=F32)


def sin_cos(angle):
    count = jnp.floor(angle * (2.0 / math.pi) + 0.5)
    rest = ((angle - count * 1.5703125) - count * 4.837512969970703125e-4) - count * 7.54978995489188216e-8
    square = rest * rest
    sine = rest + rest * square * (
        -1.6666654611e-1 + square * (8.3321608736e-3 - square * 1.9515295891e-4)
    )
    cosine = 1.0 - 0.5 * square + square * square * (
        4.166664568298827e-2 + square * (-1.388731625493765e-3 + square * 2.443315711809948e-5)
    )
    quarter = count - 4.0 * jnp.floor(count * 0.25)
    odd = (quarter == 1.0) | (quarter == 3.0)
    sin_out = jnp.where(odd, cosine, sine)
    cos_out = jnp.where(odd, sine, cosine)
    sin_out = jnp.where(quarter >= 2.0, -sin_out, sin_out)
    cos_out = jnp.where((quarter == 1.0) | (quarter == 2.0), -cos_out, cos_out)
    return sin_out, cos_out


def silu(x):
    half = 0.5 * x
    return half + half * jnp.tanh(half)


def lanes(shape):
    return lax.broadcasted_iota(jnp.int32, shape, 1)


def pack_latents(lat_ref, lev_ref, send_ref):
    lane = lanes((8, FR))
    row = lax.broadcasted_iota(jnp.int32, (8, FR), 0)
    pieces = []
    for c in range(4):
        for r in range(2):
            plane = lat_ref[:, c, r, :]
            own, left, right = c * 16 + r * 8, 64 + r * 8 + c * 2, 80 + r * 8 + c * 2
            pieces.append((3, own, pltpu.roll(plane, own, 1)))
            pieces.append((1, left, pltpu.roll(plane, left + 2, 1)))
            pieces.append((1, right, pltpu.roll(plane, right - 8, 1)))
    level = jnp.zeros((8, FR), F32)
    for f in range(8):
        level = jnp.where(row == f, lev_ref[f].astype(F32), level)

    def body(dest, carry):
        place = (lane - 8 * dest) & (FR - 1)
        total = jnp.zeros((8, FR), F32)
        for bits, base, plane in pieces:
            total = jnp.where((place >> bits) == (base >> bits), plane, total)
        total = pltpu.roll(total, lax.rem(FR - 8 * dest, FR), 1)
        send_ref[dest] = jnp.where(lane == 2 * ROW, level, total)
        return carry

    lax.fori_loop(0, NQ, body, 0)


def prepare(cin_ref, cmid_ref, gain_ref, qkv_ref, wo_ref, we_ref, ent_ref, taps_ref,
            band_ref, mid_ref, qkvt_ref, wot_ref, wet_ref, gain_out, near_ref, ent_out, q):
    taps_ref[...] = jnp.zeros(taps_ref.shape, F32)
    for i in range(9):
        taps_ref[4 * i : 4 * i + 4, :] = cin_ref[i // 3, i % 3].astype(F32)
    taps_t = taps_ref[...].T.astype(BF16)
    k = lanes((40, TAPS))
    m = lax.broadcasted_iota(jnp.int32, (40, TAPS), 0)
    dy = (k >= ROW).astype(jnp.int32) + (k >= 2 * ROW).astype(jnp.int32)
    rest = k - ROW * dy
    own = rest < 32
    left = rest < 40
    c = jnp.where(own, rest >> 3, (rest & 7) >> 1)
    rel = jnp.where(own, (rest & 7) + 2, jnp.where(left, rest & 1, (rest & 1) + 10))
    for w in range(PX + 2):
        dx = rel - w
        pick = (dx >= 0) & (dx <= 2) & (m == dy * 12 + dx * 4 + c)
        band_ref[w] = dot(taps_t, jnp.where(pick, 1.0, 0.0).astype(BF16)).astype(BF16)
    taps = [jnp.concatenate([cmid_ref[dy, dx].astype(F32) for dx in range(3)], axis=0) for dy in range(3)]
    outer = 0.5 * (taps[0] + taps[2])
    for v, mid in enumerate((taps[0], outer + 0.5 * taps[1], outer - 0.5 * taps[1], taps[2])):
        mid_ref[v] = mid.astype(BF16).T
    qkvt_ref[...] = qkv_ref[...].T
    wot_ref[...] = wo_ref[...].T
    wet_ref[...] = jnp.concatenate([we_ref[...].astype(F32), jnp.zeros((12, CH), F32)], axis=0).astype(BF16)
    gain_out[...] = jnp.broadcast_to(gain_ref[...].reshape(1, CH), (FR, CH)).T
    key_slot = lax.broadcasted_iota(jnp.int32, (FR, FR), 0)
    query_slot = lanes((FR, FR))
    near_ref[...] = jnp.where(jnp.abs(key_slot - query_slot) <= WIN, 1.0, 0.0).astype(BF16)
    lane = lanes((8, FR))
    for s in range(STEPS):
        rows = jnp.concatenate([ent_ref[s, c, r : r + 1, :] for c in range(4) for r in range(2)], axis=0)
        rows = pltpu.roll(rows, lax.rem(FR - 8 * q, FR), 1)
        columns = jnp.concatenate([rows, jnp.zeros((FR - 8, FR), F32)], axis=0).T[:8]
        for i in range(8):
            shifted = pltpu.roll(columns, FR - 1 - i, 1)
            ent_out[s, 8 * i : 8 * i + 8, :] = jnp.where(lane == FR - 1, shifted, 0.0)


def blank(query_ref, value_ref, weight_ref):
    def body(i, carry):
        for p in range(5):
            query_ref[i, p, :HD, FR:] = jnp.zeros((HD, FR), BF16)
            query_ref[i, p, HD:, :FR] = jnp.zeros((HD, FR), BF16)
            value_ref[i, p, HD:] = jnp.ones((16, 2 * FR), BF16)
            weight_ref[i, p, :FR, FR:] = jnp.zeros((FR, FR), BF16)
            weight_ref[i, p, FR:, :FR] = jnp.zeros((FR, FR), BF16)
        return carry

    lax.fori_loop(0, PX, body, 0)


def embed(level, tw_ref, emb_ref):
    index = lax.broadcasted_iota(jnp.int32, (CH // 2, FR), 0).astype(F32)
    freqs = jnp.exp(-math.log(10000.0) * index / (CH // 2))
    sine, cosine = sin_cos(level * freqs)
    feature = jnp.concatenate([sine, cosine], axis=0)
    emb_ref[...] = lax.dot_general(
        tw_ref[...].T, feature, (((1,), (0,)), ((), ())),
        precision=lax.Precision.HIGHEST, preferred_element_type=F32)


def coefficients(level):
    lane = lanes((8, FR))
    level = jnp.broadcast_to(level, (8, FR))
    target = jnp.where(lane == 0, 0.0, pltpu.roll(level, 1, 1))
    angle = lambda l: (l / 1000.0 + 0.008) / 1.008 * (math.pi / 2.0)
    s0, c0 = sin_cos(angle(level))
    s1, c1 = sin_cos(angle(target))
    alpha = c1 / c0
    return alpha, s1 - alpha * s0


def conv_in(slots, band_ref, emb_ref, rhs_ref, hid_ref, act_ref, q, t):
    rows = []
    for slot in slots:
        for r in range(2):
            rows.append(jnp.concatenate(
                [slot[g * 16 + r * 8 : g * 16 + r * 8 + 8] for g in range(6)], axis=0).astype(BF16))
    for p in range(2):
        for half in range(2):
            rhs_ref[p, :, half * FR : (half + 1) * FR] = jnp.concatenate(
                rows[2 * p + half : 2 * p + half + 3], axis=0)

    def body(w, carry):
        inside = ((w > 0) | (q > 0)) & ((w < PX + 1) | (q < NQ - 1))
        active = []
        for p in range(2):
            both = dot(band_ref[w], rhs_ref[p])
            for half in range(2):
                hidden = both[:, half * FR : (half + 1) * FR] + emb_ref[...]
                if p != half:
                    hid_ref[w, p] = hidden
                    active.append(jnp.where(inside, silu(hidden), 0.0))
                else:
                    active.append(jnp.where(inside & ((t > 0) if p == 0 else (t < NT - 1)), silu(hidden), 0.0))
        a0, a1, a2, a3 = active
        for v, part in enumerate((a0 - a2, a1 + a2, a2 - a1, a1 - a3)):
            act_ref[w, v] = part.astype(BF16)
        return carry

    lax.fori_loop(0, PX + 2, body, 0, unroll=5)


def unit(x, scale):
    return (x * (lax.rsqrt(jnp.sum(x * x, axis=0, keepdims=True) + 1e-06) * scale)).astype(BF16)


def each(bodies, count):
    def step(i, carry):
        for body in bodies:
            body(i)
        return carry

    lax.fori_loop(0, count, step, 0, unroll=count)


def places():
    pairs = [((s, 2 * p), (s, 2 * p + 1)) for s in range(2) for p in range(2)]
    return pairs + [((0, 4), (1, 4))]


def block_net(hs_ref, mid_ref, qkvt_ref, wot_ref, wet_ref, gain_ref, near_ref, hid_ref, act_ref, noise_ref,
              block_ref, normed_ref, project_ref, query_ref, stack_ref, key_ref, value_ref, weight_ref, mixed_ref):
    def norm(i, block):
        block_ref[i] = block
        center = jnp.mean(block, axis=0, keepdims=True)
        moved = block - center
        spread = jnp.mean(moved * moved, axis=0, keepdims=True)
        gain = jnp.concatenate([gain_ref[...]] * 2, axis=1)
        normed_ref[i] = (moved * lax.rsqrt(spread + 1e-05) * gain).astype(BF16)

    def conv_mid(j):
        parts = []
        for v in range(4):
            rhs = [jnp.concatenate([act_ref[2 * j + dx, v], act_ref[2 * j + dx + 1, v]], axis=1) for dx in range(3)]
            parts.append(dot(mid_ref[v], jnp.concatenate(rhs, axis=0)))
        for r, part in enumerate((parts[0] + (parts[1] + parts[2]), (parts[1] - parts[2]) - parts[3])):
            hidden = jnp.concatenate([hid_ref[2 * j + 1, r], hid_ref[2 * j + 2, r]], axis=1)
            norm(4 * r + j, hidden + part)

    def project(i):
        project_ref[i] = dot(qkvt_ref[...], normed_ref[i])

    def units(i):
        for p, pair in enumerate(places()):
            for n, (s, h) in enumerate(pair):
                cut, own = slice(s * FR, (s + 1) * FR), slice(n * FR, (n + 1) * FR)
                part = lambda k: project_ref[i, k * CH + h * HD : k * CH + (h + 1) * HD, cut]
                query_ref[i, p, n * HD : (n + 1) * HD, own] = unit(part(0), hs_ref[h] * math.log2(math.e))
                stack_ref[i, p, n * HD : (n + 1) * HD] = unit(part(1), 1.0)
                value_ref[i, p, :HD, own] = part(2).astype(BF16)
            key_ref[i, p] = stack_ref[i, p].T

    def attend(i):
        for p in range(5):
            weights = jnp.exp2(dot(key_ref[i, p], query_ref[i, p])).astype(BF16)
            for n in range(2):
                own = slice(n * FR, (n + 1) * FR)
                weight_ref[i, p, own, own] = weights[:, own] * near_ref[...]

    def mix(i):
        for p, ((s, h), _) in enumerate(places()):
            total = dot(value_ref[i, p], weight_ref[i, p])
            part = (total[:HD] * (1.0 / total[HD : HD + 1])).astype(BF16)
            if p == 4:
                mixed_ref[i, h * HD :, :] = part
            else:
                cut = slice(s * FR, (s + 1) * FR)
                mixed_ref[i, h * HD : (h + 1) * HD, cut] = part[:, :FR]
                mixed_ref[i, (h + 1) * HD : (h + 2) * HD, cut] = part[:, FR:]

    def upper(i):
        normed_ref[i] = silu(block_ref[i] + dot(wot_ref[...], mixed_ref[i])).astype(BF16)

    def noise(i):
        noise_ref[i] = dot(wet_ref[...], normed_ref[i])[:8]

    each((conv_mid,), PX // 2)
    for bodies in ((project, units), (attend,), (mix,), (upper,), (noise,)):
        each(bodies, PX)


def advance(state, noise_ref, alpha, beta, entering):
    tiles = []
    for c in range(4):
        for r in range(2):
            rows = [noise_ref[r * 4 + w // 2, c : c + 1, (w % 2) * FR : (w % 2 + 1) * FR] for w in range(PX)]
            noise = jnp.concatenate(rows, axis=0)
            at = c * 16 + r * 8
            tiles.append(alpha * state[at : at + 8] + beta * noise)
    updated = jnp.concatenate(tiles, axis=0)
    return jnp.where(lanes((64, FR)) == FR - 1, entering, pltpu.roll(updated, FR - 1, 1))


def masked(slot, index, q, t):
    inside = (t > 0) if index == 0 else (t < NT - 1) if index == 2 else None
    own, left, right = slot[:64], slot[64:80], slot[80:96]
    left = jnp.where(q > 0, left, 0.0)
    right = jnp.where(q < NQ - 1, right, 0.0)
    slot = jnp.concatenate([own, left, right], axis=0)
    return slot if inside is None else jnp.where(inside, slot, 0.0)


def kernel(lat_ref, ent_ref, lev_ref, tw_hbm, cin_ref, cmid_hbm, gain_ref, qkv_hbm, hs_ref, wo_hbm, we_ref,
           out_ref,
           tw_ref, cmid_ref, qkv_ref, wo_ref, taps_ref,
           band_ref, mid_ref, qkvt_ref, wot_ref, wet_ref, gain_out, near_ref, ent_out,
           emb_ref, rhs_ref, hid_ref, act_ref, noise_ref,
           block_ref, normed_ref, project_ref, query_ref, stack_ref, key_ref, value_ref, weight_ref, mixed_ref,
           send1, recv1, halo, own_ref, left_ref, right_ref, send3, recv3,
           load_sem, send1_sem, recv1_sem, send2_sem, recv2_sem, send3_sem, recv3_sem):
    q, t = lax.axis_index("queue"), lax.axis_index("tile")
    loads = [pltpu.make_async_copy(src, dst, load_sem.at[i]) for i, (src, dst) in enumerate(
        [(cmid_hbm, cmid_ref), (qkv_hbm, qkv_ref), (wo_hbm, wo_ref), (tw_hbm, tw_ref)])]
    for load in loads:
        load.start()

    barrier = pltpu.get_barrier_semaphore()
    above, below = lax.rem(t + NT - 1, NT), lax.rem(t + 1, NT)

    def greet(k, carry):
        peer = lax.rem(q + k, NQ)
        pl.semaphore_signal(barrier, inc=1, device_id=(peer, above), device_id_type=MESH)
        pl.semaphore_signal(barrier, inc=1, device_id=(peer, below), device_id_type=MESH)
        return carry

    def greet_row(k, carry):
        pl.semaphore_signal(barrier, inc=1, device_id=(lax.rem(q + k, NQ), t), device_id_type=MESH)
        return carry

    lax.fori_loop(0, NQ, greet, 0)
    lax.fori_loop(1, NQ, greet_row, 0)
    pack_latents(lat_ref, lev_ref, send1)
    pl.semaphore_wait(barrier, 3 * NQ - 1)

    place = pl.ds(pl.multiple_of(q * 8, 8), 8)

    def to_peer(peer, row, slot):
        pltpu.make_async_remote_copy(
            src_ref=send1.at[peer], dst_ref=recv1.at[slot, place],
            send_sem=send1_sem.at[slot], recv_sem=recv1_sem.at[slot],
            device_id=(peer, row), device_id_type=MESH).start()

    def scatter_row(k, carry):
        to_peer(lax.rem(q + k, NQ), t, 1)
        return carry

    def scatter(k, carry):
        peer = lax.rem(q + k, NQ)
        to_peer(peer, above, 2)
        to_peer(peer, below, 0)
        return carry

    lax.fori_loop(1, NQ, scatter_row, 0)
    lax.fori_loop(0, NQ, scatter, 0)
    recv1[1, place] = send1[q]

    for load in loads:
        load.wait()
    prepare(cin_ref, cmid_ref, gain_ref, qkv_ref, wo_ref, we_ref, ent_ref, taps_ref,
            band_ref, mid_ref, qkvt_ref, wot_ref, wet_ref, gain_out, near_ref, ent_out, q)

    blank(query_ref, value_ref, weight_ref)

    for slot in range(3):
        count = FR if slot != 1 else FR - 8
        part = recv1.at[slot, pl.ds(0, count)]
        pltpu.make_async_copy(part, part, recv1_sem.at[slot]).wait()
    slots = [recv1[slot].T for slot in range(3)]
    level = slots[1][2 * ROW : 2 * ROW + 1]
    embed(level, tw_ref, emb_ref)
    alpha, beta = coefficients(level)
    state = slots[1][:64]
    slots = [masked(slot[: 2 * ROW], i, q, t) for i, slot in enumerate(slots)]

    conv_in(slots, band_ref, emb_ref, rhs_ref, hid_ref, act_ref, q, t)
    block_net(hs_ref, mid_ref, qkvt_ref, wot_ref, wet_ref, gain_out, near_ref, hid_ref, act_ref, noise_ref,
              block_ref, normed_ref, project_ref, query_ref, stack_ref, key_ref, value_ref, weight_ref, mixed_ref)
    state = advance(state, noise_ref, alpha, beta, ent_out[0])

    own_ref[...] = state
    for r in range(2):
        for c in range(4):
            at = c * 16 + r * 8
            left_ref[r * 8 + c * 2 : r * 8 + c * 2 + 2, :] = state[at + 6 : at + 8]
            right_ref[r * 8 + c * 2 : r * 8 + c * 2 + 2, :] = state[at : at + 2]
    before, after = lax.rem(q + NQ - 1, NQ), lax.rem(q + 1, NQ)
    copies = []
    for row, slot in ((t, 1), (above, 2), (below, 0)):
        if slot != 1:
            copies.append((own_ref, (0, 64), q, row, slot))
        copies.append((left_ref, (64, 16), after, row, slot))
        copies.append((right_ref, (80, 16), before, row, slot))
    copies = [
        pltpu.make_async_remote_copy(
            src_ref=src, dst_ref=halo.at[slot, pl.ds(start, size)],
            send_sem=send2_sem.at[i], recv_sem=recv2_sem.at[i],
            device_id=(peer, row), device_id_type=MESH)
        for i, (src, (start, size), peer, row, slot) in enumerate(copies)]
    for copy in copies:
        copy.start()
    for copy in copies:
        copy.wait_recv()
    halo[1, :64] = own_ref[...]
    slots = [masked(halo[i], i, q, t) for i in range(3)]

    conv_in(slots, band_ref, emb_ref, rhs_ref, hid_ref, act_ref, q, t)
    block_net(hs_ref, mid_ref, qkvt_ref, wot_ref, wet_ref, gain_out, near_ref, hid_ref, act_ref, noise_ref,
              block_ref, normed_ref, project_ref, query_ref, stack_ref, key_ref, value_ref, weight_ref, mixed_ref)
    state = advance(own_ref[...], noise_ref, alpha, beta, ent_out[1])

    frames = jnp.concatenate([state, jnp.zeros((64, FR), F32)], axis=0).T
    for peer in range(NQ):
        send3[peer] = frames[peer * 8 : peer * 8 + 8]

    def give(k, carry):
        peer = lax.rem(q + k, NQ)
        pltpu.make_async_remote_copy(
            src_ref=send3.at[peer], dst_ref=recv3.at[q],
            send_sem=send3_sem.at[0], recv_sem=recv3_sem.at[0],
            device_id=(peer, t), device_id_type=MESH).start()
        return carry

    lax.fori_loop(1, NQ, give, 0)
    recv3[q] = send3[q]
    for copy in copies:
        copy.wait_send()
    for slot in range(3):
        part = send1.at[pl.ds(0, NQ if slot != 1 else NQ - 1)]
        pltpu.make_async_copy(part, part, send1_sem.at[slot]).wait()
    part = recv3.at[pl.ds(0, NQ - 1)]
    pltpu.make_async_copy(part, part, recv3_sem.at[0]).wait()
    part = send3.at[pl.ds(0, NQ - 1)]
    pltpu.make_async_copy(part, part, send3_sem.at[0]).wait()

    lane = lanes((8, FR))
    for c in range(4):
        for r in range(2):
            at = c * 16 + r * 8
            total = jnp.zeros((8, FR), F32)
            for source in range(NQ):
                moved = pltpu.roll(recv3[source], (FR + 8 * source - at) % FR, 1)
                total = jnp.where((lane >> 3) == source, moved, total)
            out_ref[:, c, r, :] = total


def per_device(queue_latents, entering, levels, time_weight, conv_in_weight, conv_mid_weight, norm_gain,
               qkv_weight, head_scale, attn_out_weight, eps_out_weight):
    vmem = pl.BlockSpec(memory_space=pltpu.VMEM)
    smem = pl.BlockSpec(memory_space=pltpu.SMEM)
    hbm = pl.BlockSpec(memory_space=pl.ANY)
    v = pltpu.VMEM
    dma = pltpu.SemaphoreType.DMA
    return pl.pallas_call(
        kernel,
        out_shape=jax.ShapeDtypeStruct(queue_latents.shape, F32),
        in_specs=[vmem, vmem, smem, hbm, vmem, hbm, vmem, hbm, smem, hbm, vmem],
        out_specs=vmem,
        scratch_shapes=[
            v((CH, CH), F32), v((3, 3, CH, CH), BF16), v((CH, 3 * CH), BF16), v((CH, CH), BF16), v((40, CH), F32),
            v((PX + 2, CH, TAPS), BF16), v((4, CH, 3 * CH), BF16), v((3 * CH, CH), BF16), v((CH, CH), BF16),
            v((16, CH), BF16), v((CH, FR), F32), v((FR, FR), BF16), v((STEPS, 64, FR), F32),
            v((CH, FR), F32), v((2, TAPS, 2 * FR), BF16), v((PX + 2, 2, CH, FR), F32),
            v((PX + 2, 4, CH, FR), BF16), v((PX, 8, 2 * FR), F32),
            v((PX, CH, 2 * FR), F32), v((PX, CH, 2 * FR), BF16), v((PX, 3 * CH, 2 * FR), F32),
            v((PX, 5, FR, 2 * FR), BF16), v((PX, 5, FR, FR), BF16), v((PX, 5, FR, FR), BF16),
            v((PX, 5, HD + 16, 2 * FR), BF16), v((PX, 5, 2 * FR, 2 * FR), BF16), v((PX, CH, 2 * FR), BF16),
            v((NQ, 8, FR), F32), v((3, FR, FR), F32), v((3, 2 * ROW, FR), F32), v((64, FR), F32),
            v((16, FR), F32), v((16, FR), F32), v((NQ, 8, FR), F32), v((NQ, 8, FR), F32),
            dma((4,)), dma((3,)), dma((3,)), dma((8,)), dma((8,)), dma((1,)), dma((1,)),
        ],
        compiler_params=pltpu.CompilerParams(
            collective_id=0, has_side_effects=True, vmem_limit_bytes=56 * 1024 * 1024),
    )(queue_latents, entering, levels, time_weight, conv_in_weight, conv_mid_weight,
      norm_gain, qkv_weight, head_scale, attn_out_weight, eps_out_weight.T)


def solution(mesh):
    placed = (
        P("queue", None, "tile", None),
        P(None, None, "tile", None),
        P("queue"),
        P(),
        P(),
        P(),
        P(),
        P(),
        P(),
        P(),
        P(),
    )
    return jax.shard_map(
        per_device,
        mesh=mesh,
        in_specs=placed,
        out_specs=P("queue", None, "tile", None),
        check_vma=False,
    )
```

```python
import math

import jax
import jax.numpy as jnp
from jax import lax
from jax.experimental import pallas as pl
from jax.experimental.pallas import tpu as pltpu
from jax.sharding import PartitionSpec as P

WIN = 8
STEPS = 2
F32 = jnp.float32
BF16 = jnp.bfloat16
MESH = pl.DeviceIdType.MESH

CH = 320
HEADS = 5
HD = 64
FR = 128
NQ = 16
NT = 8
PX = 8
ROW = 48
TAPS = 3 * ROW


def dot(a, b):
    return jnp.dot(a, b, preferred_element_type=F32)


def dot_t(a, b):
    return lax.dot_general(a, b, (((0,), (0,)), ((), ())), preferred_element_type=F32)


def sin_cos(angle):
    count = jnp.floor(angle * (2.0 / math.pi) + 0.5)
    rest = ((angle - count * 1.5703125) - count * 4.837512969970703125e-4) - count * 7.54978995489188216e-8
    square = rest * rest
    sine = rest + rest * square * (
        -1.6666654611e-1 + square * (8.3321608736e-3 - square * 1.9515295891e-4)
    )
    cosine = 1.0 - 0.5 * square + square * square * (
        4.166664568298827e-2 + square * (-1.388731625493765e-3 + square * 2.443315711809948e-5)
    )
    quarter = count - 4.0 * jnp.floor(count * 0.25)
    odd = (quarter == 1.0) | (quarter == 3.0)
    sin_out = jnp.where(odd, cosine, sine)
    cos_out = jnp.where(odd, sine, cosine)
    sin_out = jnp.where(quarter >= 2.0, -sin_out, sin_out)
    cos_out = jnp.where((quarter == 1.0) | (quarter == 2.0), -cos_out, cos_out)
    return sin_out, cos_out


def silu(x):
    half = 0.5 * x
    return half + half * jnp.tanh(half)


def lanes(shape):
    return lax.broadcasted_iota(jnp.int32, shape, 1)


OFFSETS = sorted(((z, x, c) for z in (0, 1) for x in range(4) for c in (0, 1)),
                 key=lambda o: -(2 * o[0] + min(o[1], 4 - o[1]) + 0.1 * o[2]))


def peer_at(q, offset):
    z, x, c = offset
    return ((q // 8 + z) % 2) * 8 + ((q // 2 + x) % 4) * 2 + (q + c) % 2


def group_of(q):
    return jnp.where(q < NQ // 2, q, 3 * NQ // 2 - 1 - q)


def pack_latents(lat_ref, lev_ref, send_ref):
    lane = lanes((8, FR))
    row = lax.broadcasted_iota(jnp.int32, (8, FR), 0)
    pieces = []
    for c in range(4):
        for r in range(2):
            plane = lat_ref[:, c, r, :]
            own, left, right = c * 16 + r * 8, 64 + r * 8 + c * 2, 80 + r * 8 + c * 2
            pieces.append((3, own, pltpu.roll(plane, own, 1)))
            pieces.append((1, left, pltpu.roll(plane, left + 2, 1)))
            pieces.append((1, right, pltpu.roll(plane, right - 8, 1)))
    level = jnp.zeros((8, FR), F32)
    for f in range(8):
        level = jnp.where(row == f, lev_ref[f].astype(F32), level)

    def body(dest, carry):
        place = (lane - 8 * dest) & (FR - 1)
        total = jnp.zeros((8, FR), F32)
        for bits, base, plane in pieces:
            total = jnp.where((place >> bits) == (base >> bits), plane, total)
        total = pltpu.roll(total, lax.rem(FR - 8 * dest, FR), 1)
        send_ref[dest] = jnp.where(lane == 2 * ROW, level, total)
        return carry

    lax.fori_loop(0, NQ, body, 0)


def prepare(cin_ref, cmid_ref, gain_ref, qkv_ref, wo_ref, we_ref, ent_ref, tw_ref, taps_ref,
            twt_ref, band_ref, mid_ref, qkvt_ref, wot_ref, wet_ref, gain_out, near_ref, ent_out, g):
    taps_ref[...] = jnp.zeros(taps_ref.shape, F32)
    for i in range(9):
        taps_ref[4 * i : 4 * i + 4, :] = cin_ref[i // 3, i % 3].astype(F32)
    taps_t = taps_ref[...].T.astype(BF16)
    k = lanes((40, TAPS))
    m = lax.broadcasted_iota(jnp.int32, (40, TAPS), 0)
    dy = (k >= ROW).astype(jnp.int32) + (k >= 2 * ROW).astype(jnp.int32)
    rest = k - ROW * dy
    own = rest < 32
    left = rest < 40
    c = jnp.where(own, rest >> 3, (rest & 7) >> 1)
    rel = jnp.where(own, (rest & 7) + 2, jnp.where(left, rest & 1, (rest & 1) + 10))
    for w in range(PX + 2):
        dx = rel - w
        pick = (dx >= 0) & (dx <= 2) & (m == dy * 12 + dx * 4 + c)
        band_ref[w] = dot(taps_t, jnp.where(pick, 1.0, 0.0).astype(BF16)).astype(BF16)
    taps = [jnp.concatenate([cmid_ref[dy, dx].astype(F32) for dx in range(3)], axis=0) for dy in range(3)]
    outer = 0.5 * (taps[0] + taps[2])
    for v, mid in enumerate((taps[0], outer + 0.5 * taps[1], outer - 0.5 * taps[1], taps[2])):
        mid_ref[v] = mid.astype(BF16).T
    weight = tw_ref[...].T
    high = weight.astype(BF16)
    low = (weight - high.astype(F32)).astype(BF16)
    twt_ref[...] = jnp.concatenate([high, high, low], axis=1)
    qkvt_ref[...] = qkv_ref[...].T
    wot_ref[...] = wo_ref[...].T
    wet_ref[...] = jnp.concatenate([we_ref[...].astype(F32), jnp.zeros((12, CH), F32)], axis=0).astype(BF16)
    gain_out[...] = jnp.broadcast_to(gain_ref[...].reshape(1, CH), (FR, CH)).T
    key_slot = lax.broadcasted_iota(jnp.int32, (FR, FR), 0)
    query_slot = lanes((FR, FR))
    near_ref[...] = jnp.where(jnp.abs(key_slot - query_slot) <= WIN, 1.0, 0.0).astype(BF16)
    lane = lanes((8, FR))
    for s in range(STEPS):
        rows = jnp.concatenate([ent_ref[s, c, r : r + 1, :] for c in range(4) for r in range(2)], axis=0)
        rows = pltpu.roll(rows, lax.rem(FR - 8 * g, FR), 1)
        columns = jnp.concatenate([rows, jnp.zeros((FR - 8, FR), F32)], axis=0).T[:8]
        for i in range(8):
            shifted = pltpu.roll(columns, FR - 1 - i, 1)
            ent_out[s, 8 * i : 8 * i + 8, :] = jnp.where(lane == FR - 1, shifted, 0.0)


def blank(query_ref, value_ref, weight_ref):
    def body(i, carry):
        for p in range(5):
            query_ref[i, p, :HD, FR:] = jnp.zeros((HD, FR), BF16)
            query_ref[i, p, HD:, :FR] = jnp.zeros((HD, FR), BF16)
            value_ref[i, p, HD:] = jnp.ones((16, 2 * FR), BF16)
            weight_ref[i, p, :FR, FR:] = jnp.zeros((FR, FR), BF16)
            weight_ref[i, p, FR:, :FR] = jnp.zeros((FR, FR), BF16)
        return carry

    lax.fori_loop(0, PX, body, 0)


def embed(level, twt_ref, emb_ref):
    index = lax.broadcasted_iota(jnp.int32, (CH // 2, FR), 0).astype(F32)
    freqs = jnp.exp(-math.log(10000.0) * index / (CH // 2))
    sine, cosine = sin_cos(level * freqs)
    feature = jnp.concatenate([sine, cosine], axis=0)
    high = feature.astype(BF16)
    low = (feature - high.astype(F32)).astype(BF16)
    emb_ref[...] = dot(twt_ref[...], jnp.concatenate([high, low, high], axis=0))


def coefficients(level):
    lane = lanes((8, FR))
    level = jnp.broadcast_to(level, (8, FR))
    target = jnp.where(lane == 0, 0.0, pltpu.roll(level, 1, 1))
    angle = lambda l: (l / 1000.0 + 0.008) / 1.008 * (math.pi / 2.0)
    s0, c0 = sin_cos(angle(level))
    s1, c1 = sin_cos(angle(target))
    alpha = c1 / c0
    return alpha, s1 - alpha * s0


def conv_in(slots, band_ref, emb_ref, rhs_ref, hid_ref, act_ref, g, t):
    rows = []
    for slot in slots:
        for r in range(2):
            rows.append(jnp.concatenate(
                [slot[k * 16 + r * 8 : k * 16 + r * 8 + 8] for k in range(6)], axis=0).astype(BF16))
    for p in range(2):
        for half in range(2):
            rhs_ref[p, :, half * FR : (half + 1) * FR] = jnp.concatenate(
                rows[2 * p + half : 2 * p + half + 3], axis=0)

    def body(w, carry):
        inside = ((w > 0) | (g > 0)) & ((w < PX + 1) | (g < NQ - 1))
        active = []
        for p in range(2):
            both = dot(band_ref[w], rhs_ref[p])
            for half in range(2):
                hidden = both[:, half * FR : (half + 1) * FR] + emb_ref[...]
                if p != half:
                    hid_ref[w, p] = hidden
                    active.append(jnp.where(inside, silu(hidden), 0.0))
                else:
                    active.append(jnp.where(inside & ((t > 0) if p == 0 else (t < NT - 1)), silu(hidden), 0.0))
        a0, a1, a2, a3 = active
        for v, part in enumerate((a0 - a2, a1 + a2, a2 - a1, a1 - a3)):
            act_ref[w, v] = part.astype(BF16)
        return carry

    lax.fori_loop(0, PX + 2, body, 0, unroll=PX + 2)


def unit(x, scale):
    return (x * (lax.rsqrt(jnp.sum(x * x, axis=0, keepdims=True) + 1e-06) * scale)).astype(BF16)


def each(bodies, count):
    def step(i, carry):
        for body in bodies:
            body(i)
        return carry

    lax.fori_loop(0, count, step, 0, unroll=count)


def places():
    pairs = [((s, 2 * p), (s, 2 * p + 1)) for s in range(2) for p in range(2)]
    return pairs + [((0, 4), (1, 4))]


def block_net(hs_ref, mid_ref, qkvt_ref, wot_ref, wet_ref, gain_ref, near_ref, hid_ref, act_ref, noise_ref,
              block_ref, normed_ref, project_ref, query_ref, stack_ref, key_ref, value_ref, weight_ref, mixed_ref):
    def norm(i, block):
        block_ref[i] = block
        center = jnp.mean(block, axis=0, keepdims=True)
        moved = block - center
        spread = jnp.mean(moved * moved, axis=0, keepdims=True)
        gain = jnp.concatenate([gain_ref[...]] * 2, axis=1)
        normed_ref[i] = (moved * lax.rsqrt(spread + 1e-05) * gain).astype(BF16)

    def conv_mid(j):
        parts = []
        for v in range(4):
            rhs = [jnp.concatenate([act_ref[2 * j + dx, v], act_ref[2 * j + dx + 1, v]], axis=1) for dx in range(3)]
            parts.append(dot(mid_ref[v], jnp.concatenate(rhs, axis=0)))
        for r, part in enumerate((parts[0] + (parts[1] + parts[2]), (parts[1] - parts[2]) - parts[3])):
            hidden = jnp.concatenate([hid_ref[2 * j + 1, r], hid_ref[2 * j + 2, r]], axis=1)
            norm(4 * r + j, hidden + part)

    def project(i):
        project_ref[i] = dot(qkvt_ref[...], normed_ref[i])

    def units(i):
        for p, pair in enumerate(places()):
            for n, (s, h) in enumerate(pair):
                cut, own = slice(s * FR, (s + 1) * FR), slice(n * FR, (n + 1) * FR)
                part = lambda k: project_ref[i, k * CH + h * HD : k * CH + (h + 1) * HD, cut]
                query_ref[i, p, n * HD : (n + 1) * HD, own] = unit(part(0), hs_ref[h] * math.log2(math.e))
                stack_ref[i, p, n * HD : (n + 1) * HD] = unit(part(1), 1.0)
                value_ref[i, p, :HD, own] = part(2).astype(BF16)
            key_ref[i, p] = stack_ref[i, p].T

    def attend(i):
        for p in range(5):
            weights = jnp.exp2(dot(key_ref[i, p], query_ref[i, p])).astype(BF16)
            for n in range(2):
                own = slice(n * FR, (n + 1) * FR)
                weight_ref[i, p, own, own] = weights[:, own] * near_ref[...]

    def mix(i):
        for p, ((s, h), _) in enumerate(places()):
            total = dot(value_ref[i, p], weight_ref[i, p])
            part = (total[:HD] * (1.0 / total[HD : HD + 1])).astype(BF16)
            if p == 4:
                mixed_ref[i, h * HD :, :] = part
            else:
                cut = slice(s * FR, (s + 1) * FR)
                mixed_ref[i, h * HD : (h + 1) * HD, cut] = part[:, :FR]
                mixed_ref[i, (h + 1) * HD : (h + 2) * HD, cut] = part[:, FR:]

    def upper(i):
        normed_ref[i] = silu(block_ref[i] + dot(wot_ref[...], mixed_ref[i])).astype(BF16)

    def noise(i):
        noise_ref[i] = dot(wet_ref[...], normed_ref[i])[:8]

    each((conv_mid,), PX // 2)
    for bodies in ((project, units), (attend,), (mix,), (upper,), (noise,)):
        each(bodies, PX)


def advance(state, noise_ref, alpha, beta, entering):
    tiles = []
    for c in range(4):
        for r in range(2):
            rows = [noise_ref[r * 4 + w // 2, c : c + 1, (w % 2) * FR : (w % 2 + 1) * FR] for w in range(PX)]
            noise = jnp.concatenate(rows, axis=0)
            at = c * 16 + r * 8
            tiles.append(alpha * state[at : at + 8] + beta * noise)
    updated = jnp.concatenate(tiles, axis=0)
    return jnp.where(lanes((64, FR)) == FR - 1, entering, pltpu.roll(updated, FR - 1, 1))


def masked(slot, index, g, t):
    inside = (t > 0) if index == 0 else (t < NT - 1) if index == 2 else None
    own, left, right = slot[:64], slot[64:80], slot[80:96]
    left = jnp.where(g > 0, left, 0.0)
    right = jnp.where(g < NQ - 1, right, 0.0)
    slot = jnp.concatenate([own, left, right], axis=0)
    return slot if inside is None else jnp.where(inside, slot, 0.0)


def kernel(lat_hbm, ent_hbm, lev_hbm, tw_hbm, cin_hbm, cmid_hbm, gain_hbm, qkv_hbm, hs_hbm, wo_hbm, we_hbm,
           out_ref,
           lat_ref, ent_ref, lev_ref, tw_ref, cin_ref, cmid_ref, gain_ref, qkv_ref, hs_ref, wo_ref, we_ref, taps_ref,
           twt_ref, band_ref, mid_ref, qkvt_ref, wot_ref, wet_ref, gain_out, near_ref, ent_out,
           emb_ref, rhs_ref, hid_ref, act_ref, noise_ref,
           block_ref, normed_ref, project_ref, query_ref, stack_ref, key_ref, value_ref, weight_ref, mixed_ref,
           send1, recv1, halo, state_ref, own_ref, left_ref, right_ref, send3, recv3,
           load_sem, send1_sem, recv1_sem, send2_sem, recv2_sem, send3_sem, recv3_sem):
    q, t = lax.axis_index("queue"), lax.axis_index("tile")
    g = group_of(q)
    sides = [(t > 0, t - 1, 2), (t < NT - 1, t + 1, 0)]
    others = OFFSETS[:-1]

    barrier = pltpu.get_barrier_semaphore()
    for there, row, _ in sides:
        @pl.when(there)
        def _():
            for offset in OFFSETS:
                pl.semaphore_signal(barrier, inc=1, device_id=(peer_at(q, offset), row), device_id_type=MESH)
    for offset in others:
        pl.semaphore_signal(barrier, inc=1, device_id=(peer_at(q, offset), t), device_id_type=MESH)

    loads = [pltpu.make_async_copy(src, dst, load_sem.at[i]) for i, (src, dst) in enumerate(
        [(lat_hbm, lat_ref), (lev_hbm, lev_ref), (cmid_hbm, cmid_ref), (qkv_hbm, qkv_ref), (wo_hbm, wo_ref),
         (tw_hbm, tw_ref), (ent_hbm, ent_ref), (cin_hbm, cin_ref), (gain_hbm, gain_ref), (hs_hbm, hs_ref),
         (we_hbm, we_ref)])]
    for load in loads:
        load.start()
    for load in loads[:2]:
        load.wait()
    pack_latents(lat_ref, lev_ref, send1)
    both = (t > 0).astype(jnp.int32) + (t < NT - 1).astype(jnp.int32)
    pl.semaphore_wait(barrier, NQ - 1 + NQ * both)

    place = pl.ds(pl.multiple_of(q * 8, 8), 8)

    def to_peer(offset, row, slot):
        peer = peer_at(q, offset)
        pltpu.make_async_remote_copy(
            src_ref=send1.at[group_of(peer)], dst_ref=recv1.at[slot, place],
            send_sem=send1_sem.at[slot], recv_sem=recv1_sem.at[slot],
            device_id=(peer, row), device_id_type=MESH).start()

    for there, row, slot in sides:
        @pl.when(there)
        def _():
            for offset in OFFSETS:
                to_peer(offset, row, slot)
    for offset in others:
        to_peer(offset, t, 1)
    recv1[1, place] = send1[g]

    for load in loads[2:]:
        load.wait()
    prepare(cin_ref, cmid_ref, gain_ref, qkv_ref, wo_ref, we_ref, ent_ref, tw_ref, taps_ref,
            twt_ref, band_ref, mid_ref, qkvt_ref, wot_ref, wet_ref, gain_out, near_ref, ent_out, g)
    blank(query_ref, value_ref, weight_ref)

    def settle(ref, sem, count):
        part = ref.at[pl.ds(0, count)]
        pltpu.make_async_copy(part, part, sem).wait()

    settle(recv1.at[1], recv1_sem.at[1], FR - 8)
    for there, slot in ((t > 0, 0), (t < NT - 1, 2)):
        @pl.when(there)
        def _():
            settle(recv1.at[slot], recv1_sem.at[slot], FR)
    slots = [recv1[slot].T for slot in range(3)]
    level = slots[1][2 * ROW : 2 * ROW + 1]
    embed(level, twt_ref, emb_ref)
    alpha, beta = coefficients(level)
    state = slots[1][:64]
    slots = [masked(slot[: 2 * ROW], i, g, t) for i, slot in enumerate(slots)]

    conv_in(slots, band_ref, emb_ref, rhs_ref, hid_ref, act_ref, g, t)
    block_net(hs_ref, mid_ref, qkvt_ref, wot_ref, wet_ref, gain_out, near_ref, hid_ref, act_ref, noise_ref,
              block_ref, normed_ref, project_ref, query_ref, stack_ref, key_ref, value_ref, weight_ref, mixed_ref)
    state = advance(state, noise_ref, alpha, beta, ent_out[0])

    state_ref[...] = state
    own_ref[...] = state.astype(BF16)
    lefts, rights = [], []
    for r in range(2):
        for c in range(4):
            at = c * 16 + r * 8
            lefts.append(state[at + 6 : at + 8])
            rights.append(state[at : at + 2])
    left_ref[...] = jnp.concatenate(lefts, axis=0).astype(BF16)
    right_ref[...] = jnp.concatenate(rights, axis=0).astype(BF16)
    copies = []
    for src, start, size, step in ((left_ref, 64, 16, 1), (right_ref, 80, 16, -1), (own_ref, 0, 64, 0)):
        sent, got = (g < NQ - 1, g > 0) if step == 1 else (g > 0, g < NQ - 1) if step == -1 else (None, None)
        peer = group_of(jnp.clip(g + step, 0, NQ - 1))
        for down in (-1, 1, 0):
            if step == 0 and down == 0:
                continue
            sent_too, got_too = (t > 0, t < NT - 1) if down == -1 else (t < NT - 1, t > 0) if down == 1 else (None, None)
            both_of = lambda a, b: b if a is None else a if b is None else a & b
            i = len(copies)
            copies.append((both_of(sent, sent_too), both_of(got, got_too), pltpu.make_async_remote_copy(
                src_ref=src, dst_ref=halo.at[1 - down, pl.ds(start, size)],
                send_sem=send2_sem.at[i], recv_sem=recv2_sem.at[i],
                device_id=(peer, t + down), device_id_type=MESH)))
    for sent, _, copy in copies:
        pl.when(sent)(copy.start)
    for _, got, copy in copies:
        pl.when(got)(copy.wait_recv)
    halo[1, :64] = own_ref[...]
    slots = [masked(halo[i].astype(F32), i, g, t) for i in range(3)]

    conv_in(slots, band_ref, emb_ref, rhs_ref, hid_ref, act_ref, g, t)
    block_net(hs_ref, mid_ref, qkvt_ref, wot_ref, wet_ref, gain_out, near_ref, hid_ref, act_ref, noise_ref,
              block_ref, normed_ref, project_ref, query_ref, stack_ref, key_ref, value_ref, weight_ref, mixed_ref)
    state = advance(state_ref[...], noise_ref, alpha, beta, ent_out[1])

    frames = jnp.concatenate([state, jnp.zeros((64, FR), F32)], axis=0).T
    for peer in range(NQ):
        send3[peer] = frames[peer * 8 : peer * 8 + 8]
    for offset in others:
        peer = peer_at(q, offset)
        pltpu.make_async_remote_copy(
            src_ref=send3.at[peer], dst_ref=recv3.at[g],
            send_sem=send3_sem.at[0], recv_sem=recv3_sem.at[0],
            device_id=(peer, t), device_id_type=MESH).start()
    recv3[g] = send3[q]
    for sent, _, copy in copies:
        pl.when(sent)(copy.wait_send)
    settle(send1, send1_sem.at[1], NQ - 1)
    for there, _, slot in sides:
        @pl.when(there)
        def _():
            settle(send1, send1_sem.at[slot], NQ)
    settle(recv3, recv3_sem.at[0], NQ - 1)
    settle(send3, send3_sem.at[0], NQ - 1)

    group = lanes((8, FR)) >> 3
    turned = [pltpu.roll(recv3[source], 8 * source, 1) for source in range(NQ)]
    for c in range(4):
        for r in range(2):
            at = c * 2 + r
            total = turned[0]
            for source in range(1, NQ):
                total = jnp.where(group == (source + at) % NQ, turned[source], total)
            out_ref[:, c, r, :] = pltpu.roll(total, (FR - 8 * at) % FR, 1)


def per_device(queue_latents, entering, levels, time_weight, conv_in_weight, conv_mid_weight, norm_gain,
               qkv_weight, head_scale, attn_out_weight, eps_out_weight):
    hbm = pl.BlockSpec(memory_space=pl.ANY)
    v = pltpu.VMEM
    dma = pltpu.SemaphoreType.DMA
    inputs = (queue_latents, entering, levels, time_weight, conv_in_weight, conv_mid_weight,
              norm_gain, qkv_weight, head_scale, attn_out_weight, eps_out_weight.T)
    scalars = (levels, head_scale)
    return pl.pallas_call(
        kernel,
        out_shape=jax.ShapeDtypeStruct(queue_latents.shape, F32),
        in_specs=[hbm] * len(inputs),
        out_specs=pl.BlockSpec(memory_space=pltpu.VMEM),
        scratch_shapes=[
            *[(pltpu.SMEM if any(x is y for y in scalars) else v)(x.shape, x.dtype) for x in inputs],
            v((40, CH), F32),
            v((CH, 3 * CH), BF16),
            v((PX + 2, CH, TAPS), BF16), v((4, CH, 3 * CH), BF16), v((3 * CH, CH), BF16), v((CH, CH), BF16),
            v((16, CH), BF16), v((CH, FR), F32), v((FR, FR), BF16), v((STEPS, 64, FR), F32),
            v((CH, FR), F32), v((2, TAPS, 2 * FR), BF16), v((PX + 2, 2, CH, FR), F32),
            v((PX + 2, 4, CH, FR), BF16), v((PX, 8, 2 * FR), F32),
            v((PX, CH, 2 * FR), F32), v((PX, CH, 2 * FR), BF16), v((PX, 3 * CH, 2 * FR), F32),
            v((PX, 5, FR, 2 * FR), BF16), v((PX, 5, FR, FR), BF16), v((PX, 5, FR, FR), BF16),
            v((PX, 5, HD + 16, 2 * FR), BF16), v((PX, 5, 2 * FR, 2 * FR), BF16), v((PX, CH, 2 * FR), BF16),
            v((NQ, 8, FR), F32), v((3, FR, FR), F32), v((3, 2 * ROW, FR), BF16), v((64, FR), F32), v((64, FR), BF16),
            v((16, FR), BF16), v((16, FR), BF16), v((NQ, 8, FR), F32), v((NQ, 8, FR), F32),
            dma((len(inputs),)), dma((3,)), dma((3,)), dma((8,)), dma((8,)), dma((1,)), dma((1,)),
        ],
        compiler_params=pltpu.CompilerParams(
            collective_id=0, has_side_effects=True, vmem_limit_bytes=56 * 1024 * 1024),
    )(*inputs)


def solution(mesh):
    placed = (
        P("queue", None, "tile", None),
        P(None, None, "tile", None),
        P("queue"),
        P(),
        P(),
        P(),
        P(),
        P(),
        P(),
        P(),
        P(),
    )
    return jax.shard_map(
        per_device,
        mesh=mesh,
        in_specs=placed,
        out_specs=P("queue", None, "tile", None),
        check_vma=False,
    )
```

```python
import math

import jax
import jax.numpy as jnp
from jax import lax
from jax.experimental import pallas as pl
from jax.experimental.pallas import tpu as pltpu
from jax.sharding import PartitionSpec as P

WIN = 8
STEPS = 2
F32 = jnp.float32
BF16 = jnp.bfloat16
MESH = pl.DeviceIdType.MESH

CH = 320
HEADS = 5
HD = 64
FR = 128
NQ = 16
NT = 8
PX = 8
ROW = 48
TAPS = 3 * ROW


def dot(a, b):
    return jnp.dot(a, b, preferred_element_type=F32)


def dot_t(a, b):
    return lax.dot_general(a, b, (((0,), (0,)), ((), ())), preferred_element_type=F32)


def sin_cos(angle):
    count = jnp.floor(angle * (2.0 / math.pi) + 0.5)
    rest = ((angle - count * 1.5703125) - count * 4.837512969970703125e-4) - count * 7.54978995489188216e-8
    square = rest * rest
    sine = rest + rest * square * (
        -1.6666654611e-1 + square * (8.3321608736e-3 - square * 1.9515295891e-4)
    )
    cosine = 1.0 - 0.5 * square + square * square * (
        4.166664568298827e-2 + square * (-1.388731625493765e-3 + square * 2.443315711809948e-5)
    )
    quarter = count - 4.0 * jnp.floor(count * 0.25)
    odd = (quarter == 1.0) | (quarter == 3.0)
    sin_out = jnp.where(odd, cosine, sine)
    cos_out = jnp.where(odd, sine, cosine)
    sin_out = jnp.where(quarter >= 2.0, -sin_out, sin_out)
    cos_out = jnp.where((quarter == 1.0) | (quarter == 2.0), -cos_out, cos_out)
    return sin_out, cos_out


def silu(x):
    half = 0.5 * x
    return half + half * jnp.tanh(half)


def lanes(shape):
    return lax.broadcasted_iota(jnp.int32, shape, 1)


OFFSETS = sorted(((z, x, c) for z in (0, 1) for x in range(4) for c in (0, 1)),
                 key=lambda o: -(2 * o[0] + min(o[1], 4 - o[1]) + 0.1 * o[2]))


def peer_at(q, offset):
    z, x, c = offset
    return ((q ^ (8 * z)) & 8) | ((q + 2 * x) & 6) | ((q ^ c) & 1)


def group_of(q):
    return jnp.where(q < NQ // 2, q, 3 * NQ // 2 - 1 - q)


def pack_latents(lat_ref, lev_ref, send_ref):
    lane = lanes((8, FR))
    row = lax.broadcasted_iota(jnp.int32, (8, FR), 0)
    pieces = []
    for c in range(4):
        for r in range(2):
            plane = lat_ref[:, c, r, :]
            own, left, right = c * 16 + r * 8, 64 + r * 8 + c * 2, 80 + r * 8 + c * 2
            pieces.append((3, own, pltpu.roll(plane, own, 1)))
            pieces.append((1, left, pltpu.roll(plane, left + 2, 1)))
            pieces.append((1, right, pltpu.roll(plane, right - 8, 1)))
    level = jnp.zeros((8, FR), F32)
    for f in range(8):
        level = jnp.where(row == f, lev_ref[f].astype(F32), level)

    def body(dest, carry):
        place = (lane - 8 * dest) & (FR - 1)
        total = jnp.zeros((8, FR), F32)
        for bits, base, plane in pieces:
            total = jnp.where((place >> bits) == (base >> bits), plane, total)
        total = pltpu.roll(total, lax.rem(FR - 8 * dest, FR), 1)
        send_ref[dest] = jnp.where(lane == 2 * ROW, level, total)
        return carry

    lax.fori_loop(0, NQ, body, 0)


def prepare(cin_ref, cmid_ref, gain_ref, qkv_ref, wo_ref, we_ref, ent_ref, tw_ref, taps_ref,
            twt_ref, band_ref, mid_ref, qkvt_ref, wot_ref, wet_ref, gain_out, near_ref, ent_out, g):
    taps_ref[...] = jnp.zeros(taps_ref.shape, F32)
    for i in range(9):
        taps_ref[4 * i : 4 * i + 4, :] = cin_ref[i // 3, i % 3].astype(F32)
    taps_t = taps_ref[...].T.astype(BF16)
    k = lanes((40, TAPS))
    m = lax.broadcasted_iota(jnp.int32, (40, TAPS), 0)
    dy = (k >= ROW).astype(jnp.int32) + (k >= 2 * ROW).astype(jnp.int32)
    rest = k - ROW * dy
    own = rest < 32
    left = rest < 40
    c = jnp.where(own, rest >> 3, (rest & 7) >> 1)
    rel = jnp.where(own, (rest & 7) + 2, jnp.where(left, rest & 1, (rest & 1) + 10))
    for w in range(PX + 2):
        dx = rel - w
        pick = (dx >= 0) & (dx <= 2) & (m == dy * 12 + dx * 4 + c)
        band_ref[w] = dot(taps_t, jnp.where(pick, 1.0, 0.0).astype(BF16)).astype(BF16)
    taps = [jnp.concatenate([cmid_ref[dy, dx].astype(F32) for dx in range(3)], axis=0) for dy in range(3)]
    outer = 0.5 * (taps[0] + taps[2])
    for v, mid in enumerate((taps[0], outer + 0.5 * taps[1], outer - 0.5 * taps[1], taps[2])):
        mid_ref[v] = mid.astype(BF16).T
    weight = tw_ref[...].T
    high = weight.astype(BF16)
    low = (weight - high.astype(F32)).astype(BF16)
    twt_ref[...] = jnp.concatenate([high, high, low], axis=1)
    qkvt_ref[...] = qkv_ref[...].T
    wot_ref[...] = wo_ref[...].T
    wet_ref[...] = jnp.concatenate([we_ref[...].astype(F32), jnp.zeros((12, CH), F32)], axis=0).astype(BF16)
    gain_out[...] = jnp.broadcast_to(gain_ref[...].reshape(1, CH), (FR, CH)).T
    key_slot = lax.broadcasted_iota(jnp.int32, (FR, FR), 0)
    query_slot = lanes((FR, FR))
    near_ref[...] = jnp.where(jnp.abs(key_slot - query_slot) <= WIN, 1.0, 0.0).astype(BF16)
    lane = lanes((8, FR))
    for s in range(STEPS):
        rows = jnp.concatenate([ent_ref[s, c, r : r + 1, :] for c in range(4) for r in range(2)], axis=0)
        rows = pltpu.roll(rows, lax.rem(FR - 8 * g, FR), 1)
        columns = jnp.concatenate([rows, jnp.zeros((FR - 8, FR), F32)], axis=0).T[:8]
        for i in range(8):
            shifted = pltpu.roll(columns, FR - 1 - i, 1)
            ent_out[s, 8 * i : 8 * i + 8, :] = jnp.where(lane == FR - 1, shifted, 0.0)


def blank(query_ref, value_ref, weight_ref):
    def body(i, carry):
        for p in range(5):
            query_ref[i, p, :HD, FR:] = jnp.zeros((HD, FR), BF16)
            query_ref[i, p, HD:, :FR] = jnp.zeros((HD, FR), BF16)
            value_ref[i, p, HD:] = jnp.ones((16, 2 * FR), BF16)
            weight_ref[i, p, :FR, FR:] = jnp.zeros((FR, FR), BF16)
            weight_ref[i, p, FR:, :FR] = jnp.zeros((FR, FR), BF16)
        return carry

    lax.fori_loop(0, PX, body, 0)


def embed(level, twt_ref, emb_ref):
    index = lax.broadcasted_iota(jnp.int32, (CH // 2, FR), 0).astype(F32)
    freqs = jnp.exp(-math.log(10000.0) * index / (CH // 2))
    sine, cosine = sin_cos(level * freqs)
    feature = jnp.concatenate([sine, cosine], axis=0)
    high = feature.astype(BF16)
    low = (feature - high.astype(F32)).astype(BF16)
    emb_ref[...] = dot(twt_ref[...], jnp.concatenate([high, low, high], axis=0))


def coefficients(level):
    lane = lanes((8, FR))
    level = jnp.broadcast_to(level, (8, FR))
    target = jnp.where(lane == 0, 0.0, pltpu.roll(level, 1, 1))
    angle = lambda l: (l / 1000.0 + 0.008) / 1.008 * (math.pi / 2.0)
    s0, c0 = sin_cos(angle(level))
    s1, c1 = sin_cos(angle(target))
    alpha = c1 / c0
    return alpha, s1 - alpha * s0


def conv_in(slots, band_ref, emb_ref, rhs_ref, hid_ref, act_ref, g, t):
    rows = []
    for slot in slots:
        for r in range(2):
            rows.append(jnp.concatenate(
                [slot[k * 16 + r * 8 : k * 16 + r * 8 + 8] for k in range(6)], axis=0).astype(BF16))
    for p in range(2):
        for half in range(2):
            rhs_ref[p, :, half * FR : (half + 1) * FR] = jnp.concatenate(
                rows[2 * p + half : 2 * p + half + 3], axis=0)

    def body(w, carry):
        inside = ((w > 0) | (g > 0)) & ((w < PX + 1) | (g < NQ - 1))
        active = []
        for p in range(2):
            both = dot(band_ref[w], rhs_ref[p])
            for half in range(2):
                hidden = both[:, half * FR : (half + 1) * FR] + emb_ref[...]
                if p != half:
                    hid_ref[w, p] = hidden
                    active.append(jnp.where(inside, silu(hidden), 0.0))
                else:
                    active.append(jnp.where(inside & ((t > 0) if p == 0 else (t < NT - 1)), silu(hidden), 0.0))
        a0, a1, a2, a3 = active
        for v, part in enumerate((a0 - a2, a1 + a2, a2 - a1, a1 - a3)):
            act_ref[w, v] = part.astype(BF16)
        return carry

    lax.fori_loop(0, PX + 2, body, 0, unroll=PX + 2)


def unit(x, scale):
    return (x * (lax.rsqrt(jnp.sum(x * x, axis=0, keepdims=True) + 1e-06) * scale)).astype(BF16)


def each(bodies, count):
    def step(i, carry):
        for body in bodies:
            body(i)
        return carry

    lax.fori_loop(0, count, step, 0, unroll=count)


def places():
    pairs = [((s, 2 * p), (s, 2 * p + 1)) for s in range(2) for p in range(2)]
    return pairs + [((0, 4), (1, 4))]


def block_net(hs_ref, mid_ref, qkvt_ref, wot_ref, wet_ref, gain_ref, near_ref, hid_ref, act_ref, noise_ref,
              block_ref, normed_ref, project_ref, query_ref, stack_ref, key_ref, value_ref, weight_ref, mixed_ref):
    def norm(i, block):
        block_ref[i] = block
        center = jnp.mean(block, axis=0, keepdims=True)
        moved = block - center
        spread = jnp.mean(moved * moved, axis=0, keepdims=True)
        gain = jnp.concatenate([gain_ref[...]] * 2, axis=1)
        normed_ref[i] = (moved * lax.rsqrt(spread + 1e-05) * gain).astype(BF16)

    def conv_mid(j):
        parts = []
        for v in range(4):
            rhs = [jnp.concatenate([act_ref[2 * j + dx, v], act_ref[2 * j + dx + 1, v]], axis=1) for dx in range(3)]
            parts.append(dot(mid_ref[v], jnp.concatenate(rhs, axis=0)))
        for r, part in enumerate((parts[0] + (parts[1] + parts[2]), (parts[1] - parts[2]) - parts[3])):
            hidden = jnp.concatenate([hid_ref[2 * j + 1, r], hid_ref[2 * j + 2, r]], axis=1)
            norm(4 * r + j, hidden + part)

    def project(i):
        project_ref[i] = dot(qkvt_ref[...], normed_ref[i])

    def units(i):
        for p, pair in enumerate(places()):
            for n, (s, h) in enumerate(pair):
                cut, own = slice(s * FR, (s + 1) * FR), slice(n * FR, (n + 1) * FR)
                part = lambda k: project_ref[i, k * CH + h * HD : k * CH + (h + 1) * HD, cut]
                query_ref[i, p, n * HD : (n + 1) * HD, own] = unit(part(0), hs_ref[h] * math.log2(math.e))
                stack_ref[i, p, n * HD : (n + 1) * HD] = unit(part(1), 1.0)
                value_ref[i, p, :HD, own] = part(2).astype(BF16)
            key_ref[i, p] = stack_ref[i, p].T

    def attend(i):
        for p in range(5):
            weights = jnp.exp2(dot(key_ref[i, p], query_ref[i, p])).astype(BF16)
            for n in range(2):
                own = slice(n * FR, (n + 1) * FR)
                weight_ref[i, p, own, own] = weights[:, own] * near_ref[...]

    def mix(i):
        for p, ((s, h), _) in enumerate(places()):
            total = dot(value_ref[i, p], weight_ref[i, p])
            part = (total[:HD] * (1.0 / total[HD : HD + 1])).astype(BF16)
            if p == 4:
                mixed_ref[i, h * HD :, :] = part
            else:
                cut = slice(s * FR, (s + 1) * FR)
                mixed_ref[i, h * HD : (h + 1) * HD, cut] = part[:, :FR]
                mixed_ref[i, (h + 1) * HD : (h + 2) * HD, cut] = part[:, FR:]

    def upper(i):
        normed_ref[i] = silu(block_ref[i] + dot(wot_ref[...], mixed_ref[i])).astype(BF16)

    def noise(i):
        noise_ref[i] = dot(wet_ref[...], normed_ref[i])[:8]

    each((conv_mid,), PX // 2)
    for bodies in ((project, units), (attend,), (mix,), (upper,), (noise,)):
        each(bodies, PX)


def advance(state, noise_ref, alpha, beta, entering):
    tiles = []
    for c in range(4):
        for r in range(2):
            rows = [noise_ref[r * 4 + w // 2, c : c + 1, (w % 2) * FR : (w % 2 + 1) * FR] for w in range(PX)]
            noise = jnp.concatenate(rows, axis=0)
            at = c * 16 + r * 8
            tiles.append(alpha * state[at : at + 8] + beta * noise)
    updated = jnp.concatenate(tiles, axis=0)
    return jnp.where(lanes((64, FR)) == FR - 1, entering, pltpu.roll(updated, FR - 1, 1))


def masked(slot, index, g, t):
    inside = (t > 0) if index == 0 else (t < NT - 1) if index == 2 else None
    own, left, right = slot[:64], slot[64:80], slot[80:96]
    left = jnp.where(g > 0, left, 0.0)
    right = jnp.where(g < NQ - 1, right, 0.0)
    slot = jnp.concatenate([own, left, right], axis=0)
    return slot if inside is None else jnp.where(inside, slot, 0.0)


def kernel(lat_hbm, ent_hbm, lev_hbm, tw_hbm, cin_hbm, cmid_hbm, gain_hbm, qkv_hbm, hs_hbm, wo_hbm, we_hbm,
           out_ref,
           lat_ref, ent_ref, lev_ref, tw_ref, cin_ref, cmid_ref, gain_ref, qkv_ref, hs_ref, wo_ref, we_ref, taps_ref,
           twt_ref, band_ref, mid_ref, qkvt_ref, wot_ref, wet_ref, gain_out, near_ref, ent_out,
           emb_ref, rhs_ref, hid_ref, act_ref, noise_ref,
           block_ref, normed_ref, project_ref, query_ref, stack_ref, key_ref, value_ref, weight_ref, mixed_ref,
           send1, recv1, halo, state_ref, own_ref, left_ref, right_ref, send3, recv3,
           load_sem, send1_sem, recv1_sem, send2_sem, recv2_sem, send3_sem, recv3_sem):
    q, t = lax.axis_index("queue"), lax.axis_index("tile")
    g = group_of(q)
    sides = [(t > 0, t - 1, 2), (t < NT - 1, t + 1, 0)]
    others = OFFSETS[:-1]

    barrier = pltpu.get_barrier_semaphore()
    for there, row, _ in sides:
        @pl.when(there)
        def _():
            for offset in OFFSETS:
                pl.semaphore_signal(barrier, inc=1, device_id=(peer_at(q, offset), row), device_id_type=MESH)
    for offset in others:
        pl.semaphore_signal(barrier, inc=1, device_id=(peer_at(q, offset), t), device_id_type=MESH)

    loads = [pltpu.make_async_copy(src, dst, load_sem.at[i]) for i, (src, dst) in enumerate(
        [(lat_hbm, lat_ref), (lev_hbm, lev_ref), (cmid_hbm, cmid_ref), (qkv_hbm, qkv_ref), (wo_hbm, wo_ref),
         (tw_hbm, tw_ref), (ent_hbm, ent_ref), (cin_hbm, cin_ref), (gain_hbm, gain_ref), (hs_hbm, hs_ref),
         (we_hbm, we_ref)])]
    for load in loads:
        load.start()
    for load in loads[:2]:
        load.wait()
    pack_latents(lat_ref, lev_ref, send1)
    both = (t > 0).astype(jnp.int32) + (t < NT - 1).astype(jnp.int32)
    pl.semaphore_wait(barrier, NQ - 1 + NQ * both)

    place = pl.ds(pl.multiple_of(q * 8, 8), 8)

    def to_peer(offset, row, slot):
        peer = peer_at(q, offset)
        pltpu.make_async_remote_copy(
            src_ref=send1.at[group_of(peer)], dst_ref=recv1.at[slot, place],
            send_sem=send1_sem.at[slot], recv_sem=recv1_sem.at[slot],
            device_id=(peer, row), device_id_type=MESH).start()

    for there, row, slot in sides:
        @pl.when(there)
        def _():
            for offset in OFFSETS:
                to_peer(offset, row, slot)
    for offset in others:
        to_peer(offset, t, 1)
    recv1[1, place] = send1[g]

    for load in loads[2:]:
        load.wait()
    prepare(cin_ref, cmid_ref, gain_ref, qkv_ref, wo_ref, we_ref, ent_ref, tw_ref, taps_ref,
            twt_ref, band_ref, mid_ref, qkvt_ref, wot_ref, wet_ref, gain_out, near_ref, ent_out, g)
    blank(query_ref, value_ref, weight_ref)

    def settle(ref, sem, count):
        part = ref.at[pl.ds(0, count)]
        pltpu.make_async_copy(part, part, sem).wait()

    settle(recv1.at[1], recv1_sem.at[1], FR - 8)
    for there, slot in ((t > 0, 0), (t < NT - 1, 2)):
        @pl.when(there)
        def _():
            settle(recv1.at[slot], recv1_sem.at[slot], FR)
    slots = [recv1[slot].T for slot in range(3)]
    level = slots[1][2 * ROW : 2 * ROW + 1]
    embed(level, twt_ref, emb_ref)
    alpha, beta = coefficients(level)
    state = slots[1][:64]
    slots = [masked(slot[: 2 * ROW], i, g, t) for i, slot in enumerate(slots)]

    conv_in(slots, band_ref, emb_ref, rhs_ref, hid_ref, act_ref, g, t)
    block_net(hs_ref, mid_ref, qkvt_ref, wot_ref, wet_ref, gain_out, near_ref, hid_ref, act_ref, noise_ref,
              block_ref, normed_ref, project_ref, query_ref, stack_ref, key_ref, value_ref, weight_ref, mixed_ref)
    state = advance(state, noise_ref, alpha, beta, ent_out[0])

    state_ref[...] = state
    own_ref[...] = state.astype(BF16)
    lefts, rights = [], []
    for r in range(2):
        for c in range(4):
            at = c * 16 + r * 8
            lefts.append(state[at + 6 : at + 8])
            rights.append(state[at : at + 2])
    left_ref[...] = jnp.concatenate(lefts, axis=0).astype(BF16)
    right_ref[...] = jnp.concatenate(rights, axis=0).astype(BF16)
    copies = []
    for src, start, size, step in ((left_ref, 64, 16, 1), (right_ref, 80, 16, -1), (own_ref, 0, 64, 0)):
        sent, got = (g < NQ - 1, g > 0) if step == 1 else (g > 0, g < NQ - 1) if step == -1 else (None, None)
        peer = group_of(jnp.clip(g + step, 0, NQ - 1))
        for down in (-1, 1, 0):
            if step == 0 and down == 0:
                continue
            sent_too, got_too = (t > 0, t < NT - 1) if down == -1 else (t < NT - 1, t > 0) if down == 1 else (None, None)
            both_of = lambda a, b: b if a is None else a if b is None else a & b
            i = len(copies)
            copies.append((both_of(sent, sent_too), both_of(got, got_too), pltpu.make_async_remote_copy(
                src_ref=src, dst_ref=halo.at[1 - down, pl.ds(start, size)],
                send_sem=send2_sem.at[i], recv_sem=recv2_sem.at[i],
                device_id=(peer, t + down), device_id_type=MESH)))
    for sent, _, copy in copies:
        pl.when(sent)(copy.start)
    for _, got, copy in copies:
        pl.when(got)(copy.wait_recv)
    halo[1, :64] = own_ref[...]
    slots = [masked(halo[i].astype(F32), i, g, t) for i in range(3)]

    conv_in(slots, band_ref, emb_ref, rhs_ref, hid_ref, act_ref, g, t)
    block_net(hs_ref, mid_ref, qkvt_ref, wot_ref, wet_ref, gain_out, near_ref, hid_ref, act_ref, noise_ref,
              block_ref, normed_ref, project_ref, query_ref, stack_ref, key_ref, value_ref, weight_ref, mixed_ref)
    state = advance(state_ref[...], noise_ref, alpha, beta, ent_out[1])

    frames = jnp.concatenate([state, jnp.zeros((64, FR), F32)], axis=0).T
    for peer in range(NQ):
        send3[peer] = frames[peer * 8 : peer * 8 + 8]
    for offset in others:
        peer = peer_at(q, offset)
        pltpu.make_async_remote_copy(
            src_ref=send3.at[peer], dst_ref=recv3.at[g],
            send_sem=send3_sem.at[0], recv_sem=recv3_sem.at[0],
            device_id=(peer, t), device_id_type=MESH).start()
    recv3[g] = send3[q]
    for sent, _, copy in copies:
        pl.when(sent)(copy.wait_send)
    settle(send1, send1_sem.at[1], NQ - 1)
    for there, _, slot in sides:
        @pl.when(there)
        def _():
            settle(send1, send1_sem.at[slot], NQ)
    settle(recv3, recv3_sem.at[0], NQ - 1)

    group = lanes((8, FR)) >> 3
    turned = [pltpu.roll(recv3[source], 8 * source, 1) for source in range(NQ)]
    for c in range(4):
        for r in range(2):
            at = c * 2 + r
            total = turned[0]
            for source in range(1, NQ):
                total = jnp.where(group == (source + at) % NQ, turned[source], total)
            out_ref[:, c, r, :] = pltpu.roll(total, (FR - 8 * at) % FR, 1)
    settle(send3, send3_sem.at[0], NQ - 1)


def per_device(queue_latents, entering, levels, time_weight, conv_in_weight, conv_mid_weight, norm_gain,
               qkv_weight, head_scale, attn_out_weight, eps_out_weight):
    hbm = pl.BlockSpec(memory_space=pl.ANY)
    v = pltpu.VMEM
    dma = pltpu.SemaphoreType.DMA
    inputs = (queue_latents, entering, levels, time_weight, conv_in_weight, conv_mid_weight,
              norm_gain, qkv_weight, head_scale, attn_out_weight, eps_out_weight.T)
    scalars = (levels, head_scale)
    return pl.pallas_call(
        kernel,
        out_shape=pltpu.VMEM(queue_latents.shape, F32),
        in_specs=[hbm] * len(inputs),
        out_specs=pl.BlockSpec(memory_space=pltpu.VMEM),
        scratch_shapes=[
            *[(pltpu.SMEM if any(x is y for y in scalars) else v)(x.shape, x.dtype) for x in inputs],
            v((40, CH), F32),
            v((CH, 3 * CH), BF16),
            v((PX + 2, CH, TAPS), BF16), v((4, CH, 3 * CH), BF16), v((3 * CH, CH), BF16), v((CH, CH), BF16),
            v((16, CH), BF16), v((CH, FR), F32), v((FR, FR), BF16), v((STEPS, 64, FR), F32),
            v((CH, FR), F32), v((2, TAPS, 2 * FR), BF16), v((PX + 2, 2, CH, FR), F32),
            v((PX + 2, 4, CH, FR), BF16), v((PX, 8, 2 * FR), F32),
            v((PX, CH, 2 * FR), F32), v((PX, CH, 2 * FR), BF16), v((PX, 3 * CH, 2 * FR), F32),
            v((PX, 5, FR, 2 * FR), BF16), v((PX, 5, FR, FR), BF16), v((PX, 5, FR, FR), BF16),
            v((PX, 5, HD + 16, 2 * FR), BF16), v((PX, 5, 2 * FR, 2 * FR), BF16), v((PX, CH, 2 * FR), BF16),
            v((NQ, 8, FR), F32), v((3, FR, FR), F32), v((3, 2 * ROW, FR), BF16), v((64, FR), F32), v((64, FR), BF16),
            v((16, FR), BF16), v((16, FR), BF16), v((NQ, 8, FR), F32), v((NQ, 8, FR), F32),
            dma((len(inputs),)), dma((3,)), dma((3,)), dma((8,)), dma((8,)), dma((1,)), dma((1,)),
        ],
        compiler_params=pltpu.CompilerParams(
            collective_id=0, has_side_effects=True, vmem_limit_bytes=56 * 1024 * 1024),
    )(*inputs)


def solution(mesh):
    placed = (
        P("queue", None, "tile", None),
        P(None, None, "tile", None),
        P("queue"),
        P(),
        P(),
        P(),
        P(),
        P(),
        P(),
        P(),
        P(),
    )
    return jax.shard_map(
        per_device,
        mesh=mesh,
        in_specs=placed,
        out_specs=P("queue", None, "tile", None),
        check_vma=False,
    )
```

```python
import math

import jax
import jax.numpy as jnp
from jax import lax
from jax.experimental import pallas as pl
from jax.experimental.pallas import tpu as pltpu
from jax.sharding import PartitionSpec as P

WIN = 8
STEPS = 2
F32 = jnp.float32
BF16 = jnp.bfloat16
MESH = pl.DeviceIdType.MESH

CH = 320
HEADS = 5
HD = 64
FR = 128
NQ = 16
NT = 8
PX = 8
ROW = 48
TAPS = 3 * ROW


def dot(a, b):
    return jnp.dot(a, b, preferred_element_type=F32)


def dot_t(a, b):
    return lax.dot_general(a, b, (((0,), (0,)), ((), ())), preferred_element_type=F32)


def sin_cos(angle):
    count = jnp.floor(angle * (2.0 / math.pi) + 0.5)
    rest = ((angle - count * 1.5703125) - count * 4.837512969970703125e-4) - count * 7.54978995489188216e-8
    square = rest * rest
    sine = rest + rest * square * (
        -1.6666654611e-1 + square * (8.3321608736e-3 - square * 1.9515295891e-4)
    )
    cosine = 1.0 - 0.5 * square + square * square * (
        4.166664568298827e-2 + square * (-1.388731625493765e-3 + square * 2.443315711809948e-5)
    )
    quarter = count - 4.0 * jnp.floor(count * 0.25)
    odd = (quarter == 1.0) | (quarter == 3.0)
    sin_out = jnp.where(odd, cosine, sine)
    cos_out = jnp.where(odd, sine, cosine)
    sin_out = jnp.where(quarter >= 2.0, -sin_out, sin_out)
    cos_out = jnp.where((quarter == 1.0) | (quarter == 2.0), -cos_out, cos_out)
    return sin_out, cos_out


def silu_of_half(half):
    return half + half * jnp.tanh(half)


def lanes(shape):
    return lax.broadcasted_iota(jnp.int32, shape, 1)


OFFSETS = sorted(((z, x, c) for z in (0, 1) for x in range(4) for c in (0, 1)),
                 key=lambda o: -(2 * o[0] + min(o[1], 4 - o[1]) + 0.1 * o[2]))


def peer_at(q, offset):
    z, x, c = offset
    return ((q ^ (8 * z)) & 8) | ((q + 2 * x) & 6) | ((q ^ c) & 1)


def group_of(q):
    return jnp.where(q < NQ // 2, q, 3 * NQ // 2 - 1 - q)


def pack_latents(lat_ref, lev_ref, send_ref):
    lane = lanes((8, FR))
    row = lax.broadcasted_iota(jnp.int32, (8, FR), 0)
    pieces = []
    for c in range(4):
        for r in range(2):
            plane = lat_ref[:, c, r, :]
            own, left, right = c * 16 + r * 8, 64 + r * 8 + c * 2, 80 + r * 8 + c * 2
            pieces.append((3, own, pltpu.roll(plane, own, 1)))
            pieces.append((1, left, pltpu.roll(plane, left + 2, 1)))
            pieces.append((1, right, pltpu.roll(plane, right - 8, 1)))
    level = jnp.zeros((8, FR), F32)
    for f in range(8):
        level = jnp.where(row == f, lev_ref[f].astype(F32), level)

    def body(dest, carry):
        place = (lane - 8 * dest) & (FR - 1)
        total = jnp.zeros((8, FR), F32)
        for bits, base, plane in pieces:
            total = jnp.where((place >> bits) == (base >> bits), plane, total)
        total = pltpu.roll(total, lax.rem(FR - 8 * dest, FR), 1)
        send_ref[dest] = jnp.where(lane == 2 * ROW, level, total)
        return carry

    lax.fori_loop(0, NQ, body, 0)


def prepare(cin_ref, cmid_ref, gain_ref, qkv_ref, wo_ref, we_ref, ent_ref, tw_ref, taps_ref,
            twt_ref, band_ref, mid_ref, qkvt_ref, wot_ref, wet_ref, gain_out, near_ref, ent_out, g):
    taps_ref[...] = jnp.zeros(taps_ref.shape, F32)
    for i in range(9):
        taps_ref[4 * i : 4 * i + 4, :] = cin_ref[i // 3, i % 3].astype(F32)
    taps_t = taps_ref[...].T.astype(BF16)
    k = lanes((40, TAPS))
    m = lax.broadcasted_iota(jnp.int32, (40, TAPS), 0)
    dy = (k >= ROW).astype(jnp.int32) + (k >= 2 * ROW).astype(jnp.int32)
    rest = k - ROW * dy
    own = rest < 32
    left = rest < 40
    c = jnp.where(own, rest >> 3, (rest & 7) >> 1)
    rel = jnp.where(own, (rest & 7) + 2, jnp.where(left, rest & 1, (rest & 1) + 10))
    for w in range(PX + 2):
        dx = rel - w
        pick = (dx >= 0) & (dx <= 2) & (m == dy * 12 + dx * 4 + c)
        band_ref[w] = dot(taps_t, jnp.where(pick, 0.5, 0.0).astype(BF16)).astype(BF16)
    taps = [0.5 * jnp.concatenate([cmid_ref[dy, dx].astype(F32) for dx in range(3)], axis=0) for dy in range(3)]
    outer = 0.5 * (taps[0] + taps[2])
    for v, mid in enumerate((taps[0], outer + 0.5 * taps[1], outer - 0.5 * taps[1], taps[2])):
        mid_ref[v] = mid.astype(BF16).T
    weight = 0.5 * tw_ref[...].T
    high = weight.astype(BF16)
    low = (weight - high.astype(F32)).astype(BF16)
    twt_ref[...] = jnp.concatenate([high, high, low], axis=1)
    qkvt_ref[...] = qkv_ref[...].T
    wot_ref[...] = (0.5 * wo_ref[...].astype(F32)).astype(BF16).T
    wet_ref[...] = jnp.concatenate([we_ref[...].astype(F32), jnp.zeros((12, CH), F32)], axis=0).astype(BF16)
    gain_out[...] = jnp.broadcast_to(gain_ref[...].reshape(1, CH), (FR, CH)).T
    key_slot = lax.broadcasted_iota(jnp.int32, (FR, 2 * FR), 0)
    query_slot = lanes((FR, 2 * FR)) & (FR - 1)
    near_ref[...] = jnp.where(jnp.abs(key_slot - query_slot) <= WIN, 1.0, 0.0)
    lane = lanes((8, FR))
    for s in range(STEPS):
        rows = jnp.concatenate([ent_ref[s, c, r : r + 1, :] for c in range(4) for r in range(2)], axis=0)
        rows = pltpu.roll(rows, lax.rem(FR - 8 * g, FR), 1)
        columns = jnp.concatenate([rows, jnp.zeros((FR - 8, FR), F32)], axis=0).T[:8]
        for i in range(8):
            shifted = pltpu.roll(columns, FR - 1 - i, 1)
            ent_out[s, 8 * i : 8 * i + 8, :] = jnp.where(lane == FR - 1, shifted, 0.0)


def blank(query_ref):
    def body(i, carry):
        for p in range(5):
            query_ref[i, p, :HD, FR:] = jnp.zeros((HD, FR), BF16)
            query_ref[i, p, HD:, :FR] = jnp.zeros((HD, FR), BF16)
        return carry

    lax.fori_loop(0, PX, body, 0)


def embed(level, twt_ref, emb_ref):
    index = lax.broadcasted_iota(jnp.int32, (CH // 2, FR), 0).astype(F32)
    freqs = jnp.exp(-math.log(10000.0) * index / (CH // 2))
    sine, cosine = sin_cos(level * freqs)
    feature = jnp.concatenate([sine, cosine], axis=0)
    high = feature.astype(BF16)
    low = (feature - high.astype(F32)).astype(BF16)
    emb_ref[...] = dot(twt_ref[...], jnp.concatenate([high, low, high], axis=0))


def coefficients(level):
    lane = lanes((8, FR))
    level = jnp.broadcast_to(level, (8, FR))
    target = jnp.where(lane == 0, 0.0, pltpu.roll(level, 1, 1))
    angle = lambda l: (l / 1000.0 + 0.008) / 1.008 * (math.pi / 2.0)
    s0, c0 = sin_cos(angle(level))
    s1, c1 = sin_cos(angle(target))
    alpha = c1 / c0
    return alpha, s1 - alpha * s0


def conv_in(slots, band_ref, emb_ref, rhs_ref, hid_ref, act_ref, g, t):
    rows = []
    for slot in slots:
        for r in range(2):
            rows.append(jnp.concatenate(
                [slot[k * 16 + r * 8 : k * 16 + r * 8 + 8] for k in range(6)], axis=0).astype(BF16))
    for p in range(2):
        for half in range(2):
            rhs_ref[p, :, half * FR : (half + 1) * FR] = jnp.concatenate(
                rows[2 * p + half : 2 * p + half + 3], axis=0)

    def body(w, carry):
        inside = ((w > 0) | (g > 0)) & ((w < PX + 1) | (g < NQ - 1))
        active = []
        for p in range(2):
            both = dot(band_ref[w], rhs_ref[p])
            for half in range(2):
                hidden = both[:, half * FR : (half + 1) * FR] + emb_ref[...]
                if p != half:
                    hid_ref[w, p] = hidden
                    active.append(jnp.where(inside, silu_of_half(hidden), 0.0))
                else:
                    active.append(jnp.where(inside & ((t > 0) if p == 0 else (t < NT - 1)), silu_of_half(hidden), 0.0))
        a0, a1, a2, a3 = active
        for v, part in enumerate((a0 - a2, a1 + a2, a2 - a1, a1 - a3)):
            act_ref[w, v] = part.astype(BF16)
        return carry

    lax.fori_loop(0, PX + 2, body, 0, unroll=PX + 2)


def unit(x, scale):
    return (x * (lax.rsqrt(jnp.sum(x * x, axis=0, keepdims=True) + 1e-06) * scale)).astype(BF16)


def each(bodies, count):
    def step(i, carry):
        for body in bodies:
            body(i)
        return carry

    lax.fori_loop(0, count, step, 0, unroll=count)


def places():
    pairs = [((s, 2 * p), (s, 2 * p + 1)) for s in range(2) for p in range(2)]
    return pairs + [((0, 4), (1, 4))]


def block_net(hs_ref, mid_ref, qkvt_ref, wot_ref, wet_ref, gain_ref, near_ref, hid_ref, act_ref, noise_ref,
              block_ref, normed_ref, project_ref, query_ref, stack_ref, key_ref, value_ref, weight_ref, total_ref, mixed_ref):
    def norm(i, block):
        block_ref[i] = block
        center = jnp.mean(block, axis=0, keepdims=True)
        moved = block - center
        spread = jnp.mean(moved * moved, axis=0, keepdims=True)
        gain = jnp.concatenate([gain_ref[...]] * 2, axis=1)
        normed_ref[i] = (moved * lax.rsqrt(spread + 1e-05 / 4) * gain).astype(BF16)

    def conv_mid(j):
        parts = []
        for v in range(4):
            rhs = [jnp.concatenate([act_ref[2 * j + dx, v], act_ref[2 * j + dx + 1, v]], axis=1) for dx in range(3)]
            parts.append(dot(mid_ref[v], jnp.concatenate(rhs, axis=0)))
        for r, part in enumerate((parts[0] + (parts[1] + parts[2]), (parts[1] - parts[2]) - parts[3])):
            hidden = jnp.concatenate([hid_ref[2 * j + 1, r], hid_ref[2 * j + 2, r]], axis=1)
            norm(4 * r + j, hidden + part)

    def project(i):
        project_ref[i] = dot(qkvt_ref[...], normed_ref[i])

    def units(i):
        for p, pair in enumerate(places()):
            for n, (s, h) in enumerate(pair):
                cut, own = slice(s * FR, (s + 1) * FR), slice(n * FR, (n + 1) * FR)
                part = lambda k: project_ref[i, k * CH + h * HD : k * CH + (h + 1) * HD, cut]
                query_ref[i, p, n * HD : (n + 1) * HD, own] = unit(part(0), hs_ref[h] * math.log2(math.e))
                stack_ref[i, p, n * HD : (n + 1) * HD] = unit(part(1), 1.0)
                value_ref[i, p, :, own] = part(2).astype(BF16)
            key_ref[i, p] = stack_ref[i, p].T

    def attend(i):
        for p in range(5):
            weights = jnp.exp2(dot(key_ref[i, p], query_ref[i, p])) * near_ref[...]
            total_ref[i, p] = jnp.sum(weights, axis=0, keepdims=True)
            weight_ref[i, p] = weights.astype(BF16)

    def mix(i):
        for p, pair in enumerate(places()):
            share = 1.0 / total_ref[i, p]
            for n, (s, h) in enumerate(pair):
                cut, own = slice(s * FR, (s + 1) * FR), slice(n * FR, (n + 1) * FR)
                part = dot(value_ref[i, p, :, own], weight_ref[i, p, :, own]) * share[:, own]
                mixed_ref[i, h * HD : (h + 1) * HD, cut] = part.astype(BF16)

    def upper(i):
        normed_ref[i] = silu_of_half(block_ref[i] + dot(wot_ref[...], mixed_ref[i])).astype(BF16)

    def noise(i):
        noise_ref[i] = dot(wet_ref[...], normed_ref[i])[:8]

    each((conv_mid,), PX // 2)
    for bodies in ((project, units), (attend,), (mix,), (upper,), (noise,)):
        each(bodies, PX)


def advance(state, noise_ref, alpha, beta, entering):
    tiles = []
    for c in range(4):
        for r in range(2):
            rows = [noise_ref[r * 4 + w // 2, c : c + 1, (w % 2) * FR : (w % 2 + 1) * FR] for w in range(PX)]
            noise = jnp.concatenate(rows, axis=0)
            at = c * 16 + r * 8
            tiles.append(alpha * state[at : at + 8] + beta * noise)
    updated = jnp.concatenate(tiles, axis=0)
    return jnp.where(lanes((64, FR)) == FR - 1, entering, pltpu.roll(updated, FR - 1, 1))


def masked(slot, index, g, t):
    inside = (t > 0) if index == 0 else (t < NT - 1) if index == 2 else None
    own, left, right = slot[:64], slot[64:80], slot[80:96]
    left = jnp.where(g > 0, left, 0.0)
    right = jnp.where(g < NQ - 1, right, 0.0)
    slot = jnp.concatenate([own, left, right], axis=0)
    return slot if inside is None else jnp.where(inside, slot, 0.0)


def kernel(lat_hbm, ent_hbm, lev_hbm, tw_hbm, cin_hbm, cmid_hbm, gain_hbm, qkv_hbm, hs_hbm, wo_hbm, we_hbm,
           out_ref,
           lat_ref, ent_ref, lev_ref, tw_ref, cin_ref, cmid_ref, gain_ref, qkv_ref, hs_ref, wo_ref, we_ref, taps_ref,
           twt_ref, band_ref, mid_ref, qkvt_ref, wot_ref, wet_ref, gain_out, near_ref, ent_out,
           emb_ref, rhs_ref, hid_ref, act_ref, noise_ref,
           block_ref, normed_ref, project_ref, query_ref, stack_ref, key_ref, value_ref, weight_ref, total_ref, mixed_ref,
           send1, recv1, halo, state_ref, own_ref, left_ref, right_ref, send3, recv3,
           load_sem, send1_sem, recv1_sem, send2_sem, recv2_sem, send3_sem, recv3_sem):
    q, t = lax.axis_index("queue"), lax.axis_index("tile")
    g = group_of(q)
    sides = [(t > 0, t - 1, 2), (t < NT - 1, t + 1, 0)]
    others = OFFSETS[:-1]

    barrier = pltpu.get_barrier_semaphore()
    for there, row, _ in sides:
        @pl.when(there)
        def _():
            for offset in OFFSETS:
                pl.semaphore_signal(barrier, inc=1, device_id=(peer_at(q, offset), row), device_id_type=MESH)
    for offset in others:
        pl.semaphore_signal(barrier, inc=1, device_id=(peer_at(q, offset), t), device_id_type=MESH)

    loads = [pltpu.make_async_copy(src, dst, load_sem.at[i]) for i, (src, dst) in enumerate(
        [(lat_hbm, lat_ref), (lev_hbm, lev_ref), (cmid_hbm, cmid_ref), (qkv_hbm, qkv_ref), (wo_hbm, wo_ref),
         (tw_hbm, tw_ref), (ent_hbm, ent_ref), (cin_hbm, cin_ref), (gain_hbm, gain_ref), (hs_hbm, hs_ref),
         (we_hbm, we_ref)])]
    for load in loads:
        load.start()
    for load in loads[:2]:
        load.wait()
    pack_latents(lat_ref, lev_ref, send1)
    both = (t > 0).astype(jnp.int32) + (t < NT - 1).astype(jnp.int32)
    pl.semaphore_wait(barrier, NQ - 1 + NQ * both)

    place = pl.ds(pl.multiple_of(q * 8, 8), 8)

    def to_peer(offset, row, slot):
        peer = peer_at(q, offset)
        pltpu.make_async_remote_copy(
            src_ref=send1.at[group_of(peer)], dst_ref=recv1.at[slot, place],
            send_sem=send1_sem.at[slot], recv_sem=recv1_sem.at[slot],
            device_id=(peer, row), device_id_type=MESH).start()

    for there, row, slot in sides:
        @pl.when(there)
        def _():
            for offset in OFFSETS:
                to_peer(offset, row, slot)
    for offset in others:
        to_peer(offset, t, 1)
    recv1[1, place] = send1[g]

    for load in loads[2:]:
        load.wait()
    prepare(cin_ref, cmid_ref, gain_ref, qkv_ref, wo_ref, we_ref, ent_ref, tw_ref, taps_ref,
            twt_ref, band_ref, mid_ref, qkvt_ref, wot_ref, wet_ref, gain_out, near_ref, ent_out, g)
    blank(query_ref)

    def settle(ref, sem, count):
        part = ref.at[pl.ds(0, count)]
        pltpu.make_async_copy(part, part, sem).wait()

    settle(recv1.at[1], recv1_sem.at[1], FR - 8)
    for there, slot in ((t > 0, 0), (t < NT - 1, 2)):
        @pl.when(there)
        def _():
            settle(recv1.at[slot], recv1_sem.at[slot], FR)
    slots = [recv1[slot].T for slot in range(3)]
    level = slots[1][2 * ROW : 2 * ROW + 1]
    embed(level, twt_ref, emb_ref)
    alpha, beta = coefficients(level)
    state = slots[1][:64]
    slots = [masked(slot[: 2 * ROW], i, g, t) for i, slot in enumerate(slots)]

    conv_in(slots, band_ref, emb_ref, rhs_ref, hid_ref, act_ref, g, t)
    block_net(hs_ref, mid_ref, qkvt_ref, wot_ref, wet_ref, gain_out, near_ref, hid_ref, act_ref, noise_ref,
              block_ref, normed_ref, project_ref, query_ref, stack_ref, key_ref, value_ref, weight_ref, total_ref, mixed_ref)
    state = advance(state, noise_ref, alpha, beta, ent_out[0])

    state_ref[...] = state
    own_ref[...] = state.astype(BF16)
    lefts, rights = [], []
    for r in range(2):
        for c in range(4):
            at = c * 16 + r * 8
            lefts.append(state[at + 6 : at + 8])
            rights.append(state[at : at + 2])
    left_ref[...] = jnp.concatenate(lefts, axis=0).astype(BF16)
    right_ref[...] = jnp.concatenate(rights, axis=0).astype(BF16)
    copies = []
    for src, start, size, step in ((left_ref, 64, 16, 1), (right_ref, 80, 16, -1), (own_ref, 0, 64, 0)):
        sent, got = (g < NQ - 1, g > 0) if step == 1 else (g > 0, g < NQ - 1) if step == -1 else (None, None)
        peer = group_of(jnp.clip(g + step, 0, NQ - 1))
        for down in (-1, 1, 0):
            if step == 0 and down == 0:
                continue
            sent_too, got_too = (t > 0, t < NT - 1) if down == -1 else (t < NT - 1, t > 0) if down == 1 else (None, None)
            both_of = lambda a, b: b if a is None else a if b is None else a & b
            i = len(copies)
            copies.append((both_of(sent, sent_too), both_of(got, got_too), pltpu.make_async_remote_copy(
                src_ref=src, dst_ref=halo.at[1 - down, pl.ds(start, size)],
                send_sem=send2_sem.at[i], recv_sem=recv2_sem.at[i],
                device_id=(peer, t + down), device_id_type=MESH)))
    for sent, _, copy in copies:
        pl.when(sent)(copy.start)
    for _, got, copy in copies:
        pl.when(got)(copy.wait_recv)
    halo[1, :64] = own_ref[...]
    slots = [masked(halo[i].astype(F32), i, g, t) for i in range(3)]

    conv_in(slots, band_ref, emb_ref, rhs_ref, hid_ref, act_ref, g, t)
    block_net(hs_ref, mid_ref, qkvt_ref, wot_ref, wet_ref, gain_out, near_ref, hid_ref, act_ref, noise_ref,
              block_ref, normed_ref, project_ref, query_ref, stack_ref, key_ref, value_ref, weight_ref, total_ref, mixed_ref)
    state = advance(state_ref[...], noise_ref, alpha, beta, ent_out[1])

    frames = jnp.concatenate([state, jnp.zeros((64, FR), F32)], axis=0).T
    for peer in range(NQ):
        send3[peer] = frames[peer * 8 : peer * 8 + 8]
    for offset in others:
        peer = peer_at(q, offset)
        pltpu.make_async_remote_copy(
            src_ref=send3.at[peer], dst_ref=recv3.at[g],
            send_sem=send3_sem.at[0], recv_sem=recv3_sem.at[0],
            device_id=(peer, t), device_id_type=MESH).start()
    recv3[g] = send3[q]
    for sent, _, copy in copies:
        pl.when(sent)(copy.wait_send)
    settle(send1, send1_sem.at[1], NQ - 1)
    for there, _, slot in sides:
        @pl.when(there)
        def _():
            settle(send1, send1_sem.at[slot], NQ)
    settle(recv3, recv3_sem.at[0], NQ - 1)

    group = lanes((8, FR)) >> 3
    turned = [pltpu.roll(recv3[source], 8 * source, 1) for source in range(NQ)]
    for c in range(4):
        for r in range(2):
            at = c * 2 + r
            total = turned[0]
            for source in range(1, NQ):
                total = jnp.where(group == (source + at) % NQ, turned[source], total)
            out_ref[:, c, r, :] = pltpu.roll(total, (FR - 8 * at) % FR, 1)
    settle(send3, send3_sem.at[0], NQ - 1)


def per_device(queue_latents, entering, levels, time_weight, conv_in_weight, conv_mid_weight, norm_gain,
               qkv_weight, head_scale, attn_out_weight, eps_out_weight):
    hbm = pl.BlockSpec(memory_space=pl.ANY)
    v = pltpu.VMEM
    dma = pltpu.SemaphoreType.DMA
    inputs = (queue_latents, entering, levels, time_weight, conv_in_weight, conv_mid_weight,
              norm_gain, qkv_weight, head_scale, attn_out_weight, eps_out_weight.T)
    scalars = (levels, head_scale)
    return pl.pallas_call(
        kernel,
        out_shape=pltpu.VMEM(queue_latents.shape, F32),
        in_specs=[hbm] * len(inputs),
        out_specs=pl.BlockSpec(memory_space=pltpu.VMEM),
        scratch_shapes=[
            *[(pltpu.SMEM if any(x is y for y in scalars) else v)(x.shape, x.dtype) for x in inputs],
            v((40, CH), F32),
            v((CH, 3 * CH), BF16),
            v((PX + 2, CH, TAPS), BF16), v((4, CH, 3 * CH), BF16), v((3 * CH, CH), BF16), v((CH, CH), BF16),
            v((16, CH), BF16), v((CH, FR), F32), v((FR, 2 * FR), F32), v((STEPS, 64, FR), F32),
            v((CH, FR), F32), v((2, TAPS, 2 * FR), BF16), v((PX + 2, 2, CH, FR), F32),
            v((PX + 2, 4, CH, FR), BF16), v((PX, 8, 2 * FR), F32),
            v((PX, CH, 2 * FR), F32), v((PX, CH, 2 * FR), BF16), v((PX, 3 * CH, 2 * FR), F32),
            v((PX, 5, FR, 2 * FR), BF16), v((PX, 5, FR, FR), BF16), v((PX, 5, FR, FR), BF16),
            v((PX, 5, HD, 2 * FR), BF16), v((PX, 5, FR, 2 * FR), BF16), v((PX, 5, 1, 2 * FR), F32),
            v((PX, CH, 2 * FR), BF16),
            v((NQ, 8, FR), F32), v((3, FR, FR), F32), v((3, 2 * ROW, FR), BF16), v((64, FR), F32), v((64, FR), BF16),
            v((16, FR), BF16), v((16, FR), BF16), v((NQ, 8, FR), F32), v((NQ, 8, FR), F32),
            dma((len(inputs),)), dma((3,)), dma((3,)), dma((8,)), dma((8,)), dma((1,)), dma((1,)),
        ],
        compiler_params=pltpu.CompilerParams(
            collective_id=0, has_side_effects=True, vmem_limit_bytes=56 * 1024 * 1024),
    )(*inputs)


def solution(mesh):
    placed = (
        P("queue", None, "tile", None),
        P(None, None, "tile", None),
        P("queue"),
        P(),
        P(),
        P(),
        P(),
        P(),
        P(),
        P(),
        P(),
    )
    return jax.shard_map(
        per_device,
        mesh=mesh,
        in_specs=placed,
        out_specs=P("queue", None, "tile", None),
        check_vma=False,
    )
```

```python
import math

import jax
import jax.numpy as jnp
from jax import lax
from jax.experimental import pallas as pl
from jax.experimental.pallas import tpu as pltpu
from jax.sharding import PartitionSpec as P

WIN = 8
STEPS = 2
F32 = jnp.float32
BF16 = jnp.bfloat16
MESH = pl.DeviceIdType.MESH

CH = 320
HEADS = 5
HD = 64
FR = 128
NQ = 16
NT = 8
PX = 8
ROW = 48
TAPS = 3 * ROW


def dot(a, b):
    return jnp.dot(a, b, preferred_element_type=F32)


def dot_t(a, b):
    return lax.dot_general(a, b, (((0,), (0,)), ((), ())), preferred_element_type=F32)


def sin_cos(angle):
    count = jnp.floor(angle * (2.0 / math.pi) + 0.5)
    rest = ((angle - count * 1.5703125) - count * 4.837512969970703125e-4) - count * 7.54978995489188216e-8
    square = rest * rest
    sine = rest + rest * square * (
        -1.6666654611e-1 + square * (8.3321608736e-3 - square * 1.9515295891e-4)
    )
    cosine = 1.0 - 0.5 * square + square * square * (
        4.166664568298827e-2 + square * (-1.388731625493765e-3 + square * 2.443315711809948e-5)
    )
    quarter = count - 4.0 * jnp.floor(count * 0.25)
    odd = (quarter == 1.0) | (quarter == 3.0)
    sin_out = jnp.where(odd, cosine, sine)
    cos_out = jnp.where(odd, sine, cosine)
    sin_out = jnp.where(quarter >= 2.0, -sin_out, sin_out)
    cos_out = jnp.where((quarter == 1.0) | (quarter == 2.0), -cos_out, cos_out)
    return sin_out, cos_out


def silu_of_half(half):
    return half + half * jnp.tanh(half)


def lanes(shape):
    return lax.broadcasted_iota(jnp.int32, shape, 1)


OFFSETS = sorted(((z, x, c) for z in (0, 1) for x in range(4) for c in (0, 1)),
                 key=lambda o: -(2 * o[0] + min(o[1], 4 - o[1]) + 0.1 * o[2]))


def peer_at(q, offset):
    z, x, c = offset
    return ((q ^ (8 * z)) & 8) | ((q + 2 * x) & 6) | ((q ^ c) & 1)


def group_of(q):
    return jnp.where(q < NQ // 2, q, 3 * NQ // 2 - 1 - q)


def pack_latents(lat_ref, lev_ref, send_ref):
    lane = lanes((8, FR))
    row = lax.broadcasted_iota(jnp.int32, (8, FR), 0)
    pieces = []
    for c in range(4):
        for r in range(2):
            plane = lat_ref[:, c, r, :]
            own, left, right = c * 16 + r * 8, 64 + r * 8 + c * 2, 80 + r * 8 + c * 2
            pieces.append((3, own, pltpu.roll(plane, own, 1)))
            pieces.append((1, left, pltpu.roll(plane, left + 2, 1)))
            pieces.append((1, right, pltpu.roll(plane, right - 8, 1)))
    level = jnp.zeros((8, FR), F32)
    for f in range(8):
        level = jnp.where(row == f, lev_ref[f].astype(F32), level)

    def body(dest, carry):
        place = (lane - 8 * dest) & (FR - 1)
        total = jnp.zeros((8, FR), F32)
        for bits, base, plane in pieces:
            total = jnp.where((place >> bits) == (base >> bits), plane, total)
        total = pltpu.roll(total, lax.rem(FR - 8 * dest, FR), 1)
        send_ref[dest] = jnp.where(lane == 2 * ROW, level, total)
        return carry

    lax.fori_loop(0, NQ, body, 0)


def prepare(cin_ref, cmid_ref, gain_ref, qkv_ref, wo_ref, we_ref, ent_ref, tw_ref, taps_ref,
            twt_ref, band_ref, mid_ref, qkvt_ref, wot_ref, wet_ref, near_ref, ent_out, g):
    taps_ref[...] = jnp.zeros(taps_ref.shape, F32)
    for i in range(9):
        taps_ref[4 * i : 4 * i + 4, :] = cin_ref[i // 3, i % 3].astype(F32)
    taps_t = taps_ref[...].T.astype(BF16)
    k = lanes((40, TAPS))
    m = lax.broadcasted_iota(jnp.int32, (40, TAPS), 0)
    dy = (k >= ROW).astype(jnp.int32) + (k >= 2 * ROW).astype(jnp.int32)
    rest = k - ROW * dy
    own = rest < 32
    left = rest < 40
    c = jnp.where(own, rest >> 3, (rest & 7) >> 1)
    rel = jnp.where(own, (rest & 7) + 2, jnp.where(left, rest & 1, (rest & 1) + 10))
    for w in range(PX + 2):
        dx = rel - w
        pick = (dx >= 0) & (dx <= 2) & (m == dy * 12 + dx * 4 + c)
        band_ref[w] = dot(taps_t, jnp.where(pick, 0.5, 0.0).astype(BF16)).astype(BF16)
    taps = [0.5 * jnp.concatenate([cmid_ref[dy, dx].astype(F32) for dx in range(3)], axis=0) for dy in range(3)]
    outer = 0.5 * (taps[0] + taps[2])
    for v, mid in enumerate((taps[0], outer + 0.5 * taps[1], outer - 0.5 * taps[1], taps[2])):
        mid_ref[v] = mid.astype(BF16).T
    weight = 0.5 * tw_ref[...].T
    high = weight.astype(BF16)
    low = (weight - high.astype(F32)).astype(BF16)
    twt_ref[...] = jnp.concatenate([high, high, low], axis=1)
    qkvt_ref[...] = (qkv_ref[...].T.astype(F32) * gain_ref[...].reshape(1, CH)).astype(BF16)
    wot_ref[...] = (0.5 * wo_ref[...].astype(F32)).astype(BF16).T
    wet_ref[...] = jnp.concatenate([we_ref[...].astype(F32), jnp.zeros((12, CH), F32)], axis=0).astype(BF16)
    key_slot = lax.broadcasted_iota(jnp.int32, (FR, 2 * FR), 0)
    query_slot = lanes((FR, 2 * FR)) & (FR - 1)
    near_ref[...] = jnp.where(jnp.abs(key_slot - query_slot) <= WIN, 1.0, 0.0)
    lane = lanes((8, FR))
    for s in range(STEPS):
        rows = jnp.concatenate([ent_ref[s, c, r : r + 1, :] for c in range(4) for r in range(2)], axis=0)
        rows = pltpu.roll(rows, lax.rem(FR - 8 * g, FR), 1)
        columns = jnp.concatenate([rows, jnp.zeros((FR - 8, FR), F32)], axis=0).T[:8]
        for i in range(8):
            shifted = pltpu.roll(columns, FR - 1 - i, 1)
            ent_out[s, 8 * i : 8 * i + 8, :] = jnp.where(lane == FR - 1, shifted, 0.0)


def blank(query_ref):
    def body(i, carry):
        for p in range(5):
            query_ref[i, p, :HD, FR:] = jnp.zeros((HD, FR), BF16)
            query_ref[i, p, HD:, :FR] = jnp.zeros((HD, FR), BF16)
        return carry

    lax.fori_loop(0, PX, body, 0)


def embed(level, twt_ref, emb_ref, t):
    index = lax.broadcasted_iota(jnp.int32, (CH // 2, FR), 0).astype(F32)
    freqs = jnp.exp(-math.log(10000.0) * index / (CH // 2))
    sine, cosine = sin_cos(level * freqs)
    feature = jnp.concatenate([sine, cosine], axis=0)
    high = feature.astype(BF16)
    low = (feature - high.astype(F32)).astype(BF16)
    emb = dot(twt_ref[...], jnp.concatenate([high, low, high], axis=0))
    emb_ref[0] = jnp.where(t > 0, emb, 0.0)
    emb_ref[1] = emb
    emb_ref[2] = jnp.where(t < NT - 1, emb, 0.0)


def coefficients(level):
    lane = lanes((8, FR))
    level = jnp.broadcast_to(level, (8, FR))
    target = jnp.where(lane == 0, 0.0, pltpu.roll(level, 1, 1))
    angle = lambda l: (l / 1000.0 + 0.008) / 1.008 * (math.pi / 2.0)
    s0, c0 = sin_cos(angle(level))
    s1, c1 = sin_cos(angle(target))
    alpha = c1 / c0
    return alpha, s1 - alpha * s0


def conv_in(slots, band_ref, emb_ref, rhs_ref, hid_ref, act_ref, g, t):
    rows = []
    for slot in slots:
        for r in range(2):
            rows.append(jnp.concatenate(
                [slot[k * 16 + r * 8 : k * 16 + r * 8 + 8] for k in range(6)], axis=0).astype(BF16))
    for p in range(2):
        for half in range(2):
            near = jnp.concatenate(rows[2 * p + half : 2 * p + half + 3], axis=0)
            if p == half:
                near = jnp.where((t > 0) if p == 0 else (t < NT - 1), near, jnp.zeros_like(near))
            rhs_ref[p, :, half * FR : (half + 1) * FR] = near

    def column(w, inside=None):
        active = []
        for p in range(2):
            both = dot(band_ref[w], rhs_ref[p])
            for half in range(2):
                hidden = both[:, half * FR : (half + 1) * FR] + emb_ref[p + half]
                if p != half:
                    hid_ref[w, p] = hidden
                hidden = silu_of_half(hidden)
                active.append(hidden if inside is None else jnp.where(inside, hidden, 0.0))
        a0, a1, a2, a3 = active
        for v, part in enumerate((a0 - a2, a1 + a2, a2 - a1, a1 - a3)):
            act_ref[w, v] = part.astype(BF16)

    column(0, g > 0)
    lax.fori_loop(1, PX + 1, lambda w, carry: (column(w), carry)[1], 0, unroll=PX)
    column(PX + 1, g < NQ - 1)


def unit(x, scale):
    return (x * (lax.rsqrt(jnp.sum(x * x, axis=0, keepdims=True) + 1e-06) * scale)).astype(BF16)


def each(bodies, count):
    def step(i, carry):
        for body in bodies:
            body(i)
        return carry

    lax.fori_loop(0, count, step, 0, unroll=count)


def places():
    pairs = [((s, 2 * p), (s, 2 * p + 1)) for s in range(2) for p in range(2)]
    return pairs + [((0, 4), (1, 4))]


def block_net(hs_ref, mid_ref, qkvt_ref, wot_ref, wet_ref, near_ref, hid_ref, act_ref, noise_ref,
              block_ref, normed_ref, project_ref, query_ref, stack_ref, key_ref, value_ref, weight_ref, total_ref, mixed_ref):
    def norm(i, block):
        block_ref[i] = block
        center = jnp.mean(block, axis=0, keepdims=True)
        moved = block - center
        spread = jnp.mean(moved * moved, axis=0, keepdims=True)
        normed_ref[i] = (moved * lax.rsqrt(spread + 1e-05 / 4)).astype(BF16)

    def conv_mid(j):
        parts = []
        for v in range(4):
            rhs = [jnp.concatenate([act_ref[2 * j + dx, v], act_ref[2 * j + dx + 1, v]], axis=1) for dx in range(3)]
            parts.append(dot(mid_ref[v], jnp.concatenate(rhs, axis=0)))
        for r, part in enumerate((parts[0] + (parts[1] + parts[2]), (parts[1] - parts[2]) - parts[3])):
            hidden = jnp.concatenate([hid_ref[2 * j + 1, r], hid_ref[2 * j + 2, r]], axis=1)
            norm(4 * r + j, hidden + part)

    def project(i):
        project_ref[i] = dot(qkvt_ref[...], normed_ref[i])

    def units(i):
        for p, pair in enumerate(places()):
            for n, (s, h) in enumerate(pair):
                cut, own = slice(s * FR, (s + 1) * FR), slice(n * FR, (n + 1) * FR)
                part = lambda k: project_ref[i, k * CH + h * HD : k * CH + (h + 1) * HD, cut]
                query_ref[i, p, n * HD : (n + 1) * HD, own] = unit(part(0), hs_ref[h] * math.log2(math.e))
                stack_ref[i, p, n * HD : (n + 1) * HD] = unit(part(1), 1.0)
                value_ref[i, p, :, own] = part(2).astype(BF16)
            key_ref[i, p] = stack_ref[i, p].T

    def attend(i):
        for p in range(5):
            weights = jnp.exp2(dot(key_ref[i, p], query_ref[i, p])) * near_ref[...]
            total_ref[i, p] = jnp.sum(weights, axis=0, keepdims=True)
            weight_ref[i, p] = weights.astype(BF16)

    def mix(i):
        for p, pair in enumerate(places()):
            share = 1.0 / total_ref[i, p]
            for n, (s, h) in enumerate(pair):
                cut, own = slice(s * FR, (s + 1) * FR), slice(n * FR, (n + 1) * FR)
                part = dot(value_ref[i, p, :, own], weight_ref[i, p, :, own]) * share[:, own]
                mixed_ref[i, h * HD : (h + 1) * HD, cut] = part.astype(BF16)

    def upper(i):
        normed_ref[i] = silu_of_half(block_ref[i] + dot(wot_ref[...], mixed_ref[i])).astype(BF16)

    def noise(i):
        noise_ref[i] = dot(wet_ref[...], normed_ref[i])[:8]

    each((conv_mid,), PX // 2)
    for bodies in ((project, units), (attend,), (mix,), (upper,), (noise,)):
        each(bodies, PX)


def advance(state, noise_ref, alpha, beta, entering):
    tiles = []
    for c in range(4):
        for r in range(2):
            rows = [noise_ref[r * 4 + w // 2, c : c + 1, (w % 2) * FR : (w % 2 + 1) * FR] for w in range(PX)]
            noise = jnp.concatenate(rows, axis=0)
            at = c * 16 + r * 8
            tiles.append(alpha * state[at : at + 8] + beta * noise)
    updated = jnp.concatenate(tiles, axis=0)
    return jnp.where(lanes((64, FR)) == FR - 1, entering, pltpu.roll(updated, FR - 1, 1))


def masked(slot, index, g, t):
    inside = (t > 0) if index == 0 else (t < NT - 1) if index == 2 else None
    own, left, right = slot[:64], slot[64:80], slot[80:96]
    left = jnp.where(g > 0, left, 0.0)
    right = jnp.where(g < NQ - 1, right, 0.0)
    slot = jnp.concatenate([own, left, right], axis=0)
    return slot if inside is None else jnp.where(inside, slot, 0.0)


def kernel(lat_hbm, ent_hbm, lev_hbm, tw_hbm, cin_hbm, cmid_hbm, gain_hbm, qkv_hbm, hs_hbm, wo_hbm, we_hbm,
           out_ref,
           lat_ref, ent_ref, lev_ref, tw_ref, cin_ref, cmid_ref, gain_ref, qkv_ref, hs_ref, wo_ref, we_ref, taps_ref,
           twt_ref, band_ref, mid_ref, qkvt_ref, wot_ref, wet_ref, near_ref, ent_out,
           emb_ref, rhs_ref, hid_ref, act_ref, noise_ref,
           block_ref, normed_ref, project_ref, query_ref, stack_ref, key_ref, value_ref, weight_ref, total_ref, mixed_ref,
           send1, recv1, halo, state_ref, own_ref, left_ref, right_ref, send3, recv3,
           load_sem, send1_sem, recv1_sem, send2_sem, recv2_sem, send3_sem, recv3_sem):
    q, t = lax.axis_index("queue"), lax.axis_index("tile")
    g = group_of(q)
    sides = [(t > 0, t - 1, 2), (t < NT - 1, t + 1, 0)]
    others = OFFSETS[:-1]

    barrier = pltpu.get_barrier_semaphore()
    for there, row, _ in sides:
        @pl.when(there)
        def _():
            for offset in OFFSETS:
                pl.semaphore_signal(barrier, inc=1, device_id=(peer_at(q, offset), row), device_id_type=MESH)
    for offset in others:
        pl.semaphore_signal(barrier, inc=1, device_id=(peer_at(q, offset), t), device_id_type=MESH)

    loads = [pltpu.make_async_copy(src, dst, load_sem.at[i]) for i, (src, dst) in enumerate(
        [(lat_hbm, lat_ref), (lev_hbm, lev_ref), (cmid_hbm, cmid_ref), (qkv_hbm, qkv_ref), (wo_hbm, wo_ref),
         (tw_hbm, tw_ref), (ent_hbm, ent_ref), (cin_hbm, cin_ref), (gain_hbm, gain_ref), (hs_hbm, hs_ref),
         (we_hbm, we_ref)])]
    for load in loads:
        load.start()
    for load in loads[:2]:
        load.wait()
    pack_latents(lat_ref, lev_ref, send1)
    both = (t > 0).astype(jnp.int32) + (t < NT - 1).astype(jnp.int32)
    pl.semaphore_wait(barrier, NQ - 1 + NQ * both)

    place = pl.ds(pl.multiple_of(q * 8, 8), 8)

    def to_peer(offset, row, slot):
        peer = peer_at(q, offset)
        pltpu.make_async_remote_copy(
            src_ref=send1.at[group_of(peer)], dst_ref=recv1.at[slot, place],
            send_sem=send1_sem.at[slot], recv_sem=recv1_sem.at[slot],
            device_id=(peer, row), device_id_type=MESH).start()

    for there, row, slot in sides:
        @pl.when(there)
        def _():
            for offset in OFFSETS:
                to_peer(offset, row, slot)
    for offset in others:
        to_peer(offset, t, 1)
    recv1[1, place] = send1[g]

    for load in loads[2:]:
        load.wait()
    prepare(cin_ref, cmid_ref, gain_ref, qkv_ref, wo_ref, we_ref, ent_ref, tw_ref, taps_ref,
            twt_ref, band_ref, mid_ref, qkvt_ref, wot_ref, wet_ref, near_ref, ent_out, g)
    blank(query_ref)

    def settle(ref, sem, count):
        part = ref.at[pl.ds(0, count)]
        pltpu.make_async_copy(part, part, sem).wait()

    settle(recv1.at[1], recv1_sem.at[1], FR - 8)
    for there, slot in ((t > 0, 0), (t < NT - 1, 2)):
        @pl.when(there)
        def _():
            settle(recv1.at[slot], recv1_sem.at[slot], FR)
    slots = [recv1[slot].T for slot in range(3)]
    level = slots[1][2 * ROW : 2 * ROW + 1]
    embed(level, twt_ref, emb_ref, t)
    alpha, beta = coefficients(level)
    state = slots[1][:64]
    slots = [masked(slot[: 2 * ROW], i, g, t) for i, slot in enumerate(slots)]

    conv_in(slots, band_ref, emb_ref, rhs_ref, hid_ref, act_ref, g, t)
    block_net(hs_ref, mid_ref, qkvt_ref, wot_ref, wet_ref, near_ref, hid_ref, act_ref, noise_ref,
              block_ref, normed_ref, project_ref, query_ref, stack_ref, key_ref, value_ref, weight_ref, total_ref, mixed_ref)
    state = advance(state, noise_ref, alpha, beta, ent_out[0])

    state_ref[...] = state
    own_ref[...] = state.astype(BF16)
    lefts, rights = [], []
    for r in range(2):
        for c in range(4):
            at = c * 16 + r * 8
            lefts.append(state[at + 6 : at + 8])
            rights.append(state[at : at + 2])
    left_ref[...] = jnp.concatenate(lefts, axis=0).astype(BF16)
    right_ref[...] = jnp.concatenate(rights, axis=0).astype(BF16)
    copies = []
    for src, start, size, step in ((left_ref, 64, 16, 1), (right_ref, 80, 16, -1), (own_ref, 0, 64, 0)):
        sent, got = (g < NQ - 1, g > 0) if step == 1 else (g > 0, g < NQ - 1) if step == -1 else (None, None)
        peer = group_of(jnp.clip(g + step, 0, NQ - 1))
        for down in (-1, 1, 0):
            if step == 0 and down == 0:
                continue
            sent_too, got_too = (t > 0, t < NT - 1) if down == -1 else (t < NT - 1, t > 0) if down == 1 else (None, None)
            both_of = lambda a, b: b if a is None else a if b is None else a & b
            i = len(copies)
            copies.append((both_of(sent, sent_too), both_of(got, got_too), pltpu.make_async_remote_copy(
                src_ref=src, dst_ref=halo.at[1 - down, pl.ds(start, size)],
                send_sem=send2_sem.at[i], recv_sem=recv2_sem.at[i],
                device_id=(peer, t + down), device_id_type=MESH)))
    for sent, _, copy in copies:
        pl.when(sent)(copy.start)
    for _, got, copy in copies:
        pl.when(got)(copy.wait_recv)
    halo[1, :64] = own_ref[...]
    slots = [masked(halo[i].astype(F32), i, g, t) for i in range(3)]

    conv_in(slots, band_ref, emb_ref, rhs_ref, hid_ref, act_ref, g, t)
    block_net(hs_ref, mid_ref, qkvt_ref, wot_ref, wet_ref, near_ref, hid_ref, act_ref, noise_ref,
              block_ref, normed_ref, project_ref, query_ref, stack_ref, key_ref, value_ref, weight_ref, total_ref, mixed_ref)
    state = advance(state_ref[...], noise_ref, alpha, beta, ent_out[1])

    frames = jnp.concatenate([state, jnp.zeros((64, FR), F32)], axis=0).T
    for peer in range(NQ):
        send3[peer] = frames[peer * 8 : peer * 8 + 8]
    for offset in others:
        peer = peer_at(q, offset)
        pltpu.make_async_remote_copy(
            src_ref=send3.at[peer], dst_ref=recv3.at[g],
            send_sem=send3_sem.at[0], recv_sem=recv3_sem.at[0],
            device_id=(peer, t), device_id_type=MESH).start()
    recv3[g] = send3[q]
    for sent, _, copy in copies:
        pl.when(sent)(copy.wait_send)
    settle(send1, send1_sem.at[1], NQ - 1)
    for there, _, slot in sides:
        @pl.when(there)
        def _():
            settle(send1, send1_sem.at[slot], NQ)
    settle(recv3, recv3_sem.at[0], NQ - 1)

    group = lanes((8, FR)) >> 3
    turned = [pltpu.roll(recv3[source], 8 * source, 1) for source in range(NQ)]
    for c in range(4):
        for r in range(2):
            at = c * 2 + r
            total = turned[0]
            for source in range(1, NQ):
                total = jnp.where(group == (source + at) % NQ, turned[source], total)
            out_ref[:, c, r, :] = pltpu.roll(total, (FR - 8 * at) % FR, 1)
    settle(send3, send3_sem.at[0], NQ - 1)


def per_device(queue_latents, entering, levels, time_weight, conv_in_weight, conv_mid_weight, norm_gain,
               qkv_weight, head_scale, attn_out_weight, eps_out_weight):
    hbm = pl.BlockSpec(memory_space=pl.ANY)
    v = pltpu.VMEM
    dma = pltpu.SemaphoreType.DMA
    inputs = (queue_latents, entering, levels, time_weight, conv_in_weight, conv_mid_weight,
              norm_gain, qkv_weight, head_scale, attn_out_weight, eps_out_weight.T)
    scalars = (levels, head_scale)
    return pl.pallas_call(
        kernel,
        out_shape=pltpu.VMEM(queue_latents.shape, F32),
        in_specs=[hbm] * len(inputs),
        out_specs=pl.BlockSpec(memory_space=pltpu.VMEM),
        scratch_shapes=[
            *[(pltpu.SMEM if any(x is y for y in scalars) else v)(x.shape, x.dtype) for x in inputs],
            v((40, CH), F32),
            v((CH, 3 * CH), BF16),
            v((PX + 2, CH, TAPS), BF16), v((4, CH, 3 * CH), BF16), v((3 * CH, CH), BF16), v((CH, CH), BF16),
            v((16, CH), BF16), v((FR, 2 * FR), F32), v((STEPS, 64, FR), F32),
            v((3, CH, FR), F32), v((2, TAPS, 2 * FR), BF16), v((PX + 2, 2, CH, FR), F32),
            v((PX + 2, 4, CH, FR), BF16), v((PX, 8, 2 * FR), F32),
            v((PX, CH, 2 * FR), F32), v((PX, CH, 2 * FR), BF16), v((PX, 3 * CH, 2 * FR), F32),
            v((PX, 5, FR, 2 * FR), BF16), v((PX, 5, FR, FR), BF16), v((PX, 5, FR, FR), BF16),
            v((PX, 5, HD, 2 * FR), BF16), v((PX, 5, FR, 2 * FR), BF16), v((PX, 5, 1, 2 * FR), F32),
            v((PX, CH, 2 * FR), BF16),
            v((NQ, 8, FR), F32), v((3, FR, FR), F32), v((3, 2 * ROW, FR), BF16), v((64, FR), F32), v((64, FR), BF16),
            v((16, FR), BF16), v((16, FR), BF16), v((NQ, 8, FR), F32), v((NQ, 8, FR), F32),
            dma((len(inputs),)), dma((3,)), dma((3,)), dma((8,)), dma((8,)), dma((1,)), dma((1,)),
        ],
        compiler_params=pltpu.CompilerParams(
            collective_id=0, has_side_effects=True, vmem_limit_bytes=56 * 1024 * 1024),
    )(*inputs)


def solution(mesh):
    placed = (
        P("queue", None, "tile", None),
        P(None, None, "tile", None),
        P("queue"),
        P(),
        P(),
        P(),
        P(),
        P(),
        P(),
        P(),
        P(),
    )
    return jax.shard_map(
        per_device,
        mesh=mesh,
        in_specs=placed,
        out_specs=P("queue", None, "tile", None),
        check_vma=False,
    )
```

```python
import math

import jax
import jax.numpy as jnp
from jax import lax
from jax.experimental import pallas as pl
from jax.experimental.pallas import tpu as pltpu
from jax.sharding import PartitionSpec as P

WIN = 8
STEPS = 2
F32 = jnp.float32
BF16 = jnp.bfloat16
MESH = pl.DeviceIdType.MESH

CH = 320
HEADS = 5
HD = 64
FR = 128
NQ = 16
NT = 8
PX = 8
ROW = 48
TAPS = 3 * ROW


def dot(a, b):
    return jnp.dot(a, b, preferred_element_type=F32)


def dot_t(a, b):
    return lax.dot_general(a, b, (((0,), (0,)), ((), ())), preferred_element_type=F32)


def sin_cos(angle):
    count = jnp.floor(angle * (2.0 / math.pi) + 0.5)
    rest = ((angle - count * 1.5703125) - count * 4.837512969970703125e-4) - count * 7.54978995489188216e-8
    square = rest * rest
    sine = rest + rest * square * (
        -1.6666654611e-1 + square * (8.3321608736e-3 - square * 1.9515295891e-4)
    )
    cosine = 1.0 - 0.5 * square + square * square * (
        4.166664568298827e-2 + square * (-1.388731625493765e-3 + square * 2.443315711809948e-5)
    )
    quarter = count - 4.0 * jnp.floor(count * 0.25)
    odd = (quarter == 1.0) | (quarter == 3.0)
    sin_out = jnp.where(odd, cosine, sine)
    cos_out = jnp.where(odd, sine, cosine)
    sin_out = jnp.where(quarter >= 2.0, -sin_out, sin_out)
    cos_out = jnp.where((quarter == 1.0) | (quarter == 2.0), -cos_out, cos_out)
    return sin_out, cos_out


def silu_of_half(half):
    return half + half * jnp.tanh(half)


def lanes(shape):
    return lax.broadcasted_iota(jnp.int32, shape, 1)


OFFSETS = sorted(((z, x, c) for z in (0, 1) for x in range(4) for c in (0, 1)),
                 key=lambda o: -(2 * o[0] + min(o[1], 4 - o[1]) + 0.1 * o[2]))


def peer_at(q, offset):
    z, x, c = offset
    return ((q ^ (8 * z)) & 8) | ((q + 2 * x) & 6) | ((q ^ c) & 1)


def group_of(q):
    return jnp.where(q < NQ // 2, q, 3 * NQ // 2 - 1 - q)


def pack_latents(lat_ref, lev_ref, send_ref):
    lane = lanes((8, FR))
    row = lax.broadcasted_iota(jnp.int32, (8, FR), 0)
    pieces = []
    for c in range(4):
        for r in range(2):
            plane = lat_ref[:, c, r, :]
            own, left, right = c * 16 + r * 8, 64 + r * 8 + c * 2, 80 + r * 8 + c * 2
            pieces.append((3, own, pltpu.roll(plane, own, 1)))
            pieces.append((1, left, pltpu.roll(plane, left + 2, 1)))
            pieces.append((1, right, pltpu.roll(plane, right - 8, 1)))
    level = jnp.zeros((8, FR), F32)
    for f in range(8):
        level = jnp.where(row == f, lev_ref[f].astype(F32), level)

    def body(dest, carry):
        place = (lane - 8 * dest) & (FR - 1)
        total = jnp.zeros((8, FR), F32)
        for bits, base, plane in pieces:
            total = jnp.where((place >> bits) == (base >> bits), plane, total)
        total = pltpu.roll(total, lax.rem(FR - 8 * dest, FR), 1)
        send_ref[dest] = jnp.where(lane == 2 * ROW, level, total)
        return carry

    lax.fori_loop(0, NQ, body, 0)


def prepare(cin_ref, cmid_ref, gain_ref, qkv_ref, wo_ref, we_ref, ent_ref, tw_ref, taps_ref,
            twt_ref, band_ref, mid_ref, qkvt_ref, wot_ref, wet_ref, near_ref, ent_out, g):
    taps_ref[...] = jnp.zeros(taps_ref.shape, F32)
    for i in range(9):
        taps_ref[4 * i : 4 * i + 4, :] = cin_ref[i // 3, i % 3].astype(F32)
    taps_t = taps_ref[...].T.astype(BF16)
    k = lanes((40, TAPS))
    m = lax.broadcasted_iota(jnp.int32, (40, TAPS), 0)
    dy = (k >= ROW).astype(jnp.int32) + (k >= 2 * ROW).astype(jnp.int32)
    rest = k - ROW * dy
    own = rest < 32
    left = rest < 40
    c = jnp.where(own, rest >> 3, (rest & 7) >> 1)
    rel = jnp.where(own, (rest & 7) + 2, jnp.where(left, rest & 1, (rest & 1) + 10))
    for w in range(PX + 2):
        dx = rel - w
        pick = (dx >= 0) & (dx <= 2) & (m == dy * 12 + dx * 4 + c)
        band_ref[w] = dot(taps_t, jnp.where(pick, 0.5, 0.0).astype(BF16)).astype(BF16)
    taps = [0.5 * jnp.concatenate([cmid_ref[dy, dx].astype(F32) for dx in range(3)], axis=0) for dy in range(3)]
    outer = 0.5 * (taps[0] + taps[2])
    for v, mid in enumerate((taps[0], outer + 0.5 * taps[1], outer - 0.5 * taps[1], taps[2])):
        mid_ref[v] = mid.astype(BF16).T
    weight = 0.5 * tw_ref[...].T
    high = weight.astype(BF16)
    low = (weight - high.astype(F32)).astype(BF16)
    twt_ref[...] = jnp.concatenate([high, high, low], axis=1)
    qkvt_ref[...] = (qkv_ref[...].T.astype(F32) * gain_ref[...].reshape(1, CH)).astype(BF16)
    wot_ref[...] = (0.5 * wo_ref[...].astype(F32)).astype(BF16).T
    wet_ref[...] = jnp.concatenate([we_ref[...].astype(F32), jnp.zeros((12, CH), F32)], axis=0).astype(BF16)
    key_slot = lax.broadcasted_iota(jnp.int32, (FR, 2 * FR), 0)
    query_slot = lanes((FR, 2 * FR)) & (FR - 1)
    near_ref[...] = jnp.where(jnp.abs(key_slot - query_slot) <= WIN, 1.0, 0.0)
    lane = lanes((8, FR))
    for s in range(STEPS):
        rows = jnp.concatenate([ent_ref[s, c, r : r + 1, :] for c in range(4) for r in range(2)], axis=0)
        rows = pltpu.roll(rows, lax.rem(FR - 8 * g, FR), 1)
        columns = jnp.concatenate([rows, jnp.zeros((FR - 8, FR), F32)], axis=0).T[:8]
        for i in range(8):
            shifted = pltpu.roll(columns, FR - 1 - i, 1)
            ent_out[s, 8 * i : 8 * i + 8, :] = jnp.where(lane == FR - 1, shifted, 0.0)


def blank(query_ref):
    def body(i, carry):
        for p in range(5):
            query_ref[i, p, :HD, FR:] = jnp.zeros((HD, FR), BF16)
            query_ref[i, p, HD:, :FR] = jnp.zeros((HD, FR), BF16)
        return carry

    lax.fori_loop(0, PX, body, 0)


def embed(level, twt_ref, emb_ref, t):
    index = lax.broadcasted_iota(jnp.int32, (CH // 2, FR), 0).astype(F32)
    freqs = jnp.exp(-math.log(10000.0) * index / (CH // 2))
    sine, cosine = sin_cos(level * freqs)
    feature = jnp.concatenate([sine, cosine], axis=0)
    high = feature.astype(BF16)
    low = (feature - high.astype(F32)).astype(BF16)
    emb = dot(twt_ref[...], jnp.concatenate([high, low, high], axis=0))
    emb_ref[0] = jnp.where(t > 0, emb, 0.0)
    emb_ref[1] = emb
    emb_ref[2] = jnp.where(t < NT - 1, emb, 0.0)


def coefficients(level):
    lane = lanes((8, FR))
    level = jnp.broadcast_to(level, (8, FR))
    target = jnp.where(lane == 0, 0.0, pltpu.roll(level, 1, 1))
    angle = lambda l: (l / 1000.0 + 0.008) / 1.008 * (math.pi / 2.0)
    s0, c0 = sin_cos(angle(level))
    s1, c1 = sin_cos(angle(target))
    alpha = c1 / c0
    return alpha, s1 - alpha * s0


def conv_in(slots, band_ref, emb_ref, rhs_ref, hid_ref, act_ref, g, t):
    rows = []
    for slot in slots:
        for r in range(2):
            rows.append(jnp.concatenate(
                [slot[k * 16 + r * 8 : k * 16 + r * 8 + 8] for k in range(6)], axis=0).astype(BF16))
    for p in range(2):
        for half in range(2):
            near = jnp.concatenate(rows[2 * p + half : 2 * p + half + 3], axis=0)
            if p == half:
                near = jnp.where((t > 0) if p == 0 else (t < NT - 1), near, jnp.zeros_like(near))
            rhs_ref[p, :, half * FR : (half + 1) * FR] = near

    def column(w, inside=None):
        active = []
        for p in range(2):
            both = dot(band_ref[w], rhs_ref[p])
            for half in range(2):
                hidden = both[:, half * FR : (half + 1) * FR] + emb_ref[p + half]
                if p != half:
                    hid_ref[w, p] = hidden
                hidden = silu_of_half(hidden)
                active.append(hidden if inside is None else jnp.where(inside, hidden, 0.0))
        a0, a1, a2, a3 = active
        for v, part in enumerate((a0 - a2, a1 + a2, a2 - a1, a1 - a3)):
            act_ref[w, v] = part.astype(BF16)

    column(0, g > 0)
    lax.fori_loop(1, PX + 1, lambda w, carry: (column(w), carry)[1], 0, unroll=PX)
    column(PX + 1, g < NQ - 1)


def unit(x, scale):
    return (x * (lax.rsqrt(jnp.sum(x * x, axis=0, keepdims=True) + 1e-06) * scale)).astype(BF16)


def each(bodies, count):
    def step(i, carry):
        for body in bodies:
            body(i)
        return carry

    lax.fori_loop(0, count, step, 0, unroll=count)


def places():
    pairs = [((s, 2 * p), (s, 2 * p + 1)) for s in range(2) for p in range(2)]
    return pairs + [((0, 4), (1, 4))]


def block_net(hs_ref, mid_ref, qkvt_ref, wot_ref, wet_ref, near_ref, hid_ref, act_ref, noise_ref,
              block_ref, normed_ref, project_ref, query_ref, stack_ref, key_ref, value_ref, weight_ref, total_ref, mixed_ref):
    def norm(i, block):
        block_ref[i] = block
        center = jnp.mean(block, axis=0, keepdims=True)
        moved = block - center
        spread = jnp.mean(moved * moved, axis=0, keepdims=True)
        normed_ref[i] = (moved * lax.rsqrt(spread + 1e-05 / 4)).astype(BF16)

    def conv_mid(j):
        parts = []
        for v in range(4):
            rhs = [jnp.concatenate([act_ref[2 * j + dx, v], act_ref[2 * j + dx + 1, v]], axis=1) for dx in range(3)]
            parts.append(dot(mid_ref[v], jnp.concatenate(rhs, axis=0)))
        for r, part in enumerate((parts[0] + (parts[1] + parts[2]), (parts[1] - parts[2]) - parts[3])):
            hidden = jnp.concatenate([hid_ref[2 * j + 1, r], hid_ref[2 * j + 2, r]], axis=1)
            norm(4 * r + j, hidden + part)

    def project(i):
        project_ref[i] = dot(qkvt_ref[...], normed_ref[i])

    def units(i):
        for p, pair in enumerate(places()):
            for n, (s, h) in enumerate(pair):
                cut, own = slice(s * FR, (s + 1) * FR), slice(n * FR, (n + 1) * FR)
                part = lambda k: project_ref[i, k * CH + h * HD : k * CH + (h + 1) * HD, cut]
                query_ref[i, p, n * HD : (n + 1) * HD, own] = unit(part(0), hs_ref[h] * math.log2(math.e))
                stack_ref[i, p, n * HD : (n + 1) * HD] = unit(part(1), 1.0)
                value_ref[i, p, :, own] = part(2).astype(BF16)
            key_ref[i, p] = stack_ref[i, p].T

    def attend(i):
        for p in range(5):
            weights = jnp.exp2(dot(key_ref[i, p], query_ref[i, p])) * near_ref[...]
            total_ref[i, p] = jnp.sum(weights, axis=0, keepdims=True)
            weight_ref[i, p] = weights.astype(BF16)

    def mix(i):
        for p, pair in enumerate(places()):
            share = 1.0 / total_ref[i, p]
            for n, (s, h) in enumerate(pair):
                cut, own = slice(s * FR, (s + 1) * FR), slice(n * FR, (n + 1) * FR)
                part = dot(value_ref[i, p, :, own], weight_ref[i, p, :, own]) * share[:, own]
                mixed_ref[i, h * HD : (h + 1) * HD, cut] = part.astype(BF16)

    def upper(i):
        normed_ref[i] = silu_of_half(block_ref[i] + dot(wot_ref[...], mixed_ref[i])).astype(BF16)

    def noise(i):
        noise_ref[i] = dot(wet_ref[...], normed_ref[i])[:8]

    each((conv_mid,), PX // 2)
    for bodies in ((project, units), (attend,), (mix,), (upper,), (noise,)):
        each(bodies, PX)


def advance(state, noise_ref, alpha, beta, entering):
    tiles = []
    for c in range(4):
        for r in range(2):
            rows = [noise_ref[r * 4 + w // 2, c : c + 1, (w % 2) * FR : (w % 2 + 1) * FR] for w in range(PX)]
            noise = jnp.concatenate(rows, axis=0)
            at = c * 16 + r * 8
            tiles.append(alpha * state[at : at + 8] + beta * noise)
    updated = jnp.concatenate(tiles, axis=0)
    return jnp.where(lanes((64, FR)) == FR - 1, entering, pltpu.roll(updated, FR - 1, 1))


def masked(slot, index, g, t):
    inside = (t > 0) if index == 0 else (t < NT - 1) if index == 2 else None
    own, left, right = slot[:64], slot[64:80], slot[80:96]
    left = jnp.where(g > 0, left, 0.0)
    right = jnp.where(g < NQ - 1, right, 0.0)
    slot = jnp.concatenate([own, left, right], axis=0)
    return slot if inside is None else jnp.where(inside, slot, 0.0)


def kernel(lat_hbm, ent_hbm, lev_hbm, tw_hbm, cin_hbm, cmid_hbm, gain_hbm, qkv_hbm, hs_hbm, wo_hbm, we_hbm,
           out_ref,
           lat_ref, ent_ref, lev_ref, tw_ref, cin_ref, cmid_ref, gain_ref, qkv_ref, hs_ref, wo_ref, we_ref, taps_ref,
           twt_ref, band_ref, mid_ref, qkvt_ref, wot_ref, wet_ref, near_ref, ent_out,
           emb_ref, rhs_ref, hid_ref, act_ref, noise_ref,
           block_ref, normed_ref, project_ref, query_ref, stack_ref, key_ref, value_ref, weight_ref, total_ref, mixed_ref,
           send1, recv1, halo, state_ref, own_ref, left_ref, right_ref, send3, recv3,
           load_sem, send1_sem, recv1_sem, send2_sem, recv2_sem, send3_sem, recv3_sem):
    q, t = lax.axis_index("queue"), lax.axis_index("tile")
    g = group_of(q)
    sides = [(t > 0, t - 1, 2), (t < NT - 1, t + 1, 0)]
    others = OFFSETS[:-1]

    barrier = pltpu.get_barrier_semaphore()
    for there, row, _ in sides:
        @pl.when(there)
        def _():
            for offset in OFFSETS:
                pl.semaphore_signal(barrier, inc=1, device_id=(peer_at(q, offset), row), device_id_type=MESH)
    for offset in others:
        pl.semaphore_signal(barrier, inc=1, device_id=(peer_at(q, offset), t), device_id_type=MESH)

    loads = [pltpu.make_async_copy(src, dst, load_sem.at[i]) for i, (src, dst) in enumerate(
        [(lat_hbm, lat_ref), (lev_hbm, lev_ref), (cmid_hbm, cmid_ref), (qkv_hbm, qkv_ref), (wo_hbm, wo_ref),
         (tw_hbm, tw_ref), (ent_hbm, ent_ref), (cin_hbm, cin_ref), (gain_hbm, gain_ref), (hs_hbm, hs_ref),
         (we_hbm, we_ref)])]
    for load in loads:
        load.start()
    for load in loads[:2]:
        load.wait()
    pack_latents(lat_ref, lev_ref, send1)
    both = (t > 0).astype(jnp.int32) + (t < NT - 1).astype(jnp.int32)
    pl.semaphore_wait(barrier, NQ - 1 + NQ * both)

    place = pl.ds(pl.multiple_of(q * 8, 8), 8)

    def to_peer(offset, row, slot):
        peer = peer_at(q, offset)
        pltpu.make_async_remote_copy(
            src_ref=send1.at[group_of(peer)], dst_ref=recv1.at[slot, place],
            send_sem=send1_sem.at[slot], recv_sem=recv1_sem.at[slot],
            device_id=(peer, row), device_id_type=MESH).start()

    for there, row, slot in sides:
        @pl.when(there)
        def _():
            for offset in OFFSETS:
                to_peer(offset, row, slot)
    for offset in others:
        to_peer(offset, t, 1)
    recv1[1, place] = send1[g]

    for load in loads[2:]:
        load.wait()
    prepare(cin_ref, cmid_ref, gain_ref, qkv_ref, wo_ref, we_ref, ent_ref, tw_ref, taps_ref,
            twt_ref, band_ref, mid_ref, qkvt_ref, wot_ref, wet_ref, near_ref, ent_out, g)
    blank(query_ref)

    def settle(ref, sem, count):
        part = ref.at[pl.ds(0, count)]
        pltpu.make_async_copy(part, part, sem).wait()

    settle(recv1.at[1], recv1_sem.at[1], FR - 8)
    for there, slot in ((t > 0, 0), (t < NT - 1, 2)):
        @pl.when(there)
        def _():
            settle(recv1.at[slot], recv1_sem.at[slot], FR)
    slots = [recv1[slot].T for slot in range(3)]
    level = slots[1][2 * ROW : 2 * ROW + 1]
    embed(level, twt_ref, emb_ref, t)
    alpha, beta = coefficients(level)
    state = slots[1][:64]
    slots = [masked(slot[: 2 * ROW], i, g, t) for i, slot in enumerate(slots)]

    conv_in(slots, band_ref, emb_ref, rhs_ref, hid_ref, act_ref, g, t)
    block_net(hs_ref, mid_ref, qkvt_ref, wot_ref, wet_ref, near_ref, hid_ref, act_ref, noise_ref,
              block_ref, normed_ref, project_ref, query_ref, stack_ref, key_ref, value_ref, weight_ref, total_ref, mixed_ref)
    state = advance(state, noise_ref, alpha, beta, ent_out[0])

    state_ref[...] = state
    own_ref[...] = state.astype(BF16)
    lefts, rights = [], []
    for r in range(2):
        for c in range(4):
            at = c * 16 + r * 8
            lefts.append(state[at + 6 : at + 8])
            rights.append(state[at : at + 2])
    left_ref[...] = jnp.concatenate(lefts, axis=0).astype(BF16)
    right_ref[...] = jnp.concatenate(rights, axis=0).astype(BF16)
    copies = []
    for src, start, size, step in ((left_ref, 64, 16, 1), (right_ref, 80, 16, -1), (own_ref, 0, 64, 0)):
        sent, got = (g < NQ - 1, g > 0) if step == 1 else (g > 0, g < NQ - 1) if step == -1 else (None, None)
        peer = group_of(jnp.clip(g + step, 0, NQ - 1))
        for down in (-1, 1, 0):
            if step == 0 and down == 0:
                continue
            sent_too, got_too = (t > 0, t < NT - 1) if down == -1 else (t < NT - 1, t > 0) if down == 1 else (None, None)
            both_of = lambda a, b: b if a is None else a if b is None else a & b
            i = len(copies)
            part = halo.at[1 - down, pl.ds(start, size)]
            copies.append((both_of(sent, sent_too), both_of(got, got_too), part, pltpu.make_async_remote_copy(
                src_ref=src, dst_ref=part, send_sem=send2_sem.at[i], recv_sem=recv2_sem.at[i],
                device_id=(peer, jnp.clip(t + down, 0, NT - 1)), device_id_type=MESH)))
    for sent, _, _, copy in copies:
        pl.when(sent)(copy.start)
    for i, (_, got, part, _) in enumerate(copies):
        pl.when(got)(lambda: pltpu.make_async_copy(part, part, recv2_sem.at[i]).wait())
    halo[1, :64] = own_ref[...]
    slots = [masked(halo[i].astype(F32), i, g, t) for i in range(3)]

    conv_in(slots, band_ref, emb_ref, rhs_ref, hid_ref, act_ref, g, t)
    block_net(hs_ref, mid_ref, qkvt_ref, wot_ref, wet_ref, near_ref, hid_ref, act_ref, noise_ref,
              block_ref, normed_ref, project_ref, query_ref, stack_ref, key_ref, value_ref, weight_ref, total_ref, mixed_ref)
    state = advance(state_ref[...], noise_ref, alpha, beta, ent_out[1])

    frames = jnp.concatenate([state, jnp.zeros((64, FR), F32)], axis=0).T
    for peer in range(NQ):
        send3[peer] = frames[peer * 8 : peer * 8 + 8]
    for offset in others:
        peer = peer_at(q, offset)
        pltpu.make_async_remote_copy(
            src_ref=send3.at[peer], dst_ref=recv3.at[g],
            send_sem=send3_sem.at[0], recv_sem=recv3_sem.at[0],
            device_id=(peer, t), device_id_type=MESH).start()
    recv3[g] = send3[q]
    for sent, _, _, copy in copies:
        pl.when(sent)(copy.wait_send)
    settle(send1, send1_sem.at[1], NQ - 1)
    for there, _, slot in sides:
        @pl.when(there)
        def _():
            settle(send1, send1_sem.at[slot], NQ)
    settle(recv3, recv3_sem.at[0], NQ - 1)

    group = lanes((8, FR)) >> 3
    turned = [pltpu.roll(recv3[source], 8 * source, 1) for source in range(NQ)]
    for c in range(4):
        for r in range(2):
            at = c * 2 + r
            total = turned[0]
            for source in range(1, NQ):
                total = jnp.where(group == (source + at) % NQ, turned[source], total)
            out_ref[:, c, r, :] = pltpu.roll(total, (FR - 8 * at) % FR, 1)
    settle(send3, send3_sem.at[0], NQ - 1)


def per_device(queue_latents, entering, levels, time_weight, conv_in_weight, conv_mid_weight, norm_gain,
               qkv_weight, head_scale, attn_out_weight, eps_out_weight):
    hbm = pl.BlockSpec(memory_space=pl.ANY)
    v = pltpu.VMEM
    dma = pltpu.SemaphoreType.DMA
    inputs = (queue_latents, entering, levels, time_weight, conv_in_weight, conv_mid_weight,
              norm_gain, qkv_weight, head_scale, attn_out_weight, eps_out_weight.T)
    scalars = (levels, head_scale)
    return pl.pallas_call(
        kernel,
        out_shape=pltpu.VMEM(queue_latents.shape, F32),
        in_specs=[hbm] * len(inputs),
        out_specs=pl.BlockSpec(memory_space=pltpu.VMEM),
        scratch_shapes=[
            *[(pltpu.SMEM if any(x is y for y in scalars) else v)(x.shape, x.dtype) for x in inputs],
            v((40, CH), F32),
            v((CH, 3 * CH), BF16),
            v((PX + 2, CH, TAPS), BF16), v((4, CH, 3 * CH), BF16), v((3 * CH, CH), BF16), v((CH, CH), BF16),
            v((16, CH), BF16), v((FR, 2 * FR), F32), v((STEPS, 64, FR), F32),
            v((3, CH, FR), F32), v((2, TAPS, 2 * FR), BF16), v((PX + 2, 2, CH, FR), F32),
            v((PX + 2, 4, CH, FR), BF16), v((PX, 8, 2 * FR), F32),
            v((PX, CH, 2 * FR), F32), v((PX, CH, 2 * FR), BF16), v((PX, 3 * CH, 2 * FR), F32),
            v((PX, 5, FR, 2 * FR), BF16), v((PX, 5, FR, FR), BF16), v((PX, 5, FR, FR), BF16),
            v((PX, 5, HD, 2 * FR), BF16), v((PX, 5, FR, 2 * FR), BF16), v((PX, 5, 1, 2 * FR), F32),
            v((PX, CH, 2 * FR), BF16),
            v((NQ, 8, FR), F32), v((3, FR, FR), F32), v((3, 2 * ROW, FR), BF16), v((64, FR), F32), v((64, FR), BF16),
            v((16, FR), BF16), v((16, FR), BF16), v((NQ, 8, FR), F32), v((NQ, 8, FR), F32),
            dma((len(inputs),)), dma((3,)), dma((3,)), dma((8,)), dma((8,)), dma((1,)), dma((1,)),
        ],
        compiler_params=pltpu.CompilerParams(
            collective_id=0, has_side_effects=True, vmem_limit_bytes=56 * 1024 * 1024),
    )(*inputs)


def solution(mesh):
    placed = (
        P("queue", None, "tile", None),
        P(None, None, "tile", None),
        P("queue"),
        P(),
        P(),
        P(),
        P(),
        P(),
        P(),
        P(),
        P(),
    )
    return jax.shard_map(
        per_device,
        mesh=mesh,
        in_specs=placed,
        out_specs=P("queue", None, "tile", None),
        check_vma=False,
    )
```
